32 devices in a mesh: clouds: 16 (over z, y, x), points: 2 (over core).
Axes of the slice: x: 2, y: 2, z: 4, core: 2. Of those that a mesh axis runs over, the one named last changes fastest.
Arguments:
- features: float32 [64, 32768], P(None, ('clouds', 'points')), may hold values from -24 to 24
- lengths: int32 [64], P('clouds'), may hold values from 128 to 1664, as said below
- mask: int32 [32768], P(('clouds', 'points')), may hold values from 0 to 1, as said below
- neighbours: int32 [20, 32768], P(None, ('clouds', 'points')), may hold values from 0 to 2047, as said below
- first_layer_weight: float32 [128, 128], replicated, may hold values from -0.5 to 0.5
- first_norm_gain: float32 [128], replicated, may hold values from 0.5 to 1.5
- first_norm_bias: float32 [128], replicated, may hold values from -2.5 to 2.5
- second_layer_weight: float32 [256, 256], replicated, may hold values from -0.375 to 0.375
- second_norm_gain: float32 [256], replicated, may hold values from 0.5 to 1.5
- second_norm_bias: float32 [256], replicated, may hold values from -2.5 to 2.5
- pooled_grad: float32 [64, 512], P('clouds'), may hold values from -6 to 6
Outputs:
- pooled: float32 [64, 512], P('clouds')
- grad_features: float32 [64, 32768], P(None, ('clouds', 'points'))
- grad_weight_one: float32 [128, 128], replicated
- grad_gamma_one: float32 [128], replicated
- grad_beta_one: float32 [128], replicated
- grad_weight_two: float32 [256, 256], replicated
- grad_gamma_two: float32 [256], replicated
- grad_beta_two: float32 [256], replicated
The draws below stay inside these ranges and needn't reach their ends.
Inputs may be any that keep to these rules, and one draw needn't show every extreme that they name: The 4 lengths of each cloud group sum to 2048; a group holds either four clouds of 384 to 768 points, or one cloud of exactly 1664 points and three of 128; at least one group is of the second kind. `neighbours`: each entry names a point of the same cloud as the point it belongs to, by its index within the cloud group. Every 1024-th point, beginning with the first, has mask 1.
All inputs are finite; a program needn't handle non-finite values.
Results may differ from the reference program's by a relative error of at most 0.0003.
Values sent between devices are 32-bit elements; how exact they have to be, the bound alone decides.
A program may use at most 128 MiB of HBM per device.

```python
import math
import jax
import jax.numpy as jnp
from jax import lax

CIN = 64
C1 = 128
C2 = 256
NEIGHBOUR_COUNT = 20
P_DEV = 1024
C_GRP = 4
GROUP_POINTS = 2048
MOST = 1664
NPTS = 32768
CLOUDS = 64


def cloud_layout(key):
    cloud_groups = NPTS // GROUP_POINTS
    sixteenth = GROUP_POINTS // 16
    half = GROUP_POINTS // 2
    first_len = jax.random.randint(jax.random.fold_in(key, 101), (cloud_groups,), 3 * sixteenth, 5 * sixteenth + 1)
    excess = jax.random.randint(jax.random.fold_in(key, 102), (cloud_groups,), 1, sixteenth + 1)
    second_len = half - first_len + excess
    remaining = half - excess
    wobble = jax.random.randint(jax.random.fold_in(key, 103), (cloud_groups,), -(GROUP_POINTS // 32), GROUP_POINTS // 32 + 1)
    third_len = remaining // 2 + wobble
    fourth_len = remaining - third_len
    drawn = jnp.stack([first_len, second_len, third_len, fourth_len], axis=1)
    slots = jnp.arange(C_GRP, dtype=jnp.int32)[None, :]
    big_slot = jax.random.randint(jax.random.fold_in(key, 104), (cloud_groups, 1), 0, C_GRP)
    heavy_rows = jnp.where(slots == big_slot, MOST, sixteenth)
    heavy = jax.random.randint(jax.random.fold_in(key, 105), (cloud_groups,), 0, 8) == 0
    forced = jax.random.randint(jax.random.fold_in(key, 106), (), 0, cloud_groups)
    heavy = heavy | (jnp.arange(cloud_groups, dtype=jnp.int32) == forced)
    spans = jnp.where(heavy[:, None], heavy_rows, drawn).astype(jnp.int32)
    ends = jnp.cumsum(spans, axis=1)
    starts = ends - spans
    position = jnp.arange(GROUP_POINTS, dtype=jnp.int32)
    owner = jnp.sum((position[None, None, :] >= ends[:, :, None]).astype(jnp.int32), axis=1)
    first = jnp.take_along_axis(starts, owner, axis=1)
    extent = jnp.take_along_axis(spans, owner, axis=1)
    offsets = jax.random.randint(jax.random.fold_in(key, 107), (NEIGHBOUR_COUNT, cloud_groups, GROUP_POINTS), 0, extent[None, :, :])
    linked = first[None, :, :] + offsets
    linked = linked.at[0, :, 0].set(0).at[0, :, GROUP_POINTS - 1].set(GROUP_POINTS - 1)
    return (spans.reshape(-1), linked.reshape(NEIGHBOUR_COUNT, cloud_groups * GROUP_POINTS).astype(jnp.int32))


def draw_lengths(key, part):
    spans, linked = cloud_layout(key)
    return spans


def draw_neighbours(key, part):
    spans, linked = cloud_layout(key)
    return linked


def draw_mask(key, part):
    key = jax.random.fold_in(key, 7)
    active_flag = jax.random.randint(key, (NPTS,), 0, 8) < 7
    position = jnp.arange(NPTS, dtype=jnp.int32)
    active_flag = active_flag | (position % P_DEV == 0)
    return active_flag.astype(jnp.int32)


def draw_features(key, part):
    key = jax.random.fold_in(key, 5)
    base_key = jax.random.fold_in(key, 1)
    channel_key = jax.random.fold_in(key, 2)
    channel_scale = 0.3 * 10.0 ** jax.random.uniform(channel_key, (CIN, 1), jnp.float32)
    column = jnp.arange(NPTS, dtype=jnp.float32) / NPTS
    base = jnp.clip(jax.random.normal(base_key, (CIN, NPTS), jnp.float32), -4.0, 4.0)
    point_scale = 0.6 * 3.0 ** column
    return (base * channel_scale * point_scale[None, :]).astype(jnp.float32)


def level_of(stream_key, dims, split, low, largest):
    level = 1.0
    for dim, blocks in split:
        draws = jax.random.uniform(jax.random.fold_in(jax.random.fold_in(stream_key, 6), dim), (blocks,), jnp.float32, low / len(split), largest / len(split))
        level = level * jnp.repeat(jnp.exp(draws), dims[dim] // blocks).reshape((-1,) + (1,) * (len(dims) - 1 - dim))
    return level


def scatter_about(own_key, shape, deviation, limit, split=(), kind=jnp.bfloat16):
    loudness = level_of(own_key, shape, split, -0.22, 0.18) if split else 1.0
    result = jax.random.normal(own_key, shape, jnp.float32) * deviation * loudness
    return jnp.minimum(jnp.maximum(result, -limit), limit).astype(kind)


def setup_inputs(seed: int = 0) -> dict:
    arg_keys = jax.random.split(jax.random.key(seed), 12)
    return {
        "features": draw_features(jax.random.fold_in(arg_keys[11], 71), 0),
        "lengths": draw_lengths(jax.random.fold_in(arg_keys[11], 71), 0),
        "mask": draw_mask(jax.random.fold_in(arg_keys[11], 71), 0),
        "neighbours": draw_neighbours(jax.random.fold_in(arg_keys[11], 71), 0),
        "first_layer_weight": scatter_about(arg_keys[4], (C1, 2 * CIN), (2 * CIN) ** -0.5, 0.5, (), jnp.float32),
        "first_norm_gain": jnp.clip(1.0 + 0.1 * jax.random.normal(arg_keys[5], (C1,), jnp.float32), 0.5, 1.5),
        "first_norm_bias": scatter_about(arg_keys[6], (C1,), 0.5, 2.5, (), jnp.float32),
        "second_layer_weight": scatter_about(arg_keys[7], (C2, 2 * C1), (2 * C1) ** -0.5, 0.375, (), jnp.float32),
        "second_norm_gain": jnp.clip(1.0 + 0.1 * jax.random.normal(arg_keys[8], (C2,), jnp.float32), 0.5, 1.5),
        "second_norm_bias": scatter_about(arg_keys[9], (C2,), 0.5, 2.5, (), jnp.float32),
        "pooled_grad": scatter_about(arg_keys[10], (CLOUDS, 2 * C2), 1.0, 6.0, ((0, 16),), jnp.float32),
    }


@jax.custom_vjp
def low(v):
    return lax.optimization_barrier(v.astype(jnp.bfloat16)).astype(jnp.float32)

@jax.custom_vjp
def low_back(v):
    return v

def low_keep(v):
    return (low(v), None)

def low_pass(kept, grad):
    return (grad,)

def back_keep(v):
    return (v, None)

def back_low(kept, grad):
    return (low(grad),)
low.defvjp(low_keep, low_pass)
low_back.defvjp(back_keep, back_low)
EPSILON = 1e-05
FULL_ACCURACY = lax.Precision.HIGHEST

def edge_values(input_points, neighbour_links, layer_weight):
    width = input_points.shape[0]
    direct = layer_weight[:, :width]
    relative = layer_weight[:, width:]
    fetched = input_points[:, neighbour_links]
    spread = fetched - input_points[:, None, :]
    own_term = jnp.dot(direct, input_points, precision=FULL_ACCURACY)
    edge_term = jnp.einsum('cd,dkp->ckp', relative, spread, precision=FULL_ACCURACY)
    return own_term[:, None, :] + edge_term

def edgeconv_layer(block_list, neighbour_links, active_mask, layer_weight, norm_gain, norm_bias):
    element_count = NEIGHBOUR_COUNT * jnp.sum(active_mask)

    def linear_sum(item):
        block, link, active_flag = item
        return lax.optimization_barrier(jnp.sum(edge_values(block, link, layer_weight) * active_flag[None, None, :], axis=(1, 2)))
    channel_means = lax.optimization_barrier(jnp.sum(lax.map(jax.checkpoint(linear_sum), (block_list, neighbour_links, active_mask)), axis=0)) / element_count

    def squared_sum(item):
        block, link, active_flag = item
        centred = edge_values(block, link, layer_weight) - channel_means[:, None, None]
        return lax.optimization_barrier(jnp.sum(centred * centred * active_flag[None, None, :], axis=(1, 2)))
    channel_variance = lax.optimization_barrier(jnp.sum(lax.map(jax.checkpoint(squared_sum), (block_list, neighbour_links, active_mask)), axis=0)) / element_count
    scale = lax.rsqrt(channel_variance + EPSILON)

    def layer_output(item):
        block, link, active_flag = item
        normed = (edge_values(block, link, layer_weight) - channel_means[:, None, None]) * scale[:, None, None]
        shifted = norm_gain[:, None, None] * normed + norm_bias[:, None, None]
        active = 0.2 * shifted + 0.8 * jax.nn.softplus(shifted)
        return jax.nn.logsumexp(active, axis=1) - math.log(NEIGHBOUR_COUNT)
    return lax.map(jax.checkpoint(layer_output), (block_list, neighbour_links, active_mask))

def cloud_pool(final_output, spans):
    ends = jnp.cumsum(spans, axis=1)
    starts = ends - spans
    position = jnp.arange(GROUP_POINTS, dtype=jnp.int32)
    group_member = (position[None, None, :] >= starts[:, :, None]) & (position[None, None, :] < ends[:, :, None])
    sizes = spans.astype(jnp.float32)
    peaks = jax.nn.logsumexp(jnp.broadcast_to(final_output[:, None, :, :], (final_output.shape[0], spans.shape[1], final_output.shape[1], final_output.shape[2])), axis=3, where=group_member[:, :, None, :])
    group_totals = jnp.einsum('rat,rjt->raj', group_member.astype(jnp.float32), final_output, precision=FULL_ACCURACY)
    pooled = jnp.concatenate([peaks - jnp.log(sizes)[:, :, None], group_totals / sizes[:, :, None]], axis=2)
    return pooled.reshape(-1, 2 * final_output.shape[1])

def reference(features, lengths, mask, neighbours, first_layer_weight, first_norm_gain, first_norm_bias, second_layer_weight, second_norm_gain, second_norm_bias, pooled_grad):
    cloud_groups = features.shape[1] // GROUP_POINTS
    neighbour_links = neighbours.reshape(NEIGHBOUR_COUNT, cloud_groups, GROUP_POINTS).transpose(1, 0, 2)
    active_mask = mask.astype(jnp.float32).reshape(cloud_groups, GROUP_POINTS)
    spans = lengths.reshape(cloud_groups, C_GRP)

    def forward(input_points, first_weight_local, first_gain_local, first_bias_local, second_weight_local, second_gain_local, second_bias_local):
        block_list = input_points.reshape(input_points.shape[0], cloud_groups, GROUP_POINTS).transpose(1, 0, 2)
        hidden_features = edgeconv_layer(block_list, neighbour_links, active_mask, first_weight_local, first_gain_local, first_bias_local)
        final_output = edgeconv_layer(hidden_features, neighbour_links, active_mask, second_weight_local, second_gain_local, second_bias_local)
        return cloud_pool(final_output, spans)
    pooled, backward = jax.vjp(forward, features, first_layer_weight, first_norm_gain, first_norm_bias, second_layer_weight, second_norm_gain, second_norm_bias)
    grads = backward(pooled_grad)
    return (pooled, grads[0], grads[1], grads[2], grads[3], grads[4], grads[5], grads[6])
```

```python
import functools
import math

import jax
import jax.numpy as jnp
from jax import lax
from jax.experimental import pallas as pl
from jax.experimental.pallas import tpu as pltpu
from jax.sharding import PartitionSpec as P

EPSILON = 1e-05
LOG2E = math.log2(math.e)
LN2 = math.log(2.0)
MESH = pl.DeviceIdType.MESH
F32 = jnp.float32
BF16 = jnp.bfloat16
LANES = 128
SUBLANES = 8
CHUNK = 256
MEMORY = 60 * 2**20
VMEM = pl.BlockSpec(memory_space=pltpu.VMEM)
SMEM = pl.BlockSpec(memory_space=pltpu.SMEM)


def dot(left, right, dims):
    return lax.dot_general(
        left,
        right,
        (dims, ((), ())),
        precision=lax.Precision.HIGHEST,
        preferred_element_type=F32,
    )


def mm(left, right):
    return dot(left, right, ((1,), (0,)))


def mm_nt(left, right):
    return dot(left, right, ((1,), (1,)))


def mm_tn(left, right):
    return dot(left, right, ((0,), (0,)))


def mm_low(left, right):
    return lax.dot_general(
        left, right, (((1,), (0,)), ((), ())), preferred_element_type=F32
    )


def split(value):
    high = value.astype(BF16)
    low = (value - high.astype(F32)).astype(BF16)
    return high, low


def over(count, step, body):
    def run(i, carry):
        body(pl.multiple_of(i * step, step))
        return carry

    lax.fori_loop(0, count // step, run, 0)


def log2(value):
    return jnp.log(value) * LOG2E


def tree(values, join):
    values = list(values)
    while len(values) > 1:
        values = [
            join(values[i], values[i + 1]) if i + 1 < len(values) else values[i]
            for i in range(0, len(values), 2)
        ]
    return values[0]


def iota(shape, dim):
    return lax.broadcasted_iota(jnp.int32, shape, dim)


def signal_all(barrier, cores, total):
    me = lax.axis_index("clouds") * cores + lax.axis_index("points")

    def send(d, carry):
        t = lax.rem(me + d, total)
        pl.semaphore_signal(
            barrier,
            inc=1,
            device_id=(lax.div(t, cores), lax.rem(t, cores)),
            device_id_type=MESH,
        )
        return carry

    lax.fori_loop(1, total, send, 0)


def gather_start(own, slots, send_sem, recv_sem, cores, total):
    me = lax.axis_index("clouds") * cores + lax.axis_index("points")
    slots[me] = own[...]

    def send(d, carry):
        t = lax.rem(me + d, total)
        pltpu.make_async_remote_copy(
            src_ref=own,
            dst_ref=slots.at[me],
            send_sem=send_sem,
            recv_sem=recv_sem,
            device_id=(lax.div(t, cores), lax.rem(t, cores)),
            device_id_type=MESH,
        ).start()
        return carry

    lax.fori_loop(1, total, send, 0)


def gather_wait(slots, send_sem, recv_sem, total):
    others = slots.at[pl.ds(0, total - 1)]
    arrived = pltpu.make_async_remote_copy(
        src_ref=others,
        dst_ref=others,
        send_sem=send_sem,
        recv_sem=recv_sem,
        device_id=(lax.axis_index("clouds"), 1 - lax.axis_index("points")),
        device_id_type=MESH,
    )
    arrived.wait_recv()
    arrived.wait_send()


def slot_sum(slots, total):
    def add(i, carry):
        return carry + slots[i]

    return lax.fori_loop(1, total, add, slots[0])


def to_partner(source, target, sems, index):
    return pltpu.make_async_remote_copy(
        src_ref=source,
        dst_ref=target,
        send_sem=sems.at[0, index],
        recv_sem=sems.at[1, index],
        device_id=(lax.axis_index("clouds"), 1 - lax.axis_index("points")),
        device_id_type=MESH,
    )


def edge_pass(subs, block, depth, part, index, table, own_rows, out_hbm, held, ring, sems, outs):
    level_ref, share_ref, moment_ref, inverse_ref = outs
    per = SUBLANES // subs
    groups = own_rows.shape[0] // SUBLANES
    stages = depth // part
    row = iota((SUBLANES, LANES), 0)
    mine = [(row >= subs * i) & (row < subs * (i + 1)) for i in range(per)]
    zero = jnp.zeros((SUBLANES, LANES), F32)

    def fetch(group, stage, slot):
        for k in range(part):
            target = held[slot].at[stage * part + k]
            for i in range(per):
                first = (k * per + i) * groups
                if stages > 1:
                    span = groups * (1 + (stages - 1) * part * per)
                    j = index.at[pl.ds(first, span)][stage * (part * per * groups) + group]
                else:
                    j = index.at[pl.ds(first, groups)][group]
                value = table[pl.ds(j, SUBLANES), :]
                if i == 0:
                    target[...] = value
                else:
                    pltpu.store(target, value, mask=mine[i])

    def work(group, stage, slot, ring_slot, place, carry):
        total0, share0, moment0 = carry
        rows = pl.ds(pl.multiple_of(group * SUBLANES, SUBLANES), SUBLANES)
        peak = tree([held[slot][k] for k in range(depth)], jnp.maximum)
        top = own_rows[rows, :] + peak
        shift = jnp.maximum(top, 0.0)
        rest = jnp.maximum(jnp.exp2(-shift), 2.0**-100)
        scale = jnp.exp2(top - shift)
        fifth = 0.2 * rest
        total, share, moment = [], [], []
        for k in range(part):
            value = held[slot][stage * part + k]
            away = value - peak
            grown = scale * jnp.exp2(away)
            root = jnp.exp2((away - log2(rest + grown)) * 0.2)
            weight = root * (fifth + grown)
            ring[ring_slot, place, stage * part + k] = weight
            total.append(root)
            share.append(weight)
            moment.append(weight * value)
        total, share, moment = [
            functools.reduce(jnp.add, parts) for parts in (total, share, moment)
        ]
        if stages > 1:
            start = stage == 0
            total = total + jnp.where(start, 0.0, total0)
            share = share + jnp.where(start, 0.0, share0)
            moment = moment + jnp.where(start, 0.0, moment0)
        mass = share + (0.8 * rest) * total
        inverse = 1.0 / mass
        level_ref[rows, :] = LN2 * (0.2 * top + 0.8 * shift + log2(mass)) - math.log(depth)
        inverse_ref[rows, :] = inverse
        share_ref[rows, :] = share * inverse
        moment_ref[rows, :] = moment * inverse
        return total, share, moment

    blocks = groups // block

    def push(b, slot):
        return pltpu.make_async_copy(
            ring.at[slot], out_hbm.at[pl.ds(b * block, block)], sems.at[slot]
        )

    for stage in range(stages):
        fetch(0, stage, 0)

    def one_block(b, carry):
        ring_slot = lax.rem(b, 2)

        @pl.when(b >= 2)
        def _():
            push(b - 2, ring_slot).wait()

        def pair(t, inner):
            for slot in range(2):
                place = t * 2 + slot
                group = b * block + place
                after = jnp.minimum(group + 1, groups - 1)
                if stages == 1:
                    work(group, 0, slot, ring_slot, place, (zero,) * 3)
                    fetch(after, 0, 1 - slot)
                else:

                    def one_stage(stage, sums):
                        sums = work(group, stage, slot, ring_slot, place, sums)
                        fetch(after, stage, 1 - slot)
                        return sums

                    lax.fori_loop(0, stages, one_stage, (zero,) * 3)
            return inner

        lax.fori_loop(0, block // 2, pair, 0)
        push(b, ring_slot).start()
        return carry

    lax.fori_loop(0, blocks, one_block, 0)
    if blocks > 1:
        push(blocks - 2, (blocks - 2) % 2).wait()
    push(blocks - 1, (blocks - 1) % 2).wait()


def lanes_to_rows(value, width):
    return [value[:, i * LANES : (i + 1) * LANES] for i in range(width // LANES)]


def rows_to_lanes(rows):
    return rows[0] if len(rows) == 1 else jnp.concatenate(rows, axis=1)


def forward_kernel(
    sizes,
    feat,
    near,
    live,
    index1,
    index2,
    lengths,
    weight1,
    gain1,
    bias1,
    weight2,
    gain2,
    bias2,
    pooled_grad,
    pooled,
    q1,
    q2,
    inverse1,
    share1,
    moment1,
    x1,
    away_own1,
    away_all1,
    counts,
    scales1,
    push2,
    extra2,
    x2_out,
    own2,
    grad_own2,
    scales2,
    x1_cm,
    links,
    live_col,
    parts1,
    parts2,
    u1,
    v1,
    n1,
    g1,
    table1,
    own_rows1,
    level1,
    table2,
    own_rows2,
    level2,
    share2,
    moment2,
    inverse2,
    x2,
    u2,
    v2,
    g2,
    xm,
    pool_parts,
    message,
    slots,
    held0,
    held1,
    ring,
    pair_sems,
    all_sems,
    ring_sems,
):
    cores, total = sizes
    points = feat.shape[1]
    cin = feat.shape[0]
    both = cores * points
    depth = near.shape[0]
    width1 = weight1.shape[0]
    width2 = weight2.shape[0]
    core = lax.axis_index("points")
    half = pl.multiple_of(core * points, points)
    barrier = pltpu.get_barrier_semaphore()
    signal_all(barrier, cores, total)

    row16 = iota((16, LANES), 0)
    one, none = jnp.ones((16, LANES), BF16), jnp.zeros((16, LANES), BF16)

    def build(columns):
        names = [near[k, :, columns] for k in range(depth)]

        def rows16(start):
            target = (row16 + start).astype(jnp.int16)
            found = [jnp.where(name == target, one, none) for name in names]
            links[pl.ds(start, 16), columns] = functools.reduce(jnp.add, found)

        over(both, 16, rows16)

    for tile in range(points // LANES):
        build(pl.ds(tile * LANES, LANES))

    x1_cm[core] = feat[...]
    pl.semaphore_wait(barrier, total - 1)
    swap = to_partner(feat, x1_cm.at[core], pair_sems, 0)
    swap.start()
    live_col[...] = jnp.broadcast_to(jnp.transpose(live[...])[:, :1], live_col.shape)
    swap.wait()

    direct1 = weight1[:, :cin] - weight1[:, cin:]
    relative1 = weight1[:, cin:]
    for c in range(cores):

        def turn(start):
            x1[pl.ds(c * points + start, CHUNK), :] = jnp.transpose(
                x1_cm[c, :, pl.ds(start, CHUNK)]
            )

        over(points, CHUNK, turn)
        value = x1_cm[c]
        high, low = split(value)
        lower = (value - high.astype(F32) - low.astype(F32)).astype(BF16)
        parts1[c, 0:cin, :] = high
        parts1[c, cin : 2 * cin, :] = low
        parts1[c, 2 * cin : 3 * cin, :] = lower

    def sums_near1(start):
        columns = pl.ds(start, CHUNK)
        value = mm_low(parts1[0], links[0:points, columns])
        for c in range(1, cores):
            value = value + mm_low(parts1[c], links[c * points : (c + 1) * points, columns])
        value = value[0:cin] + value[cin : 2 * cin] + value[2 * cin : 3 * cin]
        n1[columns, :] = jnp.transpose(value)

    over(points, CHUNK, sums_near1)

    own_high, own_low = split(x1_cm[core])
    both_parts = jnp.concatenate([own_high.astype(F32), own_low.astype(F32)], axis=0)
    x_parts = jnp.transpose(both_parts).astype(BF16)
    ones = jnp.ones((points, LANES), BF16)

    def linked1(start):
        rows = pl.ds(start, CHUNK)
        xm[rows, :] = mm_low(links[rows, :], x_parts)
        counts[rows, :] = mm_low(links[rows, :], ones)

    over(both, CHUNK, linked1)

    live_rows = live[...]
    live_sum = jnp.sum(live[0:1, :], axis=1, keepdims=True)
    mine = live_sum * depth

    def statistics(x_all, n_ref, direct, relative, u, v, g, width):
        def outer(start):
            rows = pl.ds(start, CHUNK)
            v[rows, :] = mm_nt(x_all[rows, :], relative)

        over(both, CHUNK, outer)

        def inner(start):
            rows = pl.ds(start, CHUNK)
            u[rows, :] = mm_nt(x_all[pl.ds(half + start, CHUNK), :], direct)
            g[rows, :] = mm_nt(n_ref[rows, :], relative)

        over(points, CHUNK, inner)
        u_sum = mm(live_rows, u[...])[0:1]
        g_sum = jnp.sum(g[...], axis=0, keepdims=True)
        u_mean = u_sum / live_sum
        v_mean = g_sum / mine
        centred = u[...] - u_mean
        spread = depth * centred * centred + 2.0 * centred * (g[...] - depth * v_mean)
        square = mm(live_rows, spread)[0:1]
        weights = rows_to_lanes([counts[...]] * (width // LANES))
        away = v[...] - v_mean
        square = square + jnp.sum(weights * away * away, axis=0, keepdims=True)
        return depth * u_sum + g_sum, square, v_mean

    def send_sums(use, rows):
        for i, value in enumerate(rows):
            message[use, i : i + 1, :] = value
        gather_start(
            message.at[use], slots.at[use], all_sems.at[0, use], all_sems.at[1, use], cores, total
        )

    def receive(use):
        gather_wait(slots.at[use], all_sems.at[0, use], all_sems.at[1, use], total)

    def combine(use, numbers, width):
        per = width // LANES
        count = numbers[0]
        for value in numbers[1:]:
            count = count + value

        def value_of(i, first):
            return rows_to_lanes([slots[use, i, first + h : first + h + 1, :] for h in range(per)])

        mean = value_of(0, 0)
        for i in range(1, total):
            mean = mean + value_of(i, 0)
        mean = mean / count
        square = None
        for i in range(total):
            gap = value_of(i, 0) / numbers[i] - mean
            term = value_of(i, per) + numbers[i] * gap * gap
            square = term if square is None else square + term
        return count, mean, square / count

    sums, square, v_mean1 = statistics(x1, n1, direct1, relative1, u1, v1, g1, width1)
    send_sums(0, [sums, square, jnp.broadcast_to(mine, (1, LANES)), jnp.zeros((1, LANES), F32)])
    receive(0)
    numbers = [slots[0, i, 2:3, 0:1] for i in range(total)]
    count, mean1, variance1 = combine(0, numbers, width1)
    r1 = lax.rsqrt(variance1 + EPSILON)
    slope1 = gain1[...] * r1
    scales1[...] = jnp.concatenate(
        [slope1, r1, jnp.broadcast_to(count, (1, LANES)), jnp.zeros((5, LANES), F32)], axis=0
    )

    def fill1(start):
        rows = pl.ds(start, CHUNK)
        table1[pl.ds(SUBLANES + start, CHUNK), :] = (v1[rows, :] - v_mean1) * (slope1 * LOG2E)
        shared = mm_nt(xm[rows, 0:cin] + xm[rows, cin : 2 * cin], direct1)
        away_all1[rows, :] = shared + counts[rows, :] * (v1[rows, :] - mean1)

    over(both, CHUNK, fill1)

    def fill_own1(start):
        rows = pl.ds(start, CHUNK)
        own_rows1[rows, :] = (u1[rows, :] - (mean1 - v_mean1)) * (slope1 * LOG2E) + bias1[
            ...
        ] * LOG2E
        away_own1[rows, :] = depth * live_col[rows, :] * (u1[rows, :] - mean1) + g1[rows, :]

    over(points, CHUNK, fill_own1)

    edge_pass(
        1,
        ring.shape[1],
        depth,
        depth // 2,
        index1,
        table1,
        own_rows1,
        q1,
        (held0, held1),
        ring,
        ring_sems,
        (level1, share1, moment1, inverse1),
    )

    def hidden(start):
        rows = pl.ds(start, CHUNK)
        x2[pl.ds(half + start, CHUNK), :] = level1[rows, :]
        offset = own_rows1[rows, :] - bias1[...] * LOG2E
        moment1[rows, :] = (share1[rows, :] * offset + moment1[rows, :]) / (gain1[...] * LOG2E)

    over(points, CHUNK, hidden)
    here = x2.at[pl.ds(half, points)]
    swap = to_partner(here, here, pair_sems, 1)
    swap.start()
    swap.wait()

    direct2 = weight2[:, :width1] - weight2[:, width1:]
    relative2 = weight2[:, width1:]

    def turn2(start):
        high, low = split(jnp.transpose(x2[pl.ds(start, CHUNK), :]))
        parts2[0:width1, pl.ds(start, CHUNK)] = high
        parts2[width1 : 2 * width1, pl.ds(start, CHUNK)] = low

    over(both, CHUNK, turn2)

    def sums_near2(start):
        columns = pl.ds(start, CHUNK)
        value = mm_low(parts2[...], links[:, columns])
        value = value[0:width1] + value[width1 : 2 * width1]
        g2[columns, :] = mm_nt(jnp.transpose(value), relative2)

    over(points, CHUNK, sums_near2)

    def statistics2():
        def outer(start):
            rows = pl.ds(start, CHUNK)
            v2[rows, :] = mm_nt(x2[rows, :], relative2)
            x2_out[rows, :] = x2[rows, :]

        over(both, CHUNK, outer)

        def inner(start):
            u2[pl.ds(start, CHUNK), :] = mm_nt(x2[pl.ds(half + start, CHUNK), :], direct2)

        over(points, CHUNK, inner)
        u_sum = jnp.zeros((1, width2), F32)
        g_sum = jnp.zeros((1, width2), F32)
        for s in range(0, points, CHUNK):
            u_sum = u_sum + mm(live[:, s : s + CHUNK], u2[s : s + CHUNK, :])[0:1]
            g_sum = g_sum + jnp.sum(g2[s : s + CHUNK, :], axis=0, keepdims=True)
        u_mean = u_sum / live_sum
        v_mean = g_sum / mine
        square = jnp.zeros((1, width2), F32)
        for s in range(0, points, CHUNK):
            centred = u2[s : s + CHUNK, :] - u_mean
            spread = depth * centred * centred + 2.0 * centred * (
                g2[s : s + CHUNK, :] - depth * v_mean
            )
            square = square + mm(live[:, s : s + CHUNK], spread)[0:1]

        def squares(i, carry):
            rows = pl.ds(pl.multiple_of(i * CHUNK, CHUNK), CHUNK)
            away = v2[rows, :] - v_mean
            weights = rows_to_lanes([counts[rows, :]] * (width2 // LANES))
            return carry + jnp.sum(weights * away * away, axis=0, keepdims=True)

        square = lax.fori_loop(0, both // CHUNK, squares, square)
        return depth * u_sum + g_sum, square, v_mean

    sums, square, v_mean2 = statistics2()
    send_sums(1, lanes_to_rows(sums, width2) + lanes_to_rows(square, width2))
    receive(1)
    count, mean2, variance2 = combine(1, numbers, width2)
    r2 = lax.rsqrt(variance2 + EPSILON)
    slope2 = gain2[...] * r2
    scales2[...] = jnp.concatenate([slope2, jnp.zeros((7, width2), F32)], axis=0)

    def fill2(start):
        rows = pl.ds(start, CHUNK)
        value = (v2[rows, :] - v_mean2) * (slope2 * LOG2E)
        for h in range(2):
            table2[pl.ds(SUBLANES + 2 * start + h, CHUNK, stride=2), :] = value[
                :, h * LANES : (h + 1) * LANES
            ]

    over(both, CHUNK, fill2)

    def fill_own2(start):
        rows = pl.ds(start, CHUNK)
        value = (u2[rows, :] - (mean2 - v_mean2)) * (slope2 * LOG2E) + bias2[...] * LOG2E
        for h in range(2):
            own_rows2[pl.ds(2 * start + h, CHUNK, stride=2), :] = value[
                :, h * LANES : (h + 1) * LANES
            ]

    over(points, CHUNK, fill_own2)

    edge_pass(
        2,
        ring.shape[1],
        depth,
        depth,
        index2,
        table2,
        own_rows2,
        q2,
        (held0, held1),
        ring,
        ring_sems,
        (level2, share2, moment2, inverse2),
    )

    clouds = pooled_grad.shape[0]
    starts, ends = [], []
    end = jnp.int32(0)
    for q in range(clouds):
        starts.append(end)
        end = end + lengths[q]
        ends.append(end)
    row = iota((SUBLANES, LANES), 0)
    odd = lax.rem(row, 2) == 1
    point_of_row = lax.div(row, 2)
    steps = level2.shape[0] // SUBLANES
    lowest = jnp.full((SUBLANES, LANES), -1e30, F32)
    zero = jnp.zeros((SUBLANES, LANES), F32)

    def members(t):
        position = point_of_row + (half + t * (SUBLANES // 2))
        return [(position >= starts[q]) & (position < ends[q]) for q in range(clouds)]

    def step_rows(t):
        return pl.ds(pl.multiple_of(t * SUBLANES, SUBLANES), SUBLANES)

    def by_parity(value, join):
        value = join(value, pltpu.roll(value, 2, 0))
        return join(value, pltpu.roll(value, 4, 0))

    def peaks(t, carry):
        value = level2[step_rows(t), :]
        inside = members(t)
        out = []
        for q in range(clouds):
            out.append(jnp.maximum(carry[q], jnp.where(inside[q], value, lowest)))
        for q in range(clouds):
            out.append(carry[clouds + q] + jnp.where(inside[q], value, zero))
        return tuple(out)

    state = lax.fori_loop(0, steps, peaks, (lowest,) * clouds + (zero,) * clouds)
    peak = [by_parity(value, jnp.maximum) for value in state[:clouds]]
    sums = [by_parity(value, jnp.add) for value in state[clouds:]]

    def pick(inside, values):
        value = values[0]
        for q in range(1, clouds):
            value = jnp.where(inside[q], values[q], value)
        return value

    def masses(t, carry):
        inside = members(t)
        value = jnp.exp(level2[step_rows(t), :] - pick(inside, peak))
        return tuple(carry[q] + jnp.where(inside[q], value, zero) for q in range(clouds))

    state = lax.fori_loop(0, steps, masses, (zero,) * clouds)
    mass = [by_parity(value, jnp.add) for value in state]
    for q in range(clouds):
        pool_parts[core, 3 * q] = peak[q]
        pool_parts[core, 3 * q + 1] = mass[q]
        pool_parts[core, 3 * q + 2] = sums[q]
    here = pool_parts.at[core]
    swap = to_partner(here, here, pair_sems, 2)
    swap.start()
    swap.wait()

    level, grad_level, grad_mean = [], [], []
    for q in range(clouds):
        top = pool_parts[0, 3 * q]
        for c in range(1, cores):
            top = jnp.maximum(top, pool_parts[c, 3 * q])
        whole, sum_all = zero, zero
        for c in range(cores):
            whole = whole + pool_parts[c, 3 * q + 1] * jnp.exp(pool_parts[c, 3 * q] - top)
            sum_all = sum_all + pool_parts[c, 3 * q + 2]
        level.append(top + jnp.log(whole))
        size = jnp.full((SUBLANES, LANES), lengths[q].astype(F32), F32)
        first = level[q] - jnp.log(size)
        second = sum_all / size
        for h in range(2):
            pooled[q : q + 1, h * LANES : (h + 1) * LANES] = first[h : h + 1]
            pooled[q : q + 1, (2 + h) * LANES : (3 + h) * LANES] = second[h : h + 1]
        given = [pooled_grad[q : q + 1, h * LANES : (h + 1) * LANES] for h in range(4)]
        grad_level.append(jnp.where(odd, given[1], given[0]))
        grad_mean.append(jnp.where(odd, given[3], given[2]) / size)

    slope_rows, bias_rows = [], []
    for ref_value, target in ((gain2[...], slope_rows), (bias2[...], bias_rows)):
        low_half, high_half = lanes_to_rows(ref_value * LOG2E, width2)
        target.append(jnp.where(odd, high_half, low_half))
    inverse_gain = 1.0 / slope_rows[0]
    bias_row = bias_rows[0]

    def gradient(t, carry):
        rows = step_rows(t)
        inside = members(t)
        value = pick(inside, grad_level) * jnp.exp(level2[rows, :] - pick(inside, level))
        value = value + pick(inside, grad_mean)
        push2[rows, :] = value * inverse2[rows, :]
        share = share2[rows, :]
        moment = (share * (own_rows2[rows, :] - bias_row) + moment2[rows, :]) * inverse_gain
        given = value * share
        share2[rows, :] = given
        return carry[0] + given, carry[1] + value * moment

    state = lax.fori_loop(0, steps, gradient, (zero, zero))
    grad_beta, grad_gamma = [by_parity(value, jnp.add) for value in state]
    send_sums(2, [grad_beta[0:1], grad_beta[1:2], grad_gamma[0:1], grad_gamma[1:2]])

    x_high, x_low = split(x2[pl.ds(half, points), :])

    def linked2(start):
        rows = pl.ds(start, CHUNK)
        value = mm_low(links[rows, :], x_high) + mm_low(links[rows, :], x_low)
        weights = rows_to_lanes([counts[rows, :]] * 2)
        v2[rows, :] = mm_nt(value, direct2) + weights * (v2[rows, :] - mean2)

    over(both, CHUNK, linked2)
    receive(2)
    sums = slot_sum(slots.at[2], total)
    grad_beta = rows_to_lanes([sums[0:1], sums[1:2]])
    grad_gamma = rows_to_lanes([sums[2:3], sums[3:4]])
    scales2[1:2, :] = grad_beta
    scales2[2:3, :] = grad_gamma
    outer_scale = slope2 / count
    gamma_scale = outer_scale * grad_gamma * r2
    beta_scale = outer_scale * grad_beta

    def extra(start):
        rows = pl.ds(start, CHUNK)
        weights = rows_to_lanes([counts[rows, :]] * 2)
        extra2[rows, :] = weights * beta_scale + v2[rows, :] * gamma_scale

    over(both, CHUNK, extra)
    grad_own2[...] = jnp.zeros(grad_own2.shape, F32)

    def own(start):
        rows = pl.ds(start, CHUNK)
        weights = rows_to_lanes([live_col[rows, :]] * 2)
        given = rows_to_lanes(
            [share2[pl.ds(2 * start + h, CHUNK, stride=2), :] for h in range(2)]
        )
        away = depth * weights * (u2[rows, :] - mean2) + g2[rows, :]
        value = given * slope2 - (depth * weights * beta_scale + away * gamma_scale)
        own2[rows, :] = mm(value, direct2)
        grad_own2[...] += mm_tn(x2[pl.ds(half + start, CHUNK), :], value)

    over(points, CHUNK, own)


def scatter_loop(subs, depth, block, step, index, q_ref, push, sums):
    per = SUBLANES // subs
    groups = index.shape[0] // (depth * per)
    row = iota((SUBLANES, LANES), 0)
    mine = [(row >= subs * i) & (row < subs * (i + 1)) for i in range(per)]
    ways = len(sums) // per

    def one_group(place, carry):
        group = step * block + place
        rows = pl.ds(pl.multiple_of(group * SUBLANES, SUBLANES), SUBLANES)
        given = push[rows, :]
        for k in range(depth):
            value = q_ref[place, k] * given
            for i in range(per):
                j = index.at[pl.ds((k * per + i) * groups, groups)][group]
                target = sums[i * ways + k % ways].at[pl.ds(j, SUBLANES), :]
                pltpu.store(target, target[...] + value, mask=mine[i])
        return carry

    lax.fori_loop(0, block, one_group, 0)


def clear(sums):
    def rows8(start):
        for ref in sums:
            ref[pl.ds(start, SUBLANES), :] = jnp.zeros((SUBLANES, LANES), F32)

    over(sums[0].shape[0], SUBLANES, rows8)


def scatter2_kernel(depth, index, q_ref, push, x2, weight, scales, extra, near, grad_near, *sums):
    step = pl.program_id(0)
    both = x2.shape[0]
    width = x2.shape[1]

    @pl.when(step == 0)
    def _():
        clear(sums)

    scatter_loop(2, depth, q_ref.shape[0], step, index, q_ref, push, sums)

    @pl.when(step == pl.num_programs(0) - 1)
    def _():
        relative = weight[:, width:]
        grad_near[...] = jnp.zeros(grad_near.shape, F32)

        def finish(start):
            rows = pl.ds(start, CHUNK)
            halves = []
            for h in range(2):
                here = pl.ds(SUBLANES + 2 * start + h, CHUNK, stride=2)
                halves.append(tree([ref[here, :] for ref in sums], jnp.add))
            value = rows_to_lanes(halves) * scales[0:1, :] - extra[rows, :]
            near[rows, :] = mm(value, relative)
            grad_near[...] += mm_tn(x2[rows, :], value)

        over(both, CHUNK, finish)


def scatter1_kernel(
    depth, index, q_ref, grad, inverse, share, moment, near, given, parts, push, *sums
):
    step = pl.program_id(0)
    both = near.shape[0]

    @pl.when(step == 0)
    def _():
        clear(sums)
        push[...] = grad[...] * inverse[...]
        weighted = grad[...] * share[...]
        given[...] = weighted
        parts[...] = jnp.concatenate(
            [
                jnp.sum(weighted, axis=0, keepdims=True),
                jnp.sum(grad[...] * moment[...], axis=0, keepdims=True),
                jnp.zeros((6, LANES), F32),
            ],
            axis=0,
        )

    scatter_loop(1, depth, q_ref.shape[0], step, index, q_ref, push, sums)

    @pl.when(step == pl.num_programs(0) - 1)
    def _():
        def finish(start):
            here = pl.ds(SUBLANES + start, CHUNK)
            near[pl.ds(start, CHUNK), :] = tree([ref[here, :] for ref in sums], jnp.add)

        over(both, CHUNK, finish)


def last_kernel(
    sizes,
    depth,
    near1,
    given1,
    parts,
    x1,
    away_own1,
    away_all1,
    counts,
    scales1,
    live,
    weight1,
    grad_own2,
    grad_near2,
    grad_features,
    grad_weight1,
    grad_gain1,
    grad_bias1,
    grad_weight2,
    slots,
    flat,
    pushed,
    arrived,
    halved,
    landed,
    reduced,
    whole,
    small_sems,
    pair_sems,
    ring_sems,
):
    cores, chips = sizes
    total = cores * chips
    points = given1.shape[0]
    both = near1.shape[0]
    cin = x1.shape[1]
    width1 = weight1.shape[0]
    piece = landed.shape[1]
    core = lax.axis_index("points")
    chip = lax.axis_index("clouds")
    half = pl.multiple_of(core * points, points)
    barrier = pltpu.get_barrier_semaphore()
    signal_all(barrier, cores, total)
    pl.semaphore_wait(barrier, total - 1)
    gather_start(parts, slots, small_sems.at[0], small_sems.at[1], cores, total)

    flat[5 * LANES :, :] = jnp.zeros((flat.shape[0] - 5 * LANES, LANES), F32)
    for h in range(2):
        columns = slice(h * LANES, (h + 1) * LANES)
        flat[h * LANES : (h + 1) * LANES, :] = grad_own2[:, columns]
        flat[(2 + h) * LANES : (3 + h) * LANES, :] = grad_near2[:, columns] - grad_own2[:, columns]

    direct1 = weight1[:, :cin] - weight1[:, cin:]
    relative1 = weight1[:, cin:]
    slope = scales1[0:1, :]
    r1 = scales1[1:2, :]
    outer_scale = slope / scales1[2:3, :]
    gather_wait(slots, small_sems.at[0], small_sems.at[1], total)
    sums = slot_sum(slots, total)
    grad_bias1[...] = sums[0:1]
    grad_gain1[...] = sums[1:2]
    beta_scale = outer_scale * sums[0:1]
    gamma_scale = outer_scale * sums[1:2] * r1

    grad_near1 = jnp.zeros((cin, width1), F32)
    for c in range(cores):

        def push(i, total_near):
            start = pl.multiple_of(i * CHUNK, CHUNK)
            rows = pl.ds(c * points + start, CHUNK)
            value = near1[rows, :] * slope
            value = value - (counts[rows, :] * beta_scale + away_all1[rows, :] * gamma_scale)
            pushed[c, :, pl.ds(start, CHUNK)] = jnp.transpose(mm(value, relative1))
            return total_near + mm_tn(x1[rows, :], value)

        grad_near1 = lax.fori_loop(0, points // CHUNK, push, grad_near1)
    swap = to_partner(pushed.at[1 - core], arrived, pair_sems, 0)
    swap.start()

    def own(i, total_own):
        start = pl.multiple_of(i * CHUNK, CHUNK)
        rows = pl.ds(start, CHUNK)
        weights = jnp.transpose(live[:, rows])[:, :1]
        value = given1[rows, :] * slope
        value = value - (depth * weights * beta_scale + away_own1[rows, :] * gamma_scale)
        grad_features[:, rows] = jnp.transpose(mm(value, direct1)) + pushed[core, :, rows]
        return total_own + mm_tn(x1[pl.ds(half + start, CHUNK), :], value)

    grad_own1 = lax.fori_loop(0, points // CHUNK, own, jnp.zeros((cin, width1), F32))
    flat[4 * LANES : 4 * LANES + cin, :] = grad_own1
    flat[4 * LANES + cin : 4 * LANES + 2 * cin, :] = grad_near1 - grad_own1
    swap.wait()
    grad_features[...] += arrived[...]

    side = chips * piece
    mine = pl.multiple_of(core * side, SUBLANES)
    other = pl.multiple_of((1 - core) * side, SUBLANES)
    swap = to_partner(flat.at[pl.ds(other, side)], halved, pair_sems, 1)
    swap.start()
    swap.wait()
    flat[pl.ds(mine, side), :] += halved[...]
    landed[chip] = flat[pl.ds(pl.multiple_of(mine + chip * piece, SUBLANES), piece), :]

    def chip_copy(d, source, target, use):
        return pltpu.make_async_remote_copy(
            src_ref=source,
            dst_ref=target,
            send_sem=ring_sems.at[0, use],
            recv_sem=ring_sems.at[1, use],
            device_id=(lax.rem(chip + d, chips), core),
            device_id_type=MESH,
        )

    def scatter(d, carry):
        to = lax.rem(chip + d, chips)
        source = flat.at[pl.ds(pl.multiple_of(mine + to * piece, SUBLANES), piece)]
        chip_copy(d, source, landed.at[chip], 0).start()
        return carry

    lax.fori_loop(1, chips, scatter, 0)
    others = landed.at[pl.ds(0, chips - 1)]
    arrival = chip_copy(1, others, others, 0)
    arrival.wait_recv()
    arrival.wait_send()
    reduced[...] = slot_sum(landed, chips)
    whole[core, chip] = reduced[...]

    def spread(d, carry):
        chip_copy(d, reduced, whole.at[core, chip], 1).start()
        return carry

    lax.fori_loop(1, chips, spread, 0)
    others = landed.at[pl.ds(0, chips - 1)]
    arrival = chip_copy(1, others, others, 1)
    arrival.wait_recv()
    arrival.wait_send()
    swap = to_partner(whole.at[core], whole.at[core], pair_sems, 2)
    swap.start()
    swap.wait()
    final = whole.reshape(cores * side, LANES)
    for h in range(2):
        rows = slice(h * LANES, (h + 1) * LANES)
        grad_weight2[rows, 0:LANES] = jnp.transpose(final[h * LANES : (h + 1) * LANES, :])
        grad_weight2[rows, LANES : 2 * LANES] = jnp.transpose(
            final[(2 + h) * LANES : (3 + h) * LANES, :]
        )
    grad_weight1[...] = jnp.transpose(final[4 * LANES : 5 * LANES, :])


def shaped(*shape):
    return jax.ShapeDtypeStruct(shape, F32)


def scratch(*shape, dtype=F32):
    return pltpu.VMEM(shape, dtype)


def program(mesh):
    cores, chips = mesh.shape["points"], mesh.shape["clouds"]
    total = cores * chips

    def on_device(
        features,
        lengths,
        mask,
        neighbours,
        first_layer_weight,
        first_norm_gain,
        first_norm_bias,
        second_layer_weight,
        second_norm_gain,
        second_norm_bias,
        pooled_grad,
    ):
        cin, points = features.shape
        depth = neighbours.shape[0]
        width1, width2 = first_layer_weight.shape[0], second_layer_weight.shape[0]
        both = cores * points
        clouds = lengths.shape[0]
        live = jnp.broadcast_to(mask.astype(F32)[None, :], (SUBLANES, points))
        near = jnp.where(mask[None, :] > 0, neighbours, -1).astype(jnp.int16)
        near = jnp.broadcast_to(near[:, None, :], (depth, 16, points))

        def layout(subs):
            per = SUBLANES // subs
            value = neighbours.reshape(depth, points // per, per) * subs
            value = value + (SUBLANES - subs * jnp.arange(per, dtype=jnp.int32))
            return value.transpose(0, 2, 1).reshape(-1)

        index1, index2 = layout(1), layout(2)
        groups1, groups2 = points // SUBLANES, points // 4
        block = 32
        anywhere = pl.BlockSpec(memory_space=pl.ANY)
        outs = pl.pallas_call(
            functools.partial(forward_kernel, (cores, total)),
            out_shape=[
                shaped(clouds, 2 * width2),
                shaped(groups1, depth, SUBLANES, LANES),
                shaped(groups2, depth, SUBLANES, LANES),
                shaped(points, width1),
                shaped(points, width1),
                shaped(points, width1),
                shaped(both, cin),
                shaped(points, width1),
                shaped(both, width1),
                shaped(both, LANES),
                shaped(SUBLANES, width1),
                shaped(2 * points, LANES),
                shaped(both, width2),
                shaped(both, width1),
                shaped(points, width1),
                shaped(width1, width2),
                shaped(SUBLANES, width2),
            ],
            in_specs=[VMEM] * 3 + [SMEM] * 3 + [VMEM] * 7,
            out_specs=[VMEM, anywhere, anywhere] + [VMEM] * 14,
            scratch_shapes=[
                scratch(cores, cin, points),
                scratch(both, points, dtype=BF16),
                scratch(points, LANES),
                scratch(cores, 3 * cin, points, dtype=BF16),
                scratch(2 * width1, both, dtype=BF16),
                scratch(points, width1),
                scratch(both, width1),
                scratch(points, cin),
                scratch(points, width1),
                scratch(both + 2 * SUBLANES, LANES),
                scratch(points, LANES),
                scratch(points, LANES),
                scratch(2 * both + 2 * SUBLANES, LANES),
                scratch(2 * points, LANES),
                scratch(2 * points, LANES),
                scratch(2 * points, LANES),
                scratch(2 * points, LANES),
                scratch(2 * points, LANES),
                scratch(both, width1),
                scratch(points, width2),
                scratch(both, width2),
                scratch(points, width2),
                scratch(both, 2 * cin),
                scratch(cores, 3 * clouds, SUBLANES, LANES),
                scratch(3, 4, LANES),
                scratch(3, total, 4, LANES),
                scratch(depth, SUBLANES, LANES),
                scratch(depth, SUBLANES, LANES),
                scratch(2, block, depth, SUBLANES, LANES),
                pltpu.SemaphoreType.DMA((2, 3)),
                pltpu.SemaphoreType.DMA((2, 3)),
                pltpu.SemaphoreType.DMA((2,)),
            ],
            compiler_params=pltpu.CompilerParams(
                collective_id=1, has_side_effects=True, vmem_limit_bytes=MEMORY
            ),
            name="forward",
        )(
            features,
            near,
            live,
            index1,
            index2,
            lengths,
            first_layer_weight,
            first_norm_gain[None, :],
            first_norm_bias[None, :],
            second_layer_weight,
            second_norm_gain[None, :],
            second_norm_bias[None, :],
            pooled_grad,
        )
        (
            pooled,
            q1,
            q2,
            inverse1,
            share1,
            moment1,
            x1,
            away_own1,
            away_all1,
            counts,
            scales1,
            push2,
            extra2,
            x2,
            own2,
            grad_own2,
            scales2,
        ) = outs

        def q_blocks():
            return pl.BlockSpec((block, depth, SUBLANES, LANES), lambda s: (s, 0, 0, 0))

        near2, grad_near2 = pl.pallas_call(
            functools.partial(scatter2_kernel, depth),
            grid=(groups2 // block,),
            out_shape=[shaped(both, width1), shaped(width1, width2)],
            in_specs=[SMEM, q_blocks()] + [VMEM] * 5,
            out_specs=[VMEM, VMEM],
            scratch_shapes=[scratch(2 * both + 2 * SUBLANES, LANES)] * 8,
            compiler_params=pltpu.CompilerParams(vmem_limit_bytes=MEMORY),
            name="scatter2",
        )(index2, q2, push2, x2, second_layer_weight, scales2, extra2)

        core = lax.axis_index("points")
        sent = lax.dynamic_slice(near2, ((1 - core) * points, 0), (points, width1))
        kept = lax.dynamic_slice(near2, (core * points, 0), (points, width1))
        other = lax.ppermute(sent, "points", [(0, 1), (1, 0)])
        grad1 = own2 + kept + other

        near1, given1, parts = pl.pallas_call(
            functools.partial(scatter1_kernel, depth),
            grid=(groups1 // block,),
            out_shape=[shaped(both, width1), shaped(points, width1), shaped(SUBLANES, width1)],
            in_specs=[SMEM, q_blocks()] + [VMEM] * 4,
            out_specs=[VMEM] * 3,
            scratch_shapes=[scratch(points, width1)]
            + [scratch(both + 2 * SUBLANES, LANES)] * SUBLANES,
            compiler_params=pltpu.CompilerParams(vmem_limit_bytes=MEMORY),
            name="scatter1",
        )(index1, q1, grad1, inverse1, share1, moment1)

        piece = -(-5 * LANES // (total * SUBLANES)) * SUBLANES
        side = chips * piece
        grad_features, grad_weight1, grad_gain1, grad_bias1, grad_weight2 = pl.pallas_call(
            functools.partial(last_kernel, (cores, chips), depth),
            out_shape=[
                shaped(cin, points),
                shaped(width1, 2 * cin),
                shaped(1, width1),
                shaped(1, width1),
                shaped(width2, 2 * width1),
            ],
            in_specs=[VMEM] * 12,
            out_specs=[VMEM] * 5,
            scratch_shapes=[
                scratch(total, SUBLANES, LANES),
                scratch(cores * side, LANES),
                scratch(cores, cin, points),
                scratch(cin, points),
                scratch(side, LANES),
                scratch(chips, piece, LANES),
                scratch(piece, LANES),
                scratch(cores, chips, piece, LANES),
                pltpu.SemaphoreType.DMA((2,)),
                pltpu.SemaphoreType.DMA((2, 3)),
                pltpu.SemaphoreType.DMA((2, 2)),
            ],
            compiler_params=pltpu.CompilerParams(
                collective_id=2, has_side_effects=True, vmem_limit_bytes=MEMORY
            ),
            name="last",
        )(
            near1,
            given1,
            parts,
            x1,
            away_own1,
            away_all1,
            counts,
            scales1,
            live,
            first_layer_weight,
            grad_own2,
            grad_near2,
        )
        return (
            pooled,
            grad_features,
            grad_weight1,
            grad_gain1.reshape(width1),
            grad_bias1.reshape(width1),
            grad_weight2,
            scales2[2],
            scales2[1],
        )

    return on_device


def solution(mesh):
    in_specs = (
        P(None, ("clouds", "points")),
        P("clouds"),
        P(("clouds", "points")),
        P(None, ("clouds", "points")),
        P(),
        P(),
        P(),
        P(),
        P(),
        P(),
        P("clouds", None),
    )
    out_specs = (P("clouds", None), P(None, ("clouds", "points")), P(), P(), P(), P(), P(), P())
    return jax.shard_map(
        program(mesh), mesh=mesh, in_specs=in_specs, out_specs=out_specs, check_vma=False
    )
```

```python
import functools
import math

import jax
import jax.numpy as jnp
from jax import lax
from jax.experimental import pallas as pl
from jax.experimental.pallas import tpu as pltpu
from jax.sharding import PartitionSpec as P

EPSILON = 1e-05
LOG2E = math.log2(math.e)
LN2 = math.log(2.0)
MESH = pl.DeviceIdType.MESH
F32 = jnp.float32
BF16 = jnp.bfloat16
LANES = 128
SUBLANES = 8
CHUNK = 256
MEMORY = 60 * 2**20
VMEM = pl.BlockSpec(memory_space=pltpu.VMEM)
SMEM = pl.BlockSpec(memory_space=pltpu.SMEM)
ANY = pl.BlockSpec(memory_space=pl.ANY)


def dot(left, right, dims):
    return lax.dot_general(
        left,
        right,
        (dims, ((), ())),
        precision=lax.Precision.HIGHEST,
        preferred_element_type=F32,
    )


def mm(left, right):
    return dot(left, right, ((1,), (0,)))


def mm_nt(left, right):
    return dot(left, right, ((1,), (1,)))


def mm_tn(left, right):
    return dot(left, right, ((0,), (0,)))


def mm_low(left, right):
    return lax.dot_general(
        left, right, (((1,), (0,)), ((), ())), preferred_element_type=F32
    )


def split(value):
    high = value.astype(BF16)
    low = (value - high.astype(F32)).astype(BF16)
    return high, low


def product(left, right, dims):
    def part(a, b):
        return lax.dot_general(a, b, (dims, ((), ())), preferred_element_type=F32)

    left_high, left_low = split(left)
    right_high, right_low = split(right)
    return part(left_high, right_high) + (part(left_high, right_low) + part(left_low, right_high))


def by(left, right):
    return product(left, right, ((1,), (0,)))


def by_t(left, right):
    return product(left, right, ((1,), (1,)))


def t_by(left, right):
    return product(left, right, ((0,), (0,)))


def over(count, step, body):
    def run(i, carry):
        body(pl.multiple_of(i * step, step))
        return carry

    lax.fori_loop(0, count // step, run, 0)


def log2(value):
    return jnp.log(value) * LOG2E


def tree(values, join):
    values = list(values)
    while len(values) > 1:
        values = [
            join(values[i], values[i + 1]) if i + 1 < len(values) else values[i]
            for i in range(0, len(values), 2)
        ]
    return values[0]


def iota(shape, dim):
    return lax.broadcasted_iota(jnp.int32, shape, dim)


def signal_all(barrier, cores, total):
    me = lax.axis_index("clouds") * cores + lax.axis_index("points")

    def send(d, carry):
        t = lax.rem(me + d, total)
        pl.semaphore_signal(
            barrier,
            inc=1,
            device_id=(lax.div(t, cores), lax.rem(t, cores)),
            device_id_type=MESH,
        )
        return carry

    lax.fori_loop(1, total, send, 0)


def gather_start(own, slots, send_sem, recv_sem, cores, total):
    me = lax.axis_index("clouds") * cores + lax.axis_index("points")
    slots[me] = own[...]

    def send(d, carry):
        t = lax.rem(me + d, total)
        pltpu.make_async_remote_copy(
            src_ref=own,
            dst_ref=slots.at[me],
            send_sem=send_sem,
            recv_sem=recv_sem,
            device_id=(lax.div(t, cores), lax.rem(t, cores)),
            device_id_type=MESH,
        ).start()
        return carry

    lax.fori_loop(1, total, send, 0)


def gather_wait(slots, send_sem, recv_sem, total):
    others = slots.at[pl.ds(0, total - 1)]
    arrived = pltpu.make_async_remote_copy(
        src_ref=others,
        dst_ref=others,
        send_sem=send_sem,
        recv_sem=recv_sem,
        device_id=(lax.axis_index("clouds"), 1 - lax.axis_index("points")),
        device_id_type=MESH,
    )
    arrived.wait_recv()
    arrived.wait_send()


def slot_sum(slots, total):
    def add(i, carry):
        return carry + slots[i]

    return lax.fori_loop(1, total, add, slots[0])


def to_partner(source, target, sems, index):
    return pltpu.make_async_remote_copy(
        src_ref=source,
        dst_ref=target,
        send_sem=sems.at[0, index],
        recv_sem=sems.at[1, index],
        device_id=(lax.axis_index("clouds"), 1 - lax.axis_index("points")),
        device_id_type=MESH,
    )


def edge_pass(subs, block, depth, part, index, table, own_rows, out_hbm, held, ring, sems, outs):
    level_ref, share_ref, moment_ref, inverse_ref = outs
    per = SUBLANES // subs
    groups = own_rows.shape[0] // SUBLANES
    stages = depth // part
    row = iota((SUBLANES, LANES), 0)
    mine = [(row >= subs * i) & (row < subs * (i + 1)) for i in range(per)]
    zero = jnp.zeros((SUBLANES, LANES), F32)

    def fetch(group, stage, slot):
        for k in range(part):
            target = held[slot].at[stage * part + k]
            for i in range(per):
                first = (k * per + i) * groups
                if stages > 1:
                    span = groups * (1 + (stages - 1) * part * per)
                    j = index.at[pl.ds(first, span)][stage * (part * per * groups) + group]
                else:
                    j = index.at[pl.ds(first, groups)][group]
                value = table[pl.ds(j, SUBLANES), :]
                if i == 0:
                    target[...] = value
                else:
                    pltpu.store(target, value, mask=mine[i])

    def work(group, stage, slot, ring_slot, place, carry):
        total0, share0, moment0 = carry
        rows = pl.ds(pl.multiple_of(group * SUBLANES, SUBLANES), SUBLANES)
        peak = tree([held[slot][k] for k in range(depth)], jnp.maximum)
        top = own_rows[rows, :] + peak
        shift = jnp.maximum(top, 0.0)
        rest = jnp.maximum(jnp.exp2(-shift), 2.0**-100)
        scale = jnp.exp2(top - shift)
        fifth = 0.2 * rest
        total, share, moment = [], [], []
        for k in range(part):
            value = held[slot][stage * part + k]
            away = value - peak
            grown = scale * jnp.exp2(away)
            root = jnp.exp2((away - log2(rest + grown)) * 0.2)
            weight = root * (fifth + grown)
            ring[ring_slot, place, stage * part + k] = weight
            total.append(root)
            share.append(weight)
            moment.append(weight * value)
        total, share, moment = [
            functools.reduce(jnp.add, parts) for parts in (total, share, moment)
        ]
        if stages > 1:
            start = stage == 0
            total = total + jnp.where(start, 0.0, total0)
            share = share + jnp.where(start, 0.0, share0)
            moment = moment + jnp.where(start, 0.0, moment0)
        mass = share + (0.8 * rest) * total
        inverse = 1.0 / mass
        level_ref[rows, :] = LN2 * (0.2 * top + 0.8 * shift + log2(mass)) - math.log(depth)
        inverse_ref[rows, :] = inverse
        share_ref[rows, :] = share * inverse
        moment_ref[rows, :] = moment * inverse
        return total, share, moment

    blocks = groups // block

    def push(b, slot):
        return pltpu.make_async_copy(
            ring.at[slot], out_hbm.at[pl.ds(b * block, block)], sems.at[slot]
        )

    for stage in range(stages):
        fetch(0, stage, 0)

    def one_block(b, carry):
        ring_slot = lax.rem(b, 2)

        @pl.when(b >= 2)
        def _():
            push(b - 2, ring_slot).wait()

        def pair(t, inner):
            for slot in range(2):
                place = t * 2 + slot
                group = b * block + place
                after = jnp.minimum(group + 1, groups - 1)
                if stages == 1:
                    work(group, 0, slot, ring_slot, place, (zero,) * 3)
                    fetch(after, 0, 1 - slot)
                else:

                    def one_stage(stage, sums):
                        sums = work(group, stage, slot, ring_slot, place, sums)
                        fetch(after, stage, 1 - slot)
                        return sums

                    lax.fori_loop(0, stages, one_stage, (zero,) * 3)
            return inner

        lax.fori_loop(0, block // 2, pair, 0)
        push(b, ring_slot).start()
        return carry

    lax.fori_loop(0, blocks, one_block, 0)
    if blocks > 1:
        push(blocks - 2, (blocks - 2) % 2).wait()
    push(blocks - 1, (blocks - 1) % 2).wait()


def lanes_to_rows(value, width):
    return [value[:, i * LANES : (i + 1) * LANES] for i in range(width // LANES)]


def rows_to_lanes(rows):
    return rows[0] if len(rows) == 1 else jnp.concatenate(rows, axis=1)


def forward_kernel(
    sizes,
    feat,
    near,
    mask,
    index1_in,
    index2_in,
    lengths,
    weight1,
    gain1,
    bias1,
    weight2_in,
    gain2,
    bias2,
    pooled_grad,
    pooled,
    q1,
    q2,
    inverse1_out,
    share1_out,
    moment1_out,
    x1_out,
    away_own1_out,
    away_all1_out,
    counts_out,
    x2_out,
    scales1,
    push2,
    extra2,
    own2,
    grad_own2,
    scales2,
    index1,
    index2,
    weight2,
    inverse1,
    share1,
    moment1,
    x1,
    away_own1,
    away_all1,
    counts,
    x1_cm,
    tallies,
    links,
    live,
    live_col,
    parts1,
    parts2,
    u1,
    v1,
    n1,
    g1,
    table1,
    own_rows1,
    level1,
    share_rows1,
    moment_rows1,
    table2,
    own_rows2,
    level2,
    share2,
    moment2,
    inverse2,
    x2,
    u2,
    v2,
    g2,
    u_parts,
    pool_parts,
    message,
    slots,
    held0,
    held1,
    ring,
    pair_sems,
    all_sems,
    ring_sems,
    load_sems,
    store_sems,
):
    cores, total = sizes
    points = feat.shape[1]
    cin = feat.shape[0]
    both = cores * points
    depth = near.shape[0]
    width1 = weight1.shape[0]
    width2 = gain2.shape[1]
    groups1, groups2 = points // SUBLANES, 2 * points // SUBLANES
    core = lax.axis_index("points")
    half = pl.multiple_of(core * points, points)
    barrier = pltpu.get_barrier_semaphore()
    signal_all(barrier, cores, total)
    loads = [
        pltpu.make_async_copy(source, target, load_sems.at[i])
        for i, (source, target) in enumerate(
            ((index1_in, index1), (index2_in, index2), (weight2_in, weight2))
        )
    ]
    for copy in loads:
        copy.start()
    stores = [
        pltpu.make_async_copy(source, target, store_sems.at[i])
        for i, (source, target) in enumerate(
            (
                (x1, x1_out),
                (counts, counts_out),
                (away_own1, away_own1_out),
                (away_all1, away_all1_out),
                (inverse1, inverse1_out),
                (share1, share1_out),
                (moment1, moment1_out),
                (x2, x2_out),
            )
        )
    ]

    live[...] = jnp.broadcast_to(mask[...].astype(F32), live.shape)
    row16 = iota((16, LANES), 0)
    one, none = jnp.ones((16, LANES), BF16), jnp.zeros((16, LANES), BF16)

    def build(columns, first):
        names = []
        for k in range(depth):
            name = jnp.where(mask[:, columns] > 0, near[k : k + 1, columns], -1)
            names.append(jnp.broadcast_to(name, (16, LANES)).astype(jnp.int16))

        def rows64(start):
            for s in range(0, 64, 16):
                target = (row16 + (start + s)).astype(jnp.int16)
                found = [jnp.where(name == target, one, none) for name in names]
                found = tree(found, jnp.add)
                links[pl.ds(start + s, 16), columns] = found
                here = pl.ds(start + s, 16)
                tallies[here, :] = found if first else tallies[here, :] + found

        over(both, 64, rows64)

    tiles = points // LANES
    early = tiles - tiles // 4
    for tile in range(early):
        build(pl.ds(tile * LANES, LANES), tile == 0)
    x1_cm[core] = feat[...]
    pl.semaphore_wait(barrier, total - 1)
    swap = to_partner(feat, x1_cm.at[core], pair_sems, 0)
    swap.start()
    for tile in range(early, tiles):
        build(pl.ds(tile * LANES, LANES), tile == 0)
    live_col[...] = jnp.broadcast_to(jnp.transpose(live[...])[:, :1], live_col.shape)
    swap.wait()

    direct1 = weight1[:, :cin] - weight1[:, cin:]
    relative1 = weight1[:, cin:]
    for c in range(cores):

        def turn(start):
            x1[pl.ds(c * points + start, CHUNK), :] = jnp.transpose(
                x1_cm[c, :, pl.ds(start, CHUNK)]
            )

        over(points, CHUNK, turn)
        value = x1_cm[c]
        high, low = split(value)
        lower = (value - high.astype(F32) - low.astype(F32)).astype(BF16)
        parts1[c, 0:cin, :] = high
        parts1[c, cin : 2 * cin, :] = low
        parts1[c, 2 * cin : 3 * cin, :] = lower

    def sums_near1(start):
        columns = pl.ds(start, CHUNK)
        value = mm_low(parts1[0], links[0:points, columns])
        for c in range(1, cores):
            value = value + mm_low(parts1[c], links[c * points : (c + 1) * points, columns])
        value = value[0:cin] + value[cin : 2 * cin] + value[2 * cin : 3 * cin]
        n1[columns, :] = jnp.transpose(value)

    over(points, CHUNK, sums_near1)

    stores[0].start()
    ones = jnp.ones((LANES, LANES), BF16)

    def count_links(start):
        rows = pl.ds(start, CHUNK)
        counts[rows, :] = mm_low(tallies[rows, :], ones)

    over(both, CHUNK, count_links)
    stores[1].start()

    live_sum = jnp.sum(live[0:1, :], axis=1, keepdims=True)
    mine = live_sum * depth

    def live_total(start, size, value):
        high, low = split(value)
        weights = live[:, start : start + size].astype(BF16)
        return (mm_low(weights, high) + mm_low(weights, low))[0:1]

    def statistics(x_all, n_ref, direct, relative, u, v, g, width):
        def outer(start):
            rows = pl.ds(start, CHUNK)
            v[rows, :] = mm_nt(x_all[rows, :], relative)

        over(both, CHUNK, outer)

        def inner(start):
            rows = pl.ds(start, CHUNK)
            u[rows, :] = mm_nt(x_all[pl.ds(half + start, CHUNK), :], direct)
            g[rows, :] = mm_nt(n_ref[rows, :], relative)

        over(points, CHUNK, inner)
        u_sum = live_total(0, points, u[...])
        g_sum = jnp.sum(g[...], axis=0, keepdims=True)
        u_mean = u_sum / live_sum
        v_mean = g_sum / mine
        centred = u[...] - u_mean
        spread = depth * centred * centred + 2.0 * centred * (g[...] - depth * v_mean)
        square = live_total(0, points, spread)
        weights = rows_to_lanes([counts[...]] * (width // LANES))
        away = v[...] - v_mean
        square = square + jnp.sum(weights * away * away, axis=0, keepdims=True)
        return depth * u_sum + g_sum, square, u_mean, v_mean

    def send_sums(use, rows):
        for i, value in enumerate(rows):
            message[use, i : i + 1, :] = value
        gather_start(
            message.at[use], slots.at[use], all_sems.at[0, use], all_sems.at[1, use], cores, total
        )

    def receive(use):
        gather_wait(slots.at[use], all_sems.at[0, use], all_sems.at[1, use], total)

    def combine(use, numbers, width):
        per = width // LANES
        count = numbers[0]
        for value in numbers[1:]:
            count = count + value

        def value_of(i, first):
            return rows_to_lanes([slots[use, i, first + h : first + h + 1, :] for h in range(per)])

        mean = value_of(0, 0)
        for i in range(1, total):
            mean = mean + value_of(i, 0)
        mean = mean / count
        square = None
        for i in range(total):
            gap = value_of(i, 0) / numbers[i] - mean
            term = value_of(i, per) + numbers[i] * gap * gap
            square = term if square is None else square + term
        return count, mean, square / count

    sums, square, u_mean1, v_mean1 = statistics(x1, n1, direct1, relative1, u1, v1, g1, width1)
    send_sums(0, [sums, square, jnp.broadcast_to(mine, (1, LANES)), jnp.zeros((1, LANES), F32)])

    for part, value in enumerate(split(u1[...] - u_mean1)):
        u_parts[:, part * LANES : (part + 1) * LANES] = value

    def shared1(start):
        rows = pl.ds(start, CHUNK)
        value = mm_low(links[rows, :], u_parts[:, 0 : 2 * LANES])
        away_all1[rows, :] = value[:, :LANES] + value[:, LANES:]

    over(both, CHUNK, shared1)
    receive(0)
    numbers = [slots[0, i, 2:3, 0:1] for i in range(total)]
    count, mean1, variance1 = combine(0, numbers, width1)
    r1 = lax.rsqrt(variance1 + EPSILON)
    slope1 = gain1[...] * r1
    scales1[...] = jnp.concatenate(
        [slope1, r1, jnp.broadcast_to(count, (1, LANES)), jnp.zeros((5, LANES), F32)], axis=0
    )

    def fill1(start):
        rows = pl.ds(start, CHUNK)
        table1[pl.ds(SUBLANES + start, CHUNK), :] = (v1[rows, :] - v_mean1) * (slope1 * LOG2E)
        away_all1[rows, :] += counts[rows, :] * (v1[rows, :] - (mean1 - u_mean1))

    over(both, CHUNK, fill1)

    def fill_own1(start):
        rows = pl.ds(start, CHUNK)
        value = (u1[rows, :] - (mean1 - v_mean1)) * (slope1 * LOG2E) + bias1[...] * LOG2E
        for s in range(0, CHUNK, groups1):
            here = pl.ds(lax.div(start, groups1) + s // groups1, groups1, stride=SUBLANES)
            own_rows1[here, :] = value[s : s + groups1]
        away_own1[rows, :] = depth * live_col[rows, :] * (u1[rows, :] - mean1) + g1[rows, :]

    over(points, CHUNK, fill_own1)

    stores[2].start()
    stores[3].start()
    loads[0].wait()
    edge_pass(
        1,
        ring.shape[1],
        depth,
        depth // 2,
        index1,
        table1,
        own_rows1,
        q1,
        (held0, held1),
        ring,
        ring_sems,
        (level1, share_rows1, moment_rows1, inverse1),
    )

    inverse_gain1 = 1.0 / (gain1[...] * LOG2E)
    for i in range(SUBLANES):
        here = pl.ds(i, groups1, stride=SUBLANES)
        x2[pl.ds(half + i * groups1, groups1), :] = level1[here, :]
        offset = own_rows1[here, :] - bias1[...] * LOG2E
        rows = slice(i * groups1, (i + 1) * groups1)
        moment1[rows, :] = (share_rows1[here, :] * offset + moment_rows1[here, :]) * inverse_gain1
        share1[rows, :] = share_rows1[here, :]
    for copy in stores[4:7]:
        copy.start()
    here = x2.at[pl.ds(half, points)]
    swap = to_partner(here, here, pair_sems, 1)
    swap.start()
    loads[1].wait()
    loads[2].wait()
    swap.wait()
    stores[7].start()

    direct2 = weight2[:, :width1] - weight2[:, width1:]
    relative2 = weight2[:, width1:]

    def turn2(start):
        high, low = split(jnp.transpose(x2[pl.ds(start, CHUNK), :]))
        parts2[0:width1, pl.ds(start, CHUNK)] = high
        parts2[width1 : 2 * width1, pl.ds(start, CHUNK)] = low

    over(both, CHUNK, turn2)

    def sums_near2(start):
        columns = pl.ds(start, CHUNK)
        value = mm_low(parts2[...], links[:, columns])
        value = value[0:width1] + value[width1 : 2 * width1]
        g2[columns, :] = mm_nt(jnp.transpose(value), relative2)

    over(points, CHUNK, sums_near2)

    def statistics2():
        def outer(start):
            rows = pl.ds(start, CHUNK)
            v2[rows, :] = mm_nt(x2[rows, :], relative2)

        over(both, CHUNK, outer)

        def inner(start):
            u2[pl.ds(start, CHUNK), :] = mm_nt(x2[pl.ds(half + start, CHUNK), :], direct2)

        over(points, CHUNK, inner)
        u_sum = jnp.zeros((1, width2), F32)
        g_sum = jnp.zeros((1, width2), F32)
        for s in range(0, points, CHUNK):
            u_sum = u_sum + live_total(s, CHUNK, u2[s : s + CHUNK, :])
            g_sum = g_sum + jnp.sum(g2[s : s + CHUNK, :], axis=0, keepdims=True)
        u_mean = u_sum / live_sum
        v_mean = g_sum / mine
        square = jnp.zeros((1, width2), F32)
        for s in range(0, points, CHUNK):
            centred = u2[s : s + CHUNK, :] - u_mean
            spread = depth * centred * centred + 2.0 * centred * (
                g2[s : s + CHUNK, :] - depth * v_mean
            )
            square = square + live_total(s, CHUNK, spread)

        def squares(i, carry):
            rows = pl.ds(pl.multiple_of(i * CHUNK, CHUNK), CHUNK)
            away = v2[rows, :] - v_mean
            weights = rows_to_lanes([counts[rows, :]] * (width2 // LANES))
            return carry + jnp.sum(weights * away * away, axis=0, keepdims=True)

        square = lax.fori_loop(0, both // CHUNK, squares, square)
        return depth * u_sum + g_sum, square, u_mean, v_mean

    sums, square, u_mean2, v_mean2 = statistics2()
    send_sums(1, lanes_to_rows(sums, width2) + lanes_to_rows(square, width2))
    for part, value in enumerate(split(u2[...] - u_mean2)):
        u_parts[:, part * width2 : (part + 1) * width2] = value

    def shared2(start):
        rows = pl.ds(start, CHUNK)
        extra2[rows, :] = mm_low(links[rows, :], u_parts[:, 0:width2]) + mm_low(
            links[rows, :], u_parts[:, width2:]
        )

    over(both, CHUNK, shared2)
    receive(1)
    count, mean2, variance2 = combine(1, numbers, width2)
    r2 = lax.rsqrt(variance2 + EPSILON)
    slope2 = gain2[...] * r2
    scales2[...] = jnp.concatenate([slope2, jnp.zeros((7, width2), F32)], axis=0)

    def fill2(start):
        rows = pl.ds(start, CHUNK)
        value = (v2[rows, :] - v_mean2) * (slope2 * LOG2E)
        for h in range(2):
            table2[pl.ds(SUBLANES + 2 * start + h, CHUNK, stride=2), :] = value[
                :, h * LANES : (h + 1) * LANES
            ]

    over(both, CHUNK, fill2)

    for i in range(SUBLANES // 2):
        rows = slice(i * groups2, (i + 1) * groups2)
        value = (u2[rows, :] - (mean2 - v_mean2)) * (slope2 * LOG2E) + bias2[...] * LOG2E
        for h in range(2):
            own_rows2[pl.ds(2 * i + h, groups2, stride=SUBLANES), :] = value[
                :, h * LANES : (h + 1) * LANES
            ]

    edge_pass(
        2,
        ring.shape[1],
        depth,
        depth,
        index2,
        table2,
        own_rows2,
        q2,
        (held0, held1),
        ring,
        ring_sems,
        (level2, share2, moment2, inverse2),
    )

    clouds = pooled_grad.shape[0]
    ends = [lengths[0]]
    for q in range(1, clouds):
        ends.append(ends[-1] + lengths[q])
    row = iota((SUBLANES, LANES), 0)
    odd = lax.rem(row, 2) == 1
    point_of_row = half + lax.div(row, 2) * groups2
    steps = level2.shape[0] // SUBLANES
    lowest = jnp.full((SUBLANES, LANES), -1e30, F32)
    zero = jnp.zeros((SUBLANES, LANES), F32)

    def past(t):
        position = point_of_row + t
        return [position >= ends[q] for q in range(clouds - 1)]

    def pick(after, values):
        value = values[0]
        for q in range(1, clouds):
            value = jnp.where(after[q - 1], values[q], value)
        return value

    def apart(after, value, none):
        out = []
        for q in range(clouds):
            kept = value if q == 0 else jnp.where(after[q - 1], value, none)
            out.append(kept if q == clouds - 1 else jnp.where(after[q], none, kept))
        return out

    def step_rows(t):
        return pl.ds(pl.multiple_of(t * SUBLANES, SUBLANES), SUBLANES)

    def by_parity(value, join):
        value = join(value, pltpu.roll(value, 2, 0))
        return join(value, pltpu.roll(value, 4, 0))

    def unrolled(body, state, times):
        def several(i, carry):
            for u in range(times):
                carry = body(i * times + u, carry)
            return carry

        return lax.fori_loop(0, steps // times, several, state)

    def peaks(t, carry):
        value = level2[step_rows(t), :]
        after = past(t)
        tops = [jnp.maximum(a, b) for a, b in zip(carry, apart(after, value, lowest))]
        adds = [a + b for a, b in zip(carry[clouds:], apart(after, value, zero))]
        return tuple(tops + adds)

    state = unrolled(peaks, (lowest,) * clouds + (zero,) * clouds, 8)
    peak = [by_parity(value, jnp.maximum) for value in state[:clouds]]
    sums = [by_parity(value, jnp.add) for value in state[clouds:]]

    def masses(t, carry):
        after = past(t)
        value = jnp.exp(level2[step_rows(t), :] - pick(after, peak))
        return tuple(a + b for a, b in zip(carry, apart(after, value, zero)))

    state = unrolled(masses, (zero,) * clouds, 8)
    mass = [by_parity(value, jnp.add) for value in state]
    for q in range(clouds):
        pool_parts[core, 3 * q] = peak[q]
        pool_parts[core, 3 * q + 1] = mass[q]
        pool_parts[core, 3 * q + 2] = sums[q]
    here = pool_parts.at[core]
    swap = to_partner(here, here, pair_sems, 2)
    swap.start()
    swap.wait()

    level, grad_level, grad_mean = [], [], []
    for q in range(clouds):
        top = pool_parts[0, 3 * q]
        for c in range(1, cores):
            top = jnp.maximum(top, pool_parts[c, 3 * q])
        whole, sum_all = zero, zero
        for c in range(cores):
            whole = whole + pool_parts[c, 3 * q + 1] * jnp.exp(pool_parts[c, 3 * q] - top)
            sum_all = sum_all + pool_parts[c, 3 * q + 2]
        level.append(top + jnp.log(whole))
        size = jnp.full((SUBLANES, LANES), lengths[q].astype(F32), F32)
        first = level[q] - jnp.log(size)
        second = sum_all / size
        for h in range(2):
            pooled[q : q + 1, h * LANES : (h + 1) * LANES] = first[h : h + 1]
            pooled[q : q + 1, (2 + h) * LANES : (3 + h) * LANES] = second[h : h + 1]
        given = [pooled_grad[q : q + 1, h * LANES : (h + 1) * LANES] for h in range(4)]
        grad_level.append(jnp.where(odd, given[1], given[0]))
        grad_mean.append(jnp.where(odd, given[3], given[2]) / size)

    slope_rows, bias_rows = [], []
    for ref_value, target in ((gain2[...], slope_rows), (bias2[...], bias_rows)):
        low_half, high_half = lanes_to_rows(ref_value * LOG2E, width2)
        target.append(jnp.where(odd, high_half, low_half))
    inverse_gain = 1.0 / slope_rows[0]
    bias_row = bias_rows[0]

    def gradient(t, carry):
        rows = step_rows(t)
        after = past(t)
        value = pick(after, grad_level) * jnp.exp(level2[rows, :] - pick(after, level))
        value = value + pick(after, grad_mean)
        push2[rows, :] = value * inverse2[rows, :]
        share = share2[rows, :]
        moment = (share * (own_rows2[rows, :] - bias_row) + moment2[rows, :]) * inverse_gain
        given = value * share
        share2[rows, :] = given
        return carry[0] + given, carry[1] + value * moment

    state = unrolled(gradient, (zero, zero), 8)
    grad_beta, grad_gamma = [by_parity(value, jnp.add) for value in state]
    send_sums(2, [grad_beta[0:1], grad_beta[1:2], grad_gamma[0:1], grad_gamma[1:2]])

    receive(2)
    sums = slot_sum(slots.at[2], total)
    grad_beta = rows_to_lanes([sums[0:1], sums[1:2]])
    grad_gamma = rows_to_lanes([sums[2:3], sums[3:4]])
    scales2[1:2, :] = grad_beta
    scales2[2:3, :] = grad_gamma
    outer_scale = slope2 / count
    gamma_scale = outer_scale * grad_gamma * r2
    beta_scale = outer_scale * grad_beta

    def extra(start):
        rows = pl.ds(start, CHUNK)
        weights = rows_to_lanes([counts[rows, :]] * 2)
        away = extra2[rows, :] + weights * (v2[rows, :] - (mean2 - u_mean2))
        extra2[rows, :] = weights * beta_scale + away * gamma_scale

    over(both, CHUNK, extra)
    grad_own2[...] = jnp.zeros(grad_own2.shape, F32)

    for i in range(SUBLANES // 2):
        rows = slice(i * groups2, (i + 1) * groups2)
        weights = rows_to_lanes([live_col[rows, :]] * 2)
        given = rows_to_lanes(
            [share2[pl.ds(2 * i + h, groups2, stride=SUBLANES), :] for h in range(2)]
        )
        away = depth * weights * (u2[rows, :] - mean2) + g2[rows, :]
        value = given * slope2 - (depth * weights * beta_scale + away * gamma_scale)
        own2[rows, :] = by(value, direct2)
        grad_own2[...] += t_by(x2[pl.ds(half + i * groups2, groups2), :], value)
    for copy in stores:
        copy.wait()


def scatter_loop(subs, depth, index, q_hbm, ring, sems, push, sums, clear):
    per = SUBLANES // subs
    groups = q_hbm.shape[0]
    slots, block = ring.shape[0], ring.shape[1]
    blocks = groups // block
    row = iota((SUBLANES, LANES), 0)
    mine = [(row >= subs * i) & (row < subs * (i + 1)) for i in range(per)]
    ways = len(sums) // per

    def pull(b):
        slot = lax.rem(b, slots)
        return pltpu.make_async_copy(
            q_hbm.at[pl.ds(b * block, block)], ring.at[slot], sems.at[slot]
        )

    for b in range(slots - 1):
        pull(b).start()
    clear()

    def one_block(b, carry):
        @pl.when(b + slots - 1 < blocks)
        def _():
            pull(b + slots - 1).start()

        pull(b).wait()
        slot = lax.rem(b, slots)

        def one_group(place, inner):
            group = b * block + place
            rows = pl.ds(pl.multiple_of(group * SUBLANES, SUBLANES), SUBLANES)
            given = push[rows, :]
            for k in range(depth):
                value = ring[slot, place, k] * given
                for i in range(per):
                    j = index.at[pl.ds((k * per + i) * groups, groups)][group]
                    target = sums[i * ways + k % ways].at[pl.ds(j, SUBLANES), :]
                    pltpu.store(target, target[...] + value, mask=mine[i])
            return inner

        lax.fori_loop(0, block, one_group, 0)
        return carry

    lax.fori_loop(0, blocks, one_block, 0)


def clear(sums):
    rows = sums[0].shape[0]
    zero = jnp.zeros((SUBLANES, LANES), F32)

    def rows32(start):
        for ref in sums:
            for s in range(0, 4 * SUBLANES, SUBLANES):
                ref[pl.ds(start + s, SUBLANES), :] = zero

    over(rows, 4 * SUBLANES, rows32)
    for s in range(rows // 32 * 32, rows, SUBLANES):
        for ref in sums:
            ref[s : s + SUBLANES, :] = zero


def scatter2_kernel(
    depth,
    index_in,
    q_hbm,
    push_in,
    x2_in,
    weight_in,
    scales,
    extra_in,
    kept,
    sent,
    grad_near,
    index,
    push,
    x2,
    weight,
    extra,
    ring,
    load_sems,
    ring_sems,
    *sums,
):
    loads = [
        pltpu.make_async_copy(source, target, load_sems.at[i])
        for i, (source, target) in enumerate(
            ((index_in, index), (push_in, push), (x2_in, x2), (weight_in, weight), (extra_in, extra))
        )
    ]

    def prepare():
        clear(sums)
        loads[0].wait()
        loads[1].wait()

    for copy in loads:
        copy.start()
    scatter_loop(2, depth, index, q_hbm, ring, ring_sems, push, sums, prepare)
    for copy in loads[2:]:
        copy.wait()
    points, width = kept.shape
    relative = weight[:, width:]
    core = lax.axis_index("points")
    grad_near[...] = jnp.zeros(grad_near.shape, F32)
    for part, out in ((1 - core, sent), (core, kept)):

        def finish(start):
            first = pl.multiple_of(part * points + start, CHUNK)
            rows = pl.ds(first, CHUNK)
            halves = []
            for h in range(2):
                here = pl.ds(SUBLANES + 2 * first + h, CHUNK, stride=2)
                halves.append(tree([ref[here, :] for ref in sums], jnp.add))
            value = rows_to_lanes(halves) * scales[0:1, :] - extra[rows, :]
            out[pl.ds(start, CHUNK), :] = by(value, relative)
            grad_near[...] += t_by(x2[rows, :], value)

        over(points, CHUNK, finish)


def scatter1_kernel(
    depth,
    index_in,
    q_hbm,
    own,
    kept,
    other,
    inverse,
    share,
    moment,
    near,
    given,
    parts,
    index,
    push,
    ring,
    load_sems,
    ring_sems,
    *sums,
):
    load = pltpu.make_async_copy(index_in, index, load_sems.at[0])
    load.start()

    def prepare():
        clear(sums)
        groups = own.shape[0] // SUBLANES
        grad_beta = jnp.zeros((1, LANES), F32)
        grad_gamma = jnp.zeros((1, LANES), F32)
        for i in range(SUBLANES):
            here = pl.ds(i, groups, stride=SUBLANES)
            rows = slice(i * groups, (i + 1) * groups)
            grad = own[rows, :] + kept[rows, :] + other[rows, :]
            push[here, :] = grad * inverse[here, :]
            weighted = grad * share[rows, :]
            given[rows, :] = weighted
            grad_beta = grad_beta + jnp.sum(weighted, axis=0, keepdims=True)
            grad_gamma = grad_gamma + jnp.sum(grad * moment[rows, :], axis=0, keepdims=True)
        parts[...] = jnp.concatenate([grad_beta, grad_gamma, jnp.zeros((6, LANES), F32)], axis=0)
        load.wait()

    scatter_loop(1, depth, index, q_hbm, ring, ring_sems, push, sums, prepare)

    def finish(start):
        here = pl.ds(SUBLANES + start, CHUNK)
        near[pl.ds(start, CHUNK), :] = tree([ref[here, :] for ref in sums], jnp.add)

    over(near.shape[0], CHUNK, finish)


def last_kernel(
    sizes,
    depth,
    near1,
    given1,
    parts,
    x1,
    away_own1,
    away_all1,
    counts,
    scales1,
    mask,
    weight1,
    grad_own2,
    grad_near2,
    from_own,
    from_near,
    norm1,
    whole1,
    whole2,
    slots,
    flat1,
    flat2,
    pushed,
    arrived,
    halved1,
    halved2,
    landed1,
    landed2,
    reduced1,
    reduced2,
    all1,
    all2,
    small_sems,
    pair_sems,
    ring_sems,
):
    cores, chips = sizes
    total = cores * chips
    points = given1.shape[0]
    cin = x1.shape[1]
    width1 = weight1.shape[0]
    core = lax.axis_index("points")
    chip = lax.axis_index("clouds")
    half = pl.multiple_of(core * points, points)
    barrier = pltpu.get_barrier_semaphore()
    signal_all(barrier, cores, total)

    def chip_copy(d, source, target, use):
        return pltpu.make_async_remote_copy(
            src_ref=source,
            dst_ref=target,
            send_sem=ring_sems.at[0, use],
            recv_sem=ring_sems.at[1, use],
            device_id=(lax.rem(chip + d, chips), core),
            device_id_type=MESH,
        )

    class Summed:
        def __init__(self, flat, halved, landed, reduced, whole, first):
            self.flat, self.halved, self.landed, self.reduced, self.whole = (
                flat,
                halved,
                landed,
                reduced,
                whole,
            )
            self.first = first
            self.piece = landed.shape[1]
            self.side = chips * self.piece
            self.mine = pl.multiple_of(core * self.side, SUBLANES)
            other = pl.multiple_of((1 - core) * self.side, SUBLANES)
            self.swap = to_partner(flat.at[pl.ds(other, self.side)], halved, pair_sems, first)
            here = whole.at[core]
            self.back = to_partner(here, here, pair_sems, first + 1)

        def scatter(self):
            self.swap.wait()
            self.flat[pl.ds(self.mine, self.side), :] += self.halved[...]
            start = pl.multiple_of(self.mine + chip * self.piece, SUBLANES)
            self.landed[chip] = self.flat[pl.ds(start, self.piece), :]

            def send(d, carry):
                to = lax.rem(chip + d, chips)
                place = pl.multiple_of(self.mine + to * self.piece, SUBLANES)
                source = self.flat.at[pl.ds(place, self.piece)]
                chip_copy(d, source, self.landed.at[chip], self.first).start()
                return carry

            lax.fori_loop(1, chips, send, 0)

        def wait(self, use):
            others = self.landed.at[pl.ds(0, chips - 1)]
            arrival = chip_copy(1, others, others, use)
            arrival.wait_recv()
            arrival.wait_send()

        def spread(self):
            self.wait(self.first)
            self.reduced[...] = slot_sum(self.landed, chips)
            self.whole[core, chip] = self.reduced[...]

            def send(d, carry):
                chip_copy(d, self.reduced, self.whole.at[core, chip], self.first + 1).start()
                return carry

            lax.fori_loop(1, chips, send, 0)

        def finish(self):
            self.wait(self.first + 1)
            self.back.start()

    sum1 = Summed(flat1, halved1, landed1, reduced1, all1, 0)
    sum2 = Summed(flat2, halved2, landed2, reduced2, all2, 2)
    for flat, rows in ((flat1, LANES), (flat2, 4 * LANES)):
        if flat.shape[0] > rows:
            flat[rows:, :] = jnp.zeros((flat.shape[0] - rows, LANES), F32)
    for h in range(2):
        columns = slice(h * LANES, (h + 1) * LANES)
        flat2[h * LANES : (h + 1) * LANES, :] = grad_own2[:, columns]
        flat2[(2 + h) * LANES : (3 + h) * LANES, :] = grad_near2[:, columns] - grad_own2[:, columns]
    direct1 = weight1[:, :cin] - weight1[:, cin:]
    relative1 = weight1[:, cin:]
    slope = scales1[0:1, :]
    r1 = scales1[1:2, :]
    outer_scale = slope / scales1[2:3, :]

    pl.semaphore_wait(barrier, total - 1)
    sum2.swap.start()
    gather_start(parts, slots, small_sems.at[0], small_sems.at[1], cores, total)
    sum2.scatter()
    gather_wait(slots, small_sems.at[0], small_sems.at[1], total)
    sums = slot_sum(slots, total)
    norm1[...] = sums
    beta_scale = outer_scale * sums[0:1]
    gamma_scale = outer_scale * sums[1:2] * r1

    grad_near1 = jnp.zeros((cin, width1), F32)
    for c in range(cores):

        def push(i, total_near):
            start = pl.multiple_of(i * CHUNK, CHUNK)
            rows = pl.ds(c * points + start, CHUNK)
            value = near1[rows, :] * slope
            value = value - (counts[rows, :] * beta_scale + away_all1[rows, :] * gamma_scale)
            pushed[c, :, pl.ds(start, CHUNK)] = jnp.transpose(by(value, relative1))
            return total_near + t_by(x1[rows, :], value)

        grad_near1 = lax.fori_loop(0, points // CHUNK, push, grad_near1)
    swap = to_partner(pushed.at[1 - core], arrived, pair_sems, 4)
    swap.start()

    def own(i, total_own):
        start = pl.multiple_of(i * CHUNK, CHUNK)
        rows = pl.ds(start, CHUNK)
        weights = jnp.broadcast_to(mask[:, rows].astype(F32), (SUBLANES, CHUNK))
        weights = jnp.transpose(weights)[:, :1]
        value = given1[rows, :] * slope
        value = value - (depth * weights * beta_scale + away_own1[rows, :] * gamma_scale)
        from_own[:, rows] = jnp.transpose(by(value, direct1)) + pushed[core, :, rows]
        return total_own + t_by(x1[pl.ds(half + start, CHUNK), :], value)

    grad_own1 = lax.fori_loop(0, points // CHUNK, own, jnp.zeros((cin, width1), F32))
    flat1[0:cin, :] = grad_own1
    flat1[cin : 2 * cin, :] = grad_near1 - grad_own1
    sum1.swap.start()
    sum2.spread()
    sum1.scatter()
    swap.wait()
    from_near[...] = arrived[...]
    sum2.finish()
    sum1.spread()
    sum2.back.wait()
    whole2[...] = all2[...]
    sum1.finish()
    sum1.back.wait()
    whole1[...] = all1[...]


def finish_kernel(
    from_own,
    from_near,
    norm1,
    whole1,
    whole2,
    scales2,
    pooled_in,
    pooled,
    grad_features,
    grad_weight1,
    grad_gain1,
    grad_bias1,
    grad_weight2,
    grad_gain2,
    grad_bias2,
):
    pooled[...] = pooled_in[...]
    grad_features[...] = from_own[...] + from_near[...]
    grad_weight1[...] = jnp.transpose(whole1[0:LANES, :])
    grad_bias1[...] = norm1[0:1, :]
    grad_gain1[...] = norm1[1:2, :]
    for h in range(2):
        rows = slice(h * LANES, (h + 1) * LANES)
        for part in range(2):
            block = (2 * part + h) * LANES
            grad_weight2[rows, part * LANES : (part + 1) * LANES] = jnp.transpose(
                whole2[block : block + LANES, :]
            )
    grad_bias2[...] = scales2[1:2, :]
    grad_gain2[...] = scales2[2:3, :]


def shaped(*shape):
    return jax.ShapeDtypeStruct(shape, F32)


def scratch(*shape, dtype=F32):
    return pltpu.VMEM(shape, dtype)


def program(mesh):
    cores, chips = mesh.shape["points"], mesh.shape["clouds"]
    total = cores * chips

    def on_device(
        features,
        lengths,
        mask,
        neighbours,
        first_layer_weight,
        first_norm_gain,
        first_norm_bias,
        second_layer_weight,
        second_norm_gain,
        second_norm_bias,
        pooled_grad,
    ):
        cin, points = features.shape
        depth = neighbours.shape[0]
        width1, width2 = first_layer_weight.shape[0], second_layer_weight.shape[0]
        both = cores * points
        clouds = lengths.shape[0]
        mask_row = mask[None, :]
        groups1, groups2 = points // SUBLANES, points // 4

        def layout(subs, groups):
            place = jnp.arange(points, dtype=jnp.int32) // groups
            return (neighbours * subs + (SUBLANES - subs * place)).reshape(-1)

        index1, index2 = layout(1, groups1), layout(2, groups2)
        block = 32
        outs = pl.pallas_call(
            functools.partial(forward_kernel, (cores, total)),
            out_shape=[
                shaped(clouds, 2 * width2),
                shaped(groups1, depth, SUBLANES, LANES),
                shaped(groups2, depth, SUBLANES, LANES),
                shaped(points, width1),
                shaped(points, width1),
                shaped(points, width1),
                shaped(both, cin),
                shaped(points, width1),
                shaped(both, width1),
                shaped(both, LANES),
                shaped(both, width1),
                shaped(SUBLANES, width1),
                shaped(2 * points, LANES),
                shaped(both, width2),
                shaped(points, width1),
                shaped(width1, width2),
                shaped(SUBLANES, width2),
            ],
            in_specs=[VMEM] * 3 + [ANY] * 2 + [SMEM] + [VMEM] * 3 + [ANY] + [VMEM] * 3,
            out_specs=[VMEM] + [ANY] * 10 + [VMEM] * 6,
            scratch_shapes=[
                pltpu.SMEM((depth * points,), jnp.int32),
                pltpu.SMEM((depth * points,), jnp.int32),
                scratch(width2, 2 * width1),
                scratch(points, width1),
                scratch(points, width1),
                scratch(points, width1),
                scratch(both, cin),
                scratch(points, width1),
                scratch(both, width1),
                scratch(both, LANES),
                scratch(cores, cin, points),
                scratch(both, LANES, dtype=BF16),
                scratch(both, points, dtype=BF16),
                scratch(SUBLANES, points),
                scratch(points, LANES),
                scratch(cores, 3 * cin, points, dtype=BF16),
                scratch(2 * width1, both, dtype=BF16),
                scratch(points, width1),
                scratch(both, width1),
                scratch(points, cin),
                scratch(points, width1),
                scratch(both + 2 * SUBLANES, LANES),
                scratch(points, LANES),
                scratch(points, LANES),
                scratch(points, LANES),
                scratch(points, LANES),
                scratch(2 * both + 2 * SUBLANES, LANES),
                scratch(2 * points, LANES),
                scratch(2 * points, LANES),
                scratch(2 * points, LANES),
                scratch(2 * points, LANES),
                scratch(2 * points, LANES),
                scratch(both, width1),
                scratch(points, width2),
                scratch(both, width2),
                scratch(points, width2),
                scratch(points, 2 * width2, dtype=BF16),
                scratch(cores, 3 * clouds, SUBLANES, LANES),
                scratch(3, 4, LANES),
                scratch(3, total, 4, LANES),
                scratch(depth, SUBLANES, LANES),
                scratch(depth, SUBLANES, LANES),
                scratch(2, block, depth, SUBLANES, LANES),
                pltpu.SemaphoreType.DMA((2, 3)),
                pltpu.SemaphoreType.DMA((2, 3)),
                pltpu.SemaphoreType.DMA((2,)),
                pltpu.SemaphoreType.DMA((3,)),
                pltpu.SemaphoreType.DMA((8,)),
            ],
            compiler_params=pltpu.CompilerParams(
                collective_id=1, has_side_effects=True, vmem_limit_bytes=MEMORY
            ),
            name="forward",
        )(
            features,
            neighbours,
            mask_row,
            index1,
            index2,
            lengths,
            first_layer_weight,
            first_norm_gain[None, :],
            first_norm_bias[None, :],
            second_layer_weight,
            second_norm_gain[None, :],
            second_norm_bias[None, :],
            pooled_grad,
        )
        (
            pooled,
            q1,
            q2,
            inverse1,
            share1,
            moment1,
            x1,
            away_own1,
            away_all1,
            counts,
            x2,
            scales1,
            push2,
            extra2,
            own2,
            grad_own2,
            scales2,
        ) = outs

        ring = scratch(3, block, depth, SUBLANES, LANES)
        kept, sent, grad_near2 = pl.pallas_call(
            functools.partial(scatter2_kernel, depth),
            out_shape=[shaped(points, width1), shaped(points, width1), shaped(width1, width2)],
            in_specs=[ANY] * 5 + [VMEM, ANY],
            out_specs=[VMEM] * 3,
            scratch_shapes=[
                pltpu.SMEM((depth * points,), jnp.int32),
                scratch(2 * points, LANES),
                scratch(both, width1),
                scratch(width2, 2 * width1),
                scratch(both, width2),
                ring,
                pltpu.SemaphoreType.DMA((5,)),
                pltpu.SemaphoreType.DMA((3,)),
            ]
            + [scratch(2 * both + 2 * SUBLANES, LANES)] * 8,
            compiler_params=pltpu.CompilerParams(vmem_limit_bytes=MEMORY),
            name="scatter2",
        )(index2, q2, push2, x2, second_layer_weight, scales2, extra2)
        other = lax.ppermute(sent, "points", [(0, 1), (1, 0)])

        near1, given1, parts = pl.pallas_call(
            functools.partial(scatter1_kernel, depth),
            out_shape=[shaped(both, width1), shaped(points, width1), shaped(SUBLANES, width1)],
            in_specs=[ANY] * 2 + [VMEM] * 6,
            out_specs=[VMEM] * 3,
            scratch_shapes=[
                pltpu.SMEM((depth * points,), jnp.int32),
                scratch(points, width1),
                ring,
                pltpu.SemaphoreType.DMA((1,)),
                pltpu.SemaphoreType.DMA((3,)),
            ]
            + [scratch(both + 2 * SUBLANES, LANES)] * SUBLANES,
            compiler_params=pltpu.CompilerParams(vmem_limit_bytes=MEMORY),
            name="scatter1",
        )(index1, q1, own2, kept, other, inverse1, share1, moment1)

        def piece_of(rows):
            return -(-rows // (total * SUBLANES)) * SUBLANES

        piece1, piece2 = piece_of(LANES), piece_of(4 * LANES)
        side1, side2 = chips * piece1, chips * piece2
        from_own, from_near, norm1, whole1, whole2 = pl.pallas_call(
            functools.partial(last_kernel, (cores, chips), depth),
            out_shape=[
                shaped(cin, points),
                shaped(cin, points),
                shaped(SUBLANES, width1),
                shaped(cores, chips, piece1, LANES),
                shaped(cores, chips, piece2, LANES),
            ],
            in_specs=[VMEM] * 12,
            out_specs=[VMEM] * 5,
            scratch_shapes=[
                scratch(total, SUBLANES, LANES),
                scratch(cores * side1, LANES),
                scratch(cores * side2, LANES),
                scratch(cores, cin, points),
                scratch(cin, points),
                scratch(side1, LANES),
                scratch(side2, LANES),
                scratch(chips, piece1, LANES),
                scratch(chips, piece2, LANES),
                scratch(piece1, LANES),
                scratch(piece2, LANES),
                scratch(cores, chips, piece1, LANES),
                scratch(cores, chips, piece2, LANES),
                pltpu.SemaphoreType.DMA((2,)),
                pltpu.SemaphoreType.DMA((2, 5)),
                pltpu.SemaphoreType.DMA((2, 4)),
            ],
            compiler_params=pltpu.CompilerParams(
                collective_id=2, has_side_effects=True, vmem_limit_bytes=MEMORY
            ),
            name="last",
        )(
            near1,
            given1,
            parts,
            x1,
            away_own1,
            away_all1,
            counts,
            scales1,
            mask_row,
            first_layer_weight,
            grad_own2,
            grad_near2,
        )
        outs = pl.pallas_call(
            finish_kernel,
            out_shape=[
                shaped(clouds, 2 * width2),
                shaped(cin, points),
                shaped(width1, 2 * cin),
                shaped(1, width1),
                shaped(1, width1),
                shaped(width2, 2 * width1),
                shaped(1, width2),
                shaped(1, width2),
            ],
            in_specs=[VMEM] * 7,
            out_specs=[VMEM] * 8,
            compiler_params=pltpu.CompilerParams(vmem_limit_bytes=MEMORY),
            name="finish",
        )(
            from_own,
            from_near,
            norm1,
            whole1.reshape(cores * side1, LANES),
            whole2.reshape(cores * side2, LANES),
            scales2,
            pooled,
        )
        return tuple(
            value.reshape(-1) if value.shape[0] == 1 else value for value in outs
        )

    return on_device


def solution(mesh):
    in_specs = (
        P(None, ("clouds", "points")),
        P("clouds"),
        P(("clouds", "points")),
        P(None, ("clouds", "points")),
        P(),
        P(),
        P(),
        P(),
        P(),
        P(),
        P("clouds", None),
    )
    out_specs = (P("clouds", None), P(None, ("clouds", "points")), P(), P(), P(), P(), P(), P())
    return jax.shard_map(
        program(mesh), mesh=mesh, in_specs=in_specs, out_specs=out_specs, check_vma=False
    )
```

```python
import functools
import math

import jax
import jax.numpy as jnp
from jax import lax
from jax.experimental import pallas as pl
from jax.experimental.pallas import tpu as pltpu
from jax.sharding import PartitionSpec as P

EPSILON = 1e-05
LOG2E = math.log2(math.e)
LN2 = math.log(2.0)
MESH = pl.DeviceIdType.MESH
F32 = jnp.float32
BF16 = jnp.bfloat16
LANES = 128
SUBLANES = 8
CHUNK = 256
MEMORY = 60 * 2**20
VMEM = pl.BlockSpec(memory_space=pltpu.VMEM)
SMEM = pl.BlockSpec(memory_space=pltpu.SMEM)
ANY = pl.BlockSpec(memory_space=pl.ANY)


def dot(left, right, dims):
    return lax.dot_general(
        left,
        right,
        (dims, ((), ())),
        precision=lax.Precision.HIGHEST,
        preferred_element_type=F32,
    )


def mm(left, right):
    return dot(left, right, ((1,), (0,)))


def mm_nt(left, right):
    return dot(left, right, ((1,), (1,)))


def mm_tn(left, right):
    return dot(left, right, ((0,), (0,)))


def mm_low(left, right):
    return lax.dot_general(
        left, right, (((1,), (0,)), ((), ())), preferred_element_type=F32
    )


def split(value):
    high = value.astype(BF16)
    low = (value - high.astype(F32)).astype(BF16)
    return high, low


def product(left, right, dims):
    def part(a, b):
        return lax.dot_general(a, b, (dims, ((), ())), preferred_element_type=F32)

    left_high, left_low = split(left)
    right_high, right_low = split(right)
    return part(left_high, right_high) + (part(left_high, right_low) + part(left_low, right_high))


def by(left, right):
    return product(left, right, ((1,), (0,)))


def by_t(left, right):
    return product(left, right, ((1,), (1,)))


def t_by(left, right):
    return product(left, right, ((0,), (0,)))


def over(count, step, body):
    def run(i, carry):
        body(pl.multiple_of(i * step, step))
        return carry

    lax.fori_loop(0, count // step, run, 0)


def tree(values, join):
    values = list(values)
    while len(values) > 1:
        values = [
            join(values[i], values[i + 1]) if i + 1 < len(values) else values[i]
            for i in range(0, len(values), 2)
        ]
    return values[0]


def iota(shape, dim):
    return lax.broadcasted_iota(jnp.int32, shape, dim)


def signal_all(barrier, cores, total):
    me = lax.axis_index("clouds") * cores + lax.axis_index("points")

    def send(d, carry):
        t = lax.rem(me + d, total)
        pl.semaphore_signal(
            barrier,
            inc=1,
            device_id=(lax.div(t, cores), lax.rem(t, cores)),
            device_id_type=MESH,
        )
        return carry

    lax.fori_loop(1, total, send, 0)


def gather_start(own, slots, send_sem, recv_sem, cores, total):
    me = lax.axis_index("clouds") * cores + lax.axis_index("points")
    slots[me] = own[...]

    def send(d, carry):
        t = lax.rem(me + d, total)
        pltpu.make_async_remote_copy(
            src_ref=own,
            dst_ref=slots.at[me],
            send_sem=send_sem,
            recv_sem=recv_sem,
            device_id=(lax.div(t, cores), lax.rem(t, cores)),
            device_id_type=MESH,
        ).start()
        return carry

    lax.fori_loop(1, total, send, 0)


def gather_wait(slots, send_sem, recv_sem, total):
    others = slots.at[pl.ds(0, total - 1)]
    arrived = pltpu.make_async_remote_copy(
        src_ref=others,
        dst_ref=others,
        send_sem=send_sem,
        recv_sem=recv_sem,
        device_id=(lax.axis_index("clouds"), 1 - lax.axis_index("points")),
        device_id_type=MESH,
    )
    arrived.wait_recv()
    arrived.wait_send()


def slot_sum(slots, total):
    def add(i, carry):
        return carry + slots[i]

    return lax.fori_loop(1, total, add, slots[0])


def to_partner(source, target, sems, index):
    return pltpu.make_async_remote_copy(
        src_ref=source,
        dst_ref=target,
        send_sem=sems.at[0, index],
        recv_sem=sems.at[1, index],
        device_id=(lax.axis_index("clouds"), 1 - lax.axis_index("points")),
        device_id_type=MESH,
    )


def edge_pass(
    subs, block, depth, part, index, table, own_rows, out_hbm, held, ring, sems, outs, pending, after_block
):
    level_ref, share_ref, moment_ref, inverse_ref = outs
    per = SUBLANES // subs
    groups = own_rows.shape[0] // SUBLANES
    stages = depth // part
    row = iota((SUBLANES, LANES), 0)
    mine = [(row >= subs * i) & (row < subs * (i + 1)) for i in range(per)]
    zero = jnp.zeros((SUBLANES, LANES), F32)

    def fetch(group, stage, slot):
        for k in range(part):
            target = held[slot].at[stage * part + k]
            for i in range(per):
                first = (k * per + i) * groups
                if stages > 1:
                    span = groups * (1 + (stages - 1) * part * per)
                    j = index.at[pl.ds(first, span)][stage * (part * per * groups) + group]
                else:
                    j = index.at[pl.ds(first, groups)][group]
                value = table[pl.ds(j, SUBLANES), :]
                if i == 0:
                    target[...] = value
                else:
                    pltpu.store(target, value, mask=mine[i])

    def work(group, stage, slot, ring_slot, place, carry):
        total0, share0, moment0 = carry
        rows = pl.ds(pl.multiple_of(group * SUBLANES, SUBLANES), SUBLANES)
        peak = tree([held[slot][k] for k in range(depth)], jnp.maximum)
        top = own_rows[rows, :] + peak
        shift = jnp.maximum(top, 0.0)
        rest = jnp.maximum(jnp.exp2(-shift), 2.0**-100)
        under = jnp.maximum(jnp.minimum(top, 0.0), -100.0)
        offset = under - peak
        fifth = 0.2 * rest
        total, share, moment = [], [], []
        for k in range(part):
            value = held[slot][stage * part + k]
            power = value + offset
            grown = jnp.exp2(power)
            root = jnp.exp2((power - lax.log2(rest + grown)) * 0.2)
            weight = root * (fifth + grown)
            ring[ring_slot, place, stage * part + k] = weight
            total.append(root)
            share.append(weight)
            moment.append(weight * value)
        total, share, moment = [
            functools.reduce(jnp.add, parts) for parts in (total, share, moment)
        ]
        if stages > 1:
            start = stage == 0
            total = total + jnp.where(start, 0.0, total0)
            share = share + jnp.where(start, 0.0, share0)
            moment = moment + jnp.where(start, 0.0, moment0)
        mass = share + (0.8 * rest) * total
        inverse = 1.0 / mass
        level = 0.2 * (top - under) + 0.8 * shift + lax.log2(mass)
        level_ref[rows, :] = LN2 * level - math.log(depth)
        inverse_ref[rows, :] = inverse
        share_ref[rows, :] = share * inverse
        moment_ref[rows, :] = moment * inverse
        return total, share, moment

    blocks = groups // block

    def push(b, slot):
        return pltpu.make_async_copy(
            ring.at[slot, pl.ds(0, block)], out_hbm.at[pl.ds(b * block, block)], sems.at[slot]
        )

    for stage in range(stages):
        fetch(0, stage, 0)

    def one_block(b, carry):
        ring_slot = lax.rem(b, 2)

        if pending is None:

            @pl.when(b >= 2)
            def _():
                push(b - 2, ring_slot).wait()

        else:

            @pl.when(b < 2)
            def _():
                pending(ring_slot).wait()

            @pl.when(b >= 2)
            def _():
                push(b - 2, ring_slot).wait()

        def pair(t, inner):
            for slot in range(2):
                place = t * 2 + slot
                group = b * block + place
                after = jnp.minimum(group + 1, groups - 1)
                if stages == 1:
                    work(group, 0, slot, ring_slot, place, (zero,) * 3)
                    fetch(after, 0, 1 - slot)
                else:

                    def one_stage(stage, sums):
                        sums = work(group, stage, slot, ring_slot, place, sums)
                        fetch(after, stage, 1 - slot)
                        return sums

                    lax.fori_loop(0, stages, one_stage, (zero,) * 3)
            return inner

        lax.fori_loop(0, block // 2, pair, 0)
        push(b, ring_slot).start()
        if after_block is not None:
            after_block(b)
        return carry

    lax.fori_loop(0, blocks, one_block, 0)
    return lambda slot: push(blocks - 2 + slot, slot)


def lanes_to_rows(value, width):
    return [value[:, i * LANES : (i + 1) * LANES] for i in range(width // LANES)]


def rows_to_lanes(rows):
    return rows[0] if len(rows) == 1 else jnp.concatenate(rows, axis=1)


def forward_kernel(
    sizes,
    feat,
    near,
    mask,
    index1_in,
    index2_in,
    lengths,
    weight1,
    gain1,
    bias1,
    weight2_in,
    gain2,
    bias2,
    pooled_grad,
    pooled,
    q1,
    q2,
    inverse1_out,
    share1_out,
    moment1_out,
    x1_out,
    away_own1_out,
    away_all1_out,
    counts_out,
    x2_out,
    push2_out,
    extra2_out,
    scales1,
    own2,
    grad_own2,
    scales2,
    known1,
    push2,
    extra2,
    index1,
    index2,
    weight2,
    inverse1,
    share1,
    moment1,
    x1,
    away_own1,
    away_all1,
    counts,
    x1_cm,
    tallies,
    lows,
    links,
    live,
    live_col,
    parts1,
    parts2,
    u1,
    v1,
    n1,
    g1,
    table1,
    own_rows1,
    level1,
    other1,
    share_rows1,
    moment_rows1,
    table2,
    own_rows2,
    level2,
    share2,
    moment2,
    inverse2,
    x2,
    u2,
    v2,
    g2,
    u_parts,
    pool_parts,
    message,
    slots,
    held0,
    held1,
    ring,
    pair_sems,
    all_sems,
    ring_sems,
    load_sems,
    store_sems,
):
    cores, total = sizes
    points = feat.shape[1]
    cin = feat.shape[0]
    both = cores * points
    depth = near.shape[0]
    width1 = weight1.shape[0]
    width2 = gain2.shape[1]
    groups1, groups2 = points // SUBLANES, 2 * points // SUBLANES
    core = lax.axis_index("points")
    half = pl.multiple_of(core * points, points)
    barrier = pltpu.get_barrier_semaphore()
    signal_all(barrier, cores, total)
    loads = [
        pltpu.make_async_copy(source, target, load_sems.at[i])
        for i, (source, target) in enumerate(
            ((index1_in, index1), (index2_in, index2), (weight2_in, weight2))
        )
    ]
    for copy in loads:
        copy.start()
    late = [
        pltpu.make_async_copy(source, target, store_sems.at[8 + i])
        for i, (source, target) in enumerate(((push2, push2_out), (extra2, extra2_out)))
    ]
    stores = [
        pltpu.make_async_copy(source, target, store_sems.at[i])
        for i, (source, target) in enumerate(
            (
                (x1, x1_out),
                (counts, counts_out),
                (away_own1, away_own1_out),
                (away_all1, away_all1_out),
                (inverse1, inverse1_out),
                (share1, share1_out),
                (moment1, moment1_out),
                (x2, x2_out),
            )
        )
    ]

    live[...] = jnp.broadcast_to(mask[...].astype(F32), live.shape)
    row16 = iota((16, LANES), 0)
    one, none = jnp.ones((16, LANES), BF16), jnp.zeros((16, LANES), BF16)

    def build(columns, first):
        high_names, low_names = [], []
        for k in range(depth):
            name = near[k : k + 1, columns]
            high = jnp.where(mask[:, columns] > 0, lax.shift_right_logical(name, 7), -1)
            for names, value in ((high_names, high), (low_names, name & (LANES - 1))):
                names.append(jnp.broadcast_to(value, (16, LANES)).astype(jnp.int16))
        for s in range(0, LANES, 16):
            target = (row16 + s).astype(jnp.int16)
            for k in range(depth):
                lows[k, s : s + 16, :] = jnp.where(low_names[k] == target, one, none)

        def one_high(start):
            target = jnp.full((16, LANES), lax.shift_right_logical(start, 7), jnp.int32)
            target = target.astype(jnp.int16)
            meant = [jnp.where(name == target, one, none) for name in high_names]
            for s in range(0, LANES, 16):
                found = tree([meant[k] * lows[k, s : s + 16, :] for k in range(depth)], jnp.add)
                here = pl.ds(start + s, 16)
                links[here, columns] = found
                tallies[here, :] = found if first else tallies[here, :] + found

        over(both, LANES, one_high)

    tiles = points // LANES
    early = tiles - tiles // 4
    for tile in range(early):
        build(pl.ds(tile * LANES, LANES), tile == 0)
    x1_cm[core] = feat[...]
    pl.semaphore_wait(barrier, total - 1)
    swap = to_partner(feat, x1_cm.at[core], pair_sems, 0)
    swap.start()
    for tile in range(early, tiles):
        build(pl.ds(tile * LANES, LANES), tile == 0)
    live_col[...] = jnp.broadcast_to(jnp.transpose(live[...])[:, :1], live_col.shape)
    swap.wait()

    direct1 = weight1[:, :cin] - weight1[:, cin:]
    relative1 = weight1[:, cin:]
    for c in range(cores):

        def turn(start):
            x1[pl.ds(c * points + start, CHUNK), :] = jnp.transpose(
                x1_cm[c, :, pl.ds(start, CHUNK)]
            )

        over(points, CHUNK, turn)
        value = x1_cm[c]
        high, low = split(value)
        lower = (value - high.astype(F32) - low.astype(F32)).astype(BF16)
        parts1[c, 0:cin, :] = high
        parts1[c, cin : 2 * cin, :] = low
        parts1[c, 2 * cin : 3 * cin, :] = lower

    def sums_near1(start):
        columns = pl.ds(start, CHUNK)
        value = mm_low(parts1[0], links[0:points, columns])
        for c in range(1, cores):
            value = value + mm_low(parts1[c], links[c * points : (c + 1) * points, columns])
        value = value[0:cin] + value[cin : 2 * cin] + value[2 * cin : 3 * cin]
        n1[columns, :] = jnp.transpose(value)

    over(points, CHUNK, sums_near1)

    stores[0].start()
    ones = jnp.ones((LANES, LANES), BF16)

    def count_links(start):
        rows = pl.ds(start, CHUNK)
        counts[rows, :] = mm_low(tallies[rows, :], ones)

    over(both, CHUNK, count_links)
    stores[1].start()

    live_sum = jnp.sum(live[0:1, :], axis=1, keepdims=True)
    mine = live_sum * depth

    def live_total(start, size, value):
        high, low = split(value)
        weights = live[:, start : start + size].astype(BF16)
        return (mm_low(weights, high) + mm_low(weights, low))[0:1]

    def statistics(x_all, n_ref, direct, relative, u, v, g, width):
        def outer(start):
            rows = pl.ds(start, CHUNK)
            v[rows, :] = mm_nt(x_all[rows, :], relative)

        over(both, CHUNK, outer)

        def inner(start):
            rows = pl.ds(start, CHUNK)
            u[rows, :] = mm_nt(x_all[pl.ds(half + start, CHUNK), :], direct)
            g[rows, :] = mm_nt(n_ref[rows, :], relative)

        over(points, CHUNK, inner)
        u_sum = live_total(0, points, u[...])
        g_sum = jnp.sum(g[...], axis=0, keepdims=True)
        u_mean = u_sum / live_sum
        v_mean = g_sum / mine
        centred = u[...] - u_mean
        spread = depth * centred * centred + 2.0 * centred * (g[...] - depth * v_mean)
        square = live_total(0, points, spread)
        weights = rows_to_lanes([counts[...]] * (width // LANES))
        away = v[...] - v_mean
        square = square + jnp.sum(weights * away * away, axis=0, keepdims=True)
        return depth * u_sum + g_sum, square, u_mean, v_mean

    def send_sums(use, rows):
        for i, value in enumerate(rows):
            message[use, i : i + 1, :] = value
        gather_start(
            message.at[use], slots.at[use], all_sems.at[0, use], all_sems.at[1, use], cores, total
        )

    def receive(use):
        gather_wait(slots.at[use], all_sems.at[0, use], all_sems.at[1, use], total)

    def combine(use, numbers, width):
        per = width // LANES
        count = numbers[0]
        for value in numbers[1:]:
            count = count + value

        def value_of(i, first):
            return rows_to_lanes([slots[use, i, first + h : first + h + 1, :] for h in range(per)])

        mean = value_of(0, 0)
        for i in range(1, total):
            mean = mean + value_of(i, 0)
        mean = mean / count
        square = None
        for i in range(total):
            gap = value_of(i, 0) / numbers[i] - mean
            term = value_of(i, per) + numbers[i] * gap * gap
            square = term if square is None else square + term
        return count, mean, square / count

    sums, square, u_mean1, v_mean1 = statistics(x1, n1, direct1, relative1, u1, v1, g1, width1)
    send_sums(0, [sums, square, jnp.broadcast_to(mine, (1, LANES)), jnp.zeros((1, LANES), F32)])

    for part, value in enumerate(split(u1[...] - u_mean1)):
        u_parts[:, part * LANES : (part + 1) * LANES] = value

    def shared1(start):
        rows = pl.ds(start, CHUNK)
        value = mm_low(links[rows, :], u_parts[:, 0 : 2 * LANES])
        away_all1[rows, :] = value[:, :LANES] + value[:, LANES:]

    over(both, CHUNK, shared1)
    receive(0)
    numbers = [slots[0, i, 2:3, 0:1] for i in range(total)]
    count, mean1, variance1 = combine(0, numbers, width1)
    r1 = lax.rsqrt(variance1 + EPSILON)
    slope1 = gain1[...] * r1
    scales1[...] = jnp.concatenate(
        [slope1, r1, jnp.broadcast_to(count, (1, LANES)), jnp.zeros((5, LANES), F32)], axis=0
    )

    def fill1(start):
        rows = pl.ds(start, CHUNK)
        table1[pl.ds(SUBLANES + start, CHUNK), :] = (v1[rows, :] - v_mean1) * (slope1 * LOG2E)
        away_all1[rows, :] += counts[rows, :] * (v1[rows, :] - (mean1 - u_mean1))

    over(both, CHUNK, fill1)

    def fill_own1(start):
        rows = pl.ds(start, CHUNK)
        value = (u1[rows, :] - (mean1 - v_mean1)) * (slope1 * LOG2E) + bias1[...] * LOG2E
        for s in range(0, CHUNK, groups1):
            here = pl.ds(lax.div(start, groups1) + s // groups1, groups1, stride=SUBLANES)
            own_rows1[here, :] = value[s : s + groups1]
        away_own1[rows, :] = depth * live_col[rows, :] * (u1[rows, :] - mean1) + g1[rows, :]

    over(points, CHUNK, fill_own1)

    stores[2].start()
    stores[3].start()
    loads[0].wait()
    block1, block2 = groups1 // 4, ring.shape[1]
    block_rows = block1 * SUBLANES
    blocks1 = 4

    def hand_over(b):
        rows = pl.ds(pl.multiple_of(b * block_rows, block_rows), block_rows)
        return to_partner(level1.at[rows], other1.at[rows], pair_sems, 3 + b)

    pending = edge_pass(
        1,
        block1,
        depth,
        depth // 2,
        index1,
        table1,
        own_rows1,
        q1,
        (held0, held1),
        ring,
        ring_sems,
        (level1, share_rows1, moment_rows1, inverse1),
        None,
        lambda b: hand_over(b).start(),
    )

    inverse_gain1 = 1.0 / (gain1[...] * LOG2E)
    for i in range(SUBLANES):
        here = pl.ds(i, groups1, stride=SUBLANES)
        x2[pl.ds(half + i * groups1, groups1), :] = level1[here, :]
        offset = own_rows1[here, :] - bias1[...] * LOG2E
        rows = slice(i * groups1, (i + 1) * groups1)
        moment1[rows, :] = (share_rows1[here, :] * offset + moment_rows1[here, :]) * inverse_gain1
        share1[rows, :] = share_rows1[here, :]
    for copy in stores[4:7]:
        copy.start()
    loads[1].wait()
    loads[2].wait()
    for b in range(blocks1):
        hand_over(b).wait()
    other_half = pl.multiple_of((1 - core) * points, points)
    for i in range(SUBLANES):
        here = pl.ds(i, groups1, stride=SUBLANES)
        x2[pl.ds(other_half + i * groups1, groups1), :] = other1[here, :]
    stores[7].start()

    direct2 = weight2[:, :width1] - weight2[:, width1:]
    relative2 = weight2[:, width1:]

    def turn2(start):
        high, low = split(jnp.transpose(x2[pl.ds(start, CHUNK), :]))
        parts2[0:width1, pl.ds(start, CHUNK)] = high
        parts2[width1 : 2 * width1, pl.ds(start, CHUNK)] = low

    over(both, CHUNK, turn2)

    def sums_near2(start):
        columns = pl.ds(start, CHUNK)
        value = mm_low(parts2[...], links[:, columns])
        value = value[0:width1] + value[width1 : 2 * width1]
        g2[columns, :] = mm_nt(jnp.transpose(value), relative2)

    over(points, CHUNK, sums_near2)

    def statistics2():
        def outer(start):
            rows = pl.ds(start, CHUNK)
            v2[rows, :] = mm_nt(x2[rows, :], relative2)

        over(both, CHUNK, outer)

        def inner(start):
            u2[pl.ds(start, CHUNK), :] = mm_nt(x2[pl.ds(half + start, CHUNK), :], direct2)

        over(points, CHUNK, inner)
        u_sum = jnp.zeros((1, width2), F32)
        g_sum = jnp.zeros((1, width2), F32)
        for s in range(0, points, CHUNK):
            u_sum = u_sum + live_total(s, CHUNK, u2[s : s + CHUNK, :])
            g_sum = g_sum + jnp.sum(g2[s : s + CHUNK, :], axis=0, keepdims=True)
        u_mean = u_sum / live_sum
        v_mean = g_sum / mine
        square = jnp.zeros((1, width2), F32)
        for s in range(0, points, CHUNK):
            centred = u2[s : s + CHUNK, :] - u_mean
            spread = depth * centred * centred + 2.0 * centred * (
                g2[s : s + CHUNK, :] - depth * v_mean
            )
            square = square + live_total(s, CHUNK, spread)

        def squares(i, carry):
            rows = pl.ds(pl.multiple_of(i * CHUNK, CHUNK), CHUNK)
            away = v2[rows, :] - v_mean
            weights = rows_to_lanes([counts[rows, :]] * (width2 // LANES))
            return carry + jnp.sum(weights * away * away, axis=0, keepdims=True)

        square = lax.fori_loop(0, both // CHUNK, squares, square)
        return depth * u_sum + g_sum, square, u_mean, v_mean

    sums, square, u_mean2, v_mean2 = statistics2()
    send_sums(1, lanes_to_rows(sums, width2) + lanes_to_rows(square, width2))
    for part, value in enumerate(split(u2[...] - u_mean2)):
        u_parts[:, part * width2 : (part + 1) * width2] = value

    def shared2(start):
        rows = pl.ds(start, CHUNK)
        extra2[rows, :] = mm_low(links[rows, :], u_parts[:, 0:width2]) + mm_low(
            links[rows, :], u_parts[:, width2:]
        )

    over(both, CHUNK, shared2)
    receive(1)
    count, mean2, variance2 = combine(1, numbers, width2)
    r2 = lax.rsqrt(variance2 + EPSILON)
    slope2 = gain2[...] * r2
    scales2[...] = jnp.concatenate([slope2, jnp.zeros((7, width2), F32)], axis=0)

    def fill2(start):
        rows = pl.ds(start, CHUNK)
        value = (v2[rows, :] - v_mean2) * (slope2 * LOG2E)
        for h in range(2):
            table2[pl.ds(SUBLANES + 2 * start + h, CHUNK, stride=2), :] = value[
                :, h * LANES : (h + 1) * LANES
            ]

    over(both, CHUNK, fill2)

    for i in range(SUBLANES // 2):
        rows = slice(i * groups2, (i + 1) * groups2)
        value = (u2[rows, :] - (mean2 - v_mean2)) * (slope2 * LOG2E) + bias2[...] * LOG2E
        for h in range(2):
            own_rows2[pl.ds(2 * i + h, groups2, stride=SUBLANES), :] = value[
                :, h * LANES : (h + 1) * LANES
            ]

    pending = edge_pass(
        2,
        block2,
        depth,
        depth,
        index2,
        table2,
        own_rows2,
        q2,
        (held0, held1),
        ring,
        ring_sems,
        (level2, share2, moment2, inverse2),
        pending,
        None,
    )

    clouds = pooled_grad.shape[0]
    ends = [lengths[0]]
    for q in range(1, clouds):
        ends.append(ends[-1] + lengths[q])
    row = iota((SUBLANES, LANES), 0)
    odd = lax.rem(row, 2) == 1
    point_of_row = half + lax.div(row, 2) * groups2
    steps = level2.shape[0] // SUBLANES
    lowest = jnp.full((SUBLANES, LANES), -1e30, F32)
    zero = jnp.zeros((SUBLANES, LANES), F32)

    def past(t):
        position = point_of_row + t
        return [position >= ends[q] for q in range(clouds - 1)]

    def pick(after, values):
        value = values[0]
        for q in range(1, clouds):
            value = jnp.where(after[q - 1], values[q], value)
        return value

    def apart(after, value, none):
        out = []
        for q in range(clouds):
            kept = value if q == 0 else jnp.where(after[q - 1], value, none)
            out.append(kept if q == clouds - 1 else jnp.where(after[q], none, kept))
        return out

    def step_rows(t):
        return pl.ds(pl.multiple_of(t * SUBLANES, SUBLANES), SUBLANES)

    def by_parity(value, join):
        value = join(value, pltpu.roll(value, 2, 0))
        return join(value, pltpu.roll(value, 4, 0))

    def unrolled(body, state, times):
        def several(i, carry):
            for u in range(times):
                carry = body(i * times + u, carry)
            return carry

        return lax.fori_loop(0, steps // times, several, state)

    def peaks(t, carry):
        value = level2[step_rows(t), :]
        after = past(t)
        tops = [jnp.maximum(a, b) for a, b in zip(carry, apart(after, value, lowest))]
        adds = [a + b for a, b in zip(carry[clouds:], apart(after, value, zero))]
        return tuple(tops + adds)

    state = unrolled(peaks, (lowest,) * clouds + (zero,) * clouds, 8)
    peak = [by_parity(value, jnp.maximum) for value in state[:clouds]]
    sums = [by_parity(value, jnp.add) for value in state[clouds:]]

    def masses(t, carry):
        after = past(t)
        value = jnp.exp(level2[step_rows(t), :] - pick(after, peak))
        return tuple(a + b for a, b in zip(carry, apart(after, value, zero)))

    state = unrolled(masses, (zero,) * clouds, 8)
    mass = [by_parity(value, jnp.add) for value in state]
    for q in range(clouds):
        pool_parts[core, 3 * q] = peak[q]
        pool_parts[core, 3 * q + 1] = mass[q]
        pool_parts[core, 3 * q + 2] = sums[q]
    here = pool_parts.at[core]
    swap = to_partner(here, here, pair_sems, 2)
    swap.start()
    swap.wait()

    level, grad_level, grad_mean = [], [], []
    for q in range(clouds):
        top = pool_parts[0, 3 * q]
        for c in range(1, cores):
            top = jnp.maximum(top, pool_parts[c, 3 * q])
        whole, sum_all = zero, zero
        for c in range(cores):
            whole = whole + pool_parts[c, 3 * q + 1] * jnp.exp(pool_parts[c, 3 * q] - top)
            sum_all = sum_all + pool_parts[c, 3 * q + 2]
        level.append(top + jnp.log(whole))
        size = jnp.full((SUBLANES, LANES), lengths[q].astype(F32), F32)
        first = level[q] - jnp.log(size)
        second = sum_all / size
        for h in range(2):
            pooled[q : q + 1, h * LANES : (h + 1) * LANES] = first[h : h + 1]
            pooled[q : q + 1, (2 + h) * LANES : (3 + h) * LANES] = second[h : h + 1]
        given = [pooled_grad[q : q + 1, h * LANES : (h + 1) * LANES] for h in range(4)]
        grad_level.append(jnp.where(odd, given[1], given[0]))
        grad_mean.append(jnp.where(odd, given[3], given[2]) / size)

    slope_rows, bias_rows = [], []
    for ref_value, target in ((gain2[...], slope_rows), (bias2[...], bias_rows)):
        low_half, high_half = lanes_to_rows(ref_value * LOG2E, width2)
        target.append(jnp.where(odd, high_half, low_half))
    inverse_gain = 1.0 / slope_rows[0]
    bias_row = bias_rows[0]

    def gradient(t, carry):
        rows = step_rows(t)
        after = past(t)
        value = pick(after, grad_level) * jnp.exp(level2[rows, :] - pick(after, level))
        value = value + pick(after, grad_mean)
        push2[rows, :] = value * inverse2[rows, :]
        share = share2[rows, :]
        moment = (share * (own_rows2[rows, :] - bias_row) + moment2[rows, :]) * inverse_gain
        given = value * share
        share2[rows, :] = given
        return carry[0] + given, carry[1] + value * moment

    state = unrolled(gradient, (zero, zero), 8)
    grad_beta, grad_gamma = [by_parity(value, jnp.add) for value in state]
    late[0].start()
    send_sums(2, [grad_beta[0:1], grad_beta[1:2], grad_gamma[0:1], grad_gamma[1:2]])

    known1[...] = jnp.zeros(known1.shape, F32)

    def known(start):
        near_rows = pl.ds(start, CHUNK)
        known1[0, cin:, :] += t_by(x1[near_rows, :], away_all1[near_rows, :])
        known1[1, cin:, :] += t_by(x1[near_rows, :], counts[near_rows, :])

    over(both, CHUNK, known)

    def known_own(start):
        rows = pl.ds(start, CHUNK)
        here = x1[pl.ds(half + start, CHUNK), :]
        known1[0, 0:cin, :] += t_by(here, away_own1[rows, :])
        known1[1, 0:cin, :] += t_by(here, depth * live_col[rows, :])

    over(points, CHUNK, known_own)
    for i in range(2):
        known1[i, cin:, :] -= known1[i, 0:cin, :]
    receive(2)
    sums = slot_sum(slots.at[2], total)
    grad_beta = rows_to_lanes([sums[0:1], sums[1:2]])
    grad_gamma = rows_to_lanes([sums[2:3], sums[3:4]])
    scales2[1:2, :] = grad_beta
    scales2[2:3, :] = grad_gamma
    outer_scale = slope2 / count
    gamma_scale = outer_scale * grad_gamma * r2
    beta_scale = outer_scale * grad_beta

    def extra(start):
        rows = pl.ds(start, CHUNK)
        weights = rows_to_lanes([counts[rows, :]] * 2)
        away = extra2[rows, :] + weights * (v2[rows, :] - (mean2 - u_mean2))
        extra2[rows, :] = weights * beta_scale + away * gamma_scale

    over(both, CHUNK, extra)
    late[1].start()
    grad_own2[...] = jnp.zeros(grad_own2.shape, F32)

    for i in range(SUBLANES // 2):
        rows = slice(i * groups2, (i + 1) * groups2)
        weights = rows_to_lanes([live_col[rows, :]] * 2)
        given = rows_to_lanes(
            [share2[pl.ds(2 * i + h, groups2, stride=SUBLANES), :] for h in range(2)]
        )
        away = depth * weights * (u2[rows, :] - mean2) + g2[rows, :]
        value = given * slope2 - (depth * weights * beta_scale + away * gamma_scale)
        own2[rows, :] = by(value, direct2)
        grad_own2[...] += t_by(x2[pl.ds(half + i * groups2, groups2), :], value)
    for copy in stores + late + [pending(0), pending(1)]:
        copy.wait()


def scatter_loop(subs, depth, part, index, q_hbm, ring, sems, push, sums, clear):
    per = SUBLANES // subs
    groups = q_hbm.shape[0]
    slots, block = ring.shape[0], ring.shape[1]
    blocks = groups // block
    row = iota((SUBLANES, LANES), 0)
    mine = [(row >= subs * i) & (row < subs * (i + 1)) for i in range(per)]
    ways = len(sums) // per
    stages = depth // part

    def pull(b):
        slot = lax.rem(b, slots)
        return pltpu.make_async_copy(
            q_hbm.at[pl.ds(b * block, block)], ring.at[slot], sems.at[slot]
        )

    for b in range(slots - 1):
        pull(b).start()
    clear()

    def one_block(b, carry):
        @pl.when(b + slots - 1 < blocks)
        def _():
            pull(b + slots - 1).start()

        pull(b).wait()
        slot = lax.rem(b, slots)

        def one_group(place, inner):
            group = b * block + place
            rows = pl.ds(pl.multiple_of(group * SUBLANES, SUBLANES), SUBLANES)
            given = push[rows, :]

            def one_part(stage):
                for k in range(part):
                    value = ring[slot, place, stage * part + k] * given
                    for i in range(per):
                        first = (k * per + i) * groups
                        if stages > 1:
                            span = groups * (1 + (stages - 1) * part * per)
                            j = index.at[pl.ds(first, span)][stage * (part * per * groups) + group]
                        else:
                            j = index.at[pl.ds(first, groups)][group]
                        target = sums[i * ways + k % ways].at[pl.ds(j, SUBLANES), :]
                        pltpu.store(target, target[...] + value, mask=mine[i])

            if stages == 1:
                one_part(0)
            else:
                lax.fori_loop(0, stages, lambda stage, c: (one_part(stage), c)[1], 0)
            return inner

        lax.fori_loop(0, block, one_group, 0)
        return carry

    lax.fori_loop(0, blocks, one_block, 0)


def clear(sums):
    rows = sums[0].shape[0]
    zero = jnp.zeros((SUBLANES, LANES), F32)

    def rows32(start):
        for ref in sums:
            for s in range(0, 4 * SUBLANES, SUBLANES):
                ref[pl.ds(start + s, SUBLANES), :] = zero

    over(rows, 4 * SUBLANES, rows32)
    for s in range(rows // 32 * 32, rows, SUBLANES):
        for ref in sums:
            ref[s : s + SUBLANES, :] = zero


def scatter2_kernel(
    depth,
    index_in,
    q_hbm,
    push_in,
    x2_in,
    weight_in,
    scales,
    extra_in,
    kept,
    sent,
    grad_near,
    index,
    push,
    x2,
    weight,
    extra,
    ring,
    load_sems,
    ring_sems,
    *sums,
):
    loads = [
        pltpu.make_async_copy(source, target, load_sems.at[i])
        for i, (source, target) in enumerate(
            ((index_in, index), (push_in, push), (x2_in, x2), (weight_in, weight), (extra_in, extra))
        )
    ]

    def prepare():
        for copy in loads[2:]:
            copy.start()
        clear(sums)
        loads[0].wait()
        loads[1].wait()

    for copy in loads[:2]:
        copy.start()
    scatter_loop(2, depth, depth, index, q_hbm, ring, ring_sems, push, sums, prepare)
    for copy in loads[2:]:
        copy.wait()
    points, width = kept.shape
    relative = weight[:, width:]
    core = lax.axis_index("points")
    grad_near[...] = jnp.zeros(grad_near.shape, F32)
    for part, out in ((1 - core, sent), (core, kept)):

        def finish(start):
            first = pl.multiple_of(part * points + start, CHUNK)
            rows = pl.ds(first, CHUNK)
            halves = []
            for h in range(2):
                here = pl.ds(SUBLANES + 2 * first + h, CHUNK, stride=2)
                halves.append(tree([ref[here, :] for ref in sums], jnp.add))
            value = rows_to_lanes(halves) * scales[0:1, :] - extra[rows, :]
            out[pl.ds(start, CHUNK), :] = by(value, relative)
            grad_near[...] += t_by(x2[rows, :], value)

        over(points, CHUNK, finish)


def scatter1_kernel(
    depth,
    index_in,
    q_hbm,
    own,
    kept,
    other,
    inverse,
    share,
    moment,
    near,
    given,
    parts,
    index,
    push,
    ring,
    load_sems,
    ring_sems,
    *sums,
):
    load = pltpu.make_async_copy(index_in, index, load_sems.at[0])
    load.start()

    def prepare():
        clear(sums)
        groups = own.shape[0] // SUBLANES
        grad_beta = jnp.zeros((1, LANES), F32)
        grad_gamma = jnp.zeros((1, LANES), F32)
        for i in range(SUBLANES):
            here = pl.ds(i, groups, stride=SUBLANES)
            rows = slice(i * groups, (i + 1) * groups)
            grad = own[rows, :] + kept[rows, :] + other[rows, :]
            push[here, :] = grad * inverse[here, :]
            weighted = grad * share[rows, :]
            given[rows, :] = weighted
            grad_beta = grad_beta + jnp.sum(weighted, axis=0, keepdims=True)
            grad_gamma = grad_gamma + jnp.sum(grad * moment[rows, :], axis=0, keepdims=True)
        parts[...] = jnp.concatenate([grad_beta, grad_gamma, jnp.zeros((6, LANES), F32)], axis=0)
        load.wait()

    scatter_loop(1, depth, depth // 1, index, q_hbm, ring, ring_sems, push, sums, prepare)

    def finish(start):
        here = pl.ds(SUBLANES + start, CHUNK)
        near[pl.ds(start, CHUNK), :] = tree([ref[here, :] for ref in sums], jnp.add)

    over(near.shape[0], CHUNK, finish)


def last_kernel(
    sizes,
    depth,
    near1_in,
    given1_in,
    parts,
    x1_in,
    away_own1_in,
    away_all1_in,
    counts_in,
    scales1,
    mask,
    weight1,
    grad_own2_in,
    grad_near2_in,
    known1_in,
    from_own,
    from_near,
    norm1,
    whole1,
    whole2,
    near1,
    given1,
    x1,
    away_own1,
    away_all1,
    counts,
    grad_own2,
    grad_near2,
    known1,
    slots,
    flat1,
    flat2,
    pushed,
    arrived,
    halved1,
    halved2,
    landed1,
    landed2,
    reduced1,
    reduced2,
    all1,
    all2,
    small_sems,
    pair_sems,
    ring_sems,
    load_sems,
):
    cores, chips = sizes
    total = cores * chips
    points = given1.shape[0]
    cin = x1.shape[1]
    width1 = weight1.shape[0]
    core = lax.axis_index("points")
    chip = lax.axis_index("clouds")
    half = pl.multiple_of(core * points, points)
    barrier = pltpu.get_barrier_semaphore()
    signal_all(barrier, cores, total)
    loads = [
        pltpu.make_async_copy(source, target, load_sems.at[i])
        for i, (source, target) in enumerate(
            (
                (x1_in, x1),
                (near1_in, near1),
                (given1_in, given1),
                (known1_in, known1),
                (grad_own2_in, grad_own2),
                (grad_near2_in, grad_near2),
                (counts_in, counts),
                (away_all1_in, away_all1),
                (away_own1_in, away_own1),
            )
        )
    ]
    for copy in loads:
        copy.start()

    def chip_copy(d, source, target, use):
        return pltpu.make_async_remote_copy(
            src_ref=source,
            dst_ref=target,
            send_sem=ring_sems.at[0, use],
            recv_sem=ring_sems.at[1, use],
            device_id=(lax.rem(chip + d, chips), core),
            device_id_type=MESH,
        )

    class Summed:
        def __init__(self, flat, halved, landed, reduced, whole, first):
            self.flat, self.halved, self.landed = flat, halved, landed
            self.reduced, self.whole, self.first = reduced, whole, first
            self.swap = to_partner(flat.at[1 - core], halved, pair_sems, first)
            here = whole.at[core]
            self.back = to_partner(here, here, pair_sems, first + 1)

        def scatter(self):
            self.swap.wait()
            self.flat[core] += self.halved[...]
            self.landed[chip] = self.flat[core, chip]

            def send(d, carry):
                source = self.flat.at[core, lax.rem(chip + d, chips)]
                chip_copy(d, source, self.landed.at[chip], self.first).start()
                return carry

            lax.fori_loop(1, chips, send, 0)

        def wait(self, ref, use):
            others = ref.at[pl.ds(0, chips - 1)]
            arrival = chip_copy(1, others, others, use)
            arrival.wait_recv()
            arrival.wait_send()

        def spread(self, change):
            self.wait(self.landed, self.first)
            self.reduced[...] = change(slot_sum(self.landed, chips))
            self.whole[core, chip] = self.reduced[...]

            def send(d, carry):
                chip_copy(d, self.reduced, self.whole.at[core, chip], self.first + 1).start()
                return carry

            lax.fori_loop(1, chips, send, 0)

        def finish(self):
            self.wait(self.whole.at[core], self.first + 1)
            self.back.start()

    sum1 = Summed(flat1, halved1, landed1, reduced1, all1, 0)
    sum2 = Summed(flat2, halved2, landed2, reduced2, all2, 2)
    direct1 = weight1[:, :cin] - weight1[:, cin:]
    relative1 = weight1[:, cin:]
    slope = scales1[0:1, :]
    r1 = scales1[1:2, :]
    outer_scale = slope / scales1[2:3, :]

    pieces = [(n // chips, n % chips) for n in range(total)]
    size1 = -(-2 * cin // total)
    size2 = reduced2.shape[0]
    blocks2 = 4 * LANES // size2
    for copy in loads[:6]:
        copy.wait()

    def sums_of(count, base, values):
        def add(i, carry):
            start = pl.multiple_of(i * CHUNK, CHUNK)
            rows = pl.ds(start, CHUNK)
            return carry + t_by(x1[pl.ds(base + start, CHUNK), :], values[rows, :])

        return lax.fori_loop(0, count // CHUNK, add, jnp.zeros((cin, width1), F32))

    grad_own1 = sums_of(points, half, given1) * slope
    grad_near1 = sums_of(cores * points, 0, near1) * slope
    summed = [
        jnp.concatenate([grad_own1, grad_near1 - grad_own1], axis=0),
        known1[0],
        known1[1],
    ]
    flat1[...] = jnp.zeros(flat1.shape, F32)
    for n, (c, place) in enumerate(pieces):
        if n * size1 < 2 * cin:
            for i, value in enumerate(summed):
                flat1[c, place, i * size1 : (i + 1) * size1, :] = value[
                    n * size1 : (n + 1) * size1
                ]
    flat2[...] = jnp.zeros(flat2.shape, F32)
    for n, (c, place) in enumerate(pieces[:blocks2]):
        block, row = divmod(n * size2, LANES)
        columns = slice(block % 2 * LANES, (block % 2 + 1) * LANES)
        value = grad_own2[row : row + size2, columns]
        if block >= 2:
            value = grad_near2[row : row + size2, columns] - value
        flat2[c, place] = value

    pl.semaphore_wait(barrier, total - 1)
    sum1.swap.start()
    sum2.swap.start()
    gather_start(parts, slots, small_sems.at[0], small_sems.at[1], cores, total)
    sum1.scatter()
    sum2.scatter()
    for copy in loads[6:]:
        copy.wait()
    gather_wait(slots, small_sems.at[0], small_sems.at[1], total)
    sums = slot_sum(slots, total)
    norm1[...] = sums
    beta_scale = outer_scale * sums[0:1]
    gamma_scale = outer_scale * sums[1:2] * r1

    def corrected(value):
        main, gamma_part, beta_part = [
            value[i * size1 : (i + 1) * size1] for i in range(3)
        ]
        main = main - (gamma_part * gamma_scale + beta_part * beta_scale)
        if size1 == SUBLANES:
            return main
        return jnp.concatenate([main, jnp.zeros((SUBLANES - size1, LANES), F32)], axis=0)

    sum1.spread(corrected)
    sum2.spread(lambda value: value)
    for c in range(cores):

        def push(start):
            rows = pl.ds(c * points + start, CHUNK)
            value = near1[rows, :] * slope
            value = value - (counts[rows, :] * beta_scale + away_all1[rows, :] * gamma_scale)
            pushed[c, :, pl.ds(start, CHUNK)] = jnp.transpose(by(value, relative1))

        over(points, CHUNK, push)
    swap = to_partner(pushed.at[1 - core], arrived, pair_sems, 4)
    swap.start()

    def own(start):
        rows = pl.ds(start, CHUNK)
        weights = jnp.broadcast_to(mask[:, rows].astype(F32), (SUBLANES, CHUNK))
        weights = jnp.transpose(weights)[:, :1]
        value = given1[rows, :] * slope
        value = value - (depth * weights * beta_scale + away_own1[rows, :] * gamma_scale)
        from_own[:, rows] = jnp.transpose(by(value, direct1)) + pushed[core, :, rows]

    over(points, CHUNK, own)
    sum1.finish()
    sum2.finish()
    swap.wait()
    from_near[...] = arrived[...]
    sum1.back.wait()
    whole1[...] = all1[...]
    sum2.back.wait()
    whole2[...] = all2[...]


def finish_kernel(
    from_own,
    from_near,
    norm1,
    whole1,
    whole2,
    scales2,
    pooled_in,
    pooled,
    grad_features,
    grad_weight1,
    grad_gain1,
    grad_bias1,
    grad_weight2,
    grad_gain2,
    grad_bias2,
):
    pooled[...] = pooled_in[...]
    grad_features[...] = from_own[...] + from_near[...]
    cores, chips = whole1.shape[:2]
    cin = from_own.shape[0]
    size1 = -(-2 * cin // (cores * chips))
    rows1 = [whole1[n // chips, n % chips, 0:size1, :] for n in range(2 * cin // size1)]
    grad_weight1[...] = jnp.transpose(jnp.concatenate(rows1, axis=0))
    size2 = whole2.shape[2]
    grad_bias1[...] = norm1[0:1, :]
    grad_gain1[...] = norm1[1:2, :]
    for h in range(2):
        rows = slice(h * LANES, (h + 1) * LANES)
        for part in range(2):
            first = (2 * part + h) * LANES // size2
            block = [
                whole2[n // chips, n % chips] for n in range(first, first + LANES // size2)
            ]
            grad_weight2[rows, part * LANES : (part + 1) * LANES] = jnp.transpose(
                jnp.concatenate(block, axis=0)
            )
    grad_bias2[...] = scales2[1:2, :]
    grad_gain2[...] = scales2[2:3, :]


def shaped(*shape):
    return jax.ShapeDtypeStruct(shape, F32)


def scratch(*shape, dtype=F32):
    return pltpu.VMEM(shape, dtype)


def program(mesh):
    cores, chips = mesh.shape["points"], mesh.shape["clouds"]
    total = cores * chips

    def on_device(
        features,
        lengths,
        mask,
        neighbours,
        first_layer_weight,
        first_norm_gain,
        first_norm_bias,
        second_layer_weight,
        second_norm_gain,
        second_norm_bias,
        pooled_grad,
    ):
        cin, points = features.shape
        depth = neighbours.shape[0]
        width1, width2 = first_layer_weight.shape[0], second_layer_weight.shape[0]
        both = cores * points
        clouds = lengths.shape[0]
        mask_row = mask[None, :]
        groups1, groups2 = points // SUBLANES, points // 4

        def layout(subs, groups):
            place = jnp.arange(points, dtype=jnp.int32) // groups
            return (neighbours * subs + (SUBLANES - subs * place)).reshape(-1)

        index1, index2 = layout(1, groups1), layout(2, groups2)
        block = 32
        outs = pl.pallas_call(
            functools.partial(forward_kernel, (cores, total)),
            out_shape=[
                shaped(clouds, 2 * width2),
                shaped(groups1, depth, SUBLANES, LANES),
                shaped(groups2, depth, SUBLANES, LANES),
                shaped(points, width1),
                shaped(points, width1),
                shaped(points, width1),
                shaped(both, cin),
                shaped(points, width1),
                shaped(both, width1),
                shaped(both, LANES),
                shaped(both, width1),
                shaped(2 * points, LANES),
                shaped(both, width2),
                shaped(SUBLANES, width1),
                shaped(points, width1),
                shaped(width1, width2),
                shaped(SUBLANES, width2),
                shaped(2, 2 * cin, width1),
            ],
            in_specs=[VMEM] * 3 + [ANY] * 2 + [SMEM] + [VMEM] * 3 + [ANY] + [VMEM] * 3,
            out_specs=[VMEM] + [ANY] * 12 + [VMEM] * 5,
            scratch_shapes=[
                scratch(2 * points, LANES),
                scratch(both, width2),
                pltpu.SMEM((depth * points,), jnp.int32),
                pltpu.SMEM((depth * points,), jnp.int32),
                scratch(width2, 2 * width1),
                scratch(points, width1),
                scratch(points, width1),
                scratch(points, width1),
                scratch(both, cin),
                scratch(points, width1),
                scratch(both, width1),
                scratch(both, LANES),
                scratch(cores, cin, points),
                scratch(both, LANES, dtype=BF16),
                scratch(depth, LANES, LANES, dtype=BF16),
                scratch(both, points, dtype=BF16),
                scratch(SUBLANES, points),
                scratch(points, LANES),
                scratch(cores, 3 * cin, points, dtype=BF16),
                scratch(2 * width1, both, dtype=BF16),
                scratch(points, width1),
                scratch(both, width1),
                scratch(points, cin),
                scratch(points, width1),
                scratch(both + 2 * SUBLANES, LANES),
                scratch(points, LANES),
                scratch(points, LANES),
                scratch(points, LANES),
                scratch(points, LANES),
                scratch(points, LANES),
                scratch(2 * both + 2 * SUBLANES, LANES),
                scratch(2 * points, LANES),
                scratch(2 * points, LANES),
                scratch(2 * points, LANES),
                scratch(2 * points, LANES),
                scratch(2 * points, LANES),
                scratch(both, width1),
                scratch(points, width2),
                scratch(both, width2),
                scratch(points, width2),
                scratch(points, 2 * width2, dtype=BF16),
                scratch(cores, 3 * clouds, SUBLANES, LANES),
                scratch(3, 4, LANES),
                scratch(3, total, 4, LANES),
                scratch(depth, SUBLANES, LANES),
                scratch(depth, SUBLANES, LANES),
                scratch(2, 2 * block, depth, SUBLANES, LANES),
                pltpu.SemaphoreType.DMA((2, 7)),
                pltpu.SemaphoreType.DMA((2, 3)),
                pltpu.SemaphoreType.DMA((2,)),
                pltpu.SemaphoreType.DMA((3,)),
                pltpu.SemaphoreType.DMA((10,)),
            ],
            compiler_params=pltpu.CompilerParams(
                collective_id=1, has_side_effects=True, vmem_limit_bytes=MEMORY
            ),
            name="forward",
        )(
            features,
            neighbours,
            mask_row,
            index1,
            index2,
            lengths,
            first_layer_weight,
            first_norm_gain[None, :],
            first_norm_bias[None, :],
            second_layer_weight,
            second_norm_gain[None, :],
            second_norm_bias[None, :],
            pooled_grad,
        )
        (
            pooled,
            q1,
            q2,
            inverse1,
            share1,
            moment1,
            x1,
            away_own1,
            away_all1,
            counts,
            x2,
            push2,
            extra2,
            scales1,
            own2,
            grad_own2,
            scales2,
            known1,
        ) = outs

        ring = scratch(3, block, depth, SUBLANES, LANES)
        kept, sent, grad_near2 = pl.pallas_call(
            functools.partial(scatter2_kernel, depth),
            out_shape=[shaped(points, width1), shaped(points, width1), shaped(width1, width2)],
            in_specs=[ANY] * 5 + [VMEM, ANY],
            out_specs=[VMEM] * 3,
            scratch_shapes=[
                pltpu.SMEM((depth * points,), jnp.int32),
                scratch(2 * points, LANES),
                scratch(both, width1),
                scratch(width2, 2 * width1),
                scratch(both, width2),
                ring,
                pltpu.SemaphoreType.DMA((5,)),
                pltpu.SemaphoreType.DMA((3,)),
            ]
            + [scratch(2 * both + 2 * SUBLANES, LANES)] * 12,
            compiler_params=pltpu.CompilerParams(vmem_limit_bytes=MEMORY),
            name="scatter2",
        )(index2, q2, push2, x2, second_layer_weight, scales2, extra2)
        other = lax.ppermute(sent, "points", [(0, 1), (1, 0)])

        near1, given1, parts = pl.pallas_call(
            functools.partial(scatter1_kernel, depth),
            out_shape=[shaped(both, width1), shaped(points, width1), shaped(SUBLANES, width1)],
            in_specs=[ANY] * 2 + [VMEM] * 6,
            out_specs=[VMEM] * 3,
            scratch_shapes=[
                pltpu.SMEM((depth * points,), jnp.int32),
                scratch(points, width1),
                ring,
                pltpu.SemaphoreType.DMA((1,)),
                pltpu.SemaphoreType.DMA((3,)),
            ]
            + [scratch(both + 2 * SUBLANES, LANES)] * (SUBLANES * 2),
            compiler_params=pltpu.CompilerParams(vmem_limit_bytes=MEMORY),
            name="scatter1",
        )(index1, q1, own2, kept, other, inverse1, share1, moment1)

        size1 = -(-2 * cin // total)
        size2 = -(-4 * LANES // (total * SUBLANES)) * SUBLANES
        stacked1 = -(-3 * size1 // SUBLANES) * SUBLANES
        padded1 = -(-size1 // SUBLANES) * SUBLANES
        from_own, from_near, norm1, whole1, whole2 = pl.pallas_call(
            functools.partial(last_kernel, (cores, chips), depth),
            out_shape=[
                shaped(cin, points),
                shaped(cin, points),
                shaped(SUBLANES, width1),
                shaped(cores, chips, padded1, LANES),
                shaped(cores, chips, size2, LANES),
            ],
            in_specs=[ANY] * 2 + [VMEM] + [ANY] * 4 + [VMEM] * 3 + [ANY] * 3,
            out_specs=[VMEM] * 5,
            scratch_shapes=[
                scratch(both, width1),
                scratch(points, width1),
                scratch(both, cin),
                scratch(points, width1),
                scratch(both, width1),
                scratch(both, LANES),
                scratch(width1, width2),
                scratch(width1, width2),
                scratch(2, 2 * cin, width1),
                scratch(total, SUBLANES, LANES),
                scratch(cores, chips, stacked1, LANES),
                scratch(cores, chips, size2, LANES),
                scratch(cores, cin, points),
                scratch(cin, points),
                scratch(chips, stacked1, LANES),
                scratch(chips, size2, LANES),
                scratch(chips, stacked1, LANES),
                scratch(chips, size2, LANES),
                scratch(padded1, LANES),
                scratch(size2, LANES),
                scratch(cores, chips, padded1, LANES),
                scratch(cores, chips, size2, LANES),
                pltpu.SemaphoreType.DMA((2,)),
                pltpu.SemaphoreType.DMA((2, 5)),
                pltpu.SemaphoreType.DMA((2, 4)),
                pltpu.SemaphoreType.DMA((9,)),
            ],
            compiler_params=pltpu.CompilerParams(
                collective_id=2, has_side_effects=True, vmem_limit_bytes=MEMORY
            ),
            name="last",
        )(
            near1,
            given1,
            parts,
            x1,
            away_own1,
            away_all1,
            counts,
            scales1,
            mask_row,
            first_layer_weight,
            grad_own2,
            grad_near2,
            known1,
        )
        outs = pl.pallas_call(
            finish_kernel,
            out_shape=[
                shaped(clouds, 2 * width2),
                shaped(cin, points),
                shaped(width1, 2 * cin),
                shaped(1, width1),
                shaped(1, width1),
                shaped(width2, 2 * width1),
                shaped(1, width2),
                shaped(1, width2),
            ],
            in_specs=[VMEM] * 7,
            out_specs=[VMEM] * 8,
            compiler_params=pltpu.CompilerParams(vmem_limit_bytes=MEMORY),
            name="finish",
        )(
            from_own,
            from_near,
            norm1,
            whole1,
            whole2,
            scales2,
            pooled,
        )
        return tuple(
            value.reshape(-1) if value.shape[0] == 1 else value for value in outs
        )

    return on_device


def solution(mesh):
    in_specs = (
        P(None, ("clouds", "points")),
        P("clouds"),
        P(("clouds", "points")),
        P(None, ("clouds", "points")),
        P(),
        P(),
        P(),
        P(),
        P(),
        P(),
        P("clouds", None),
    )
    out_specs = (P("clouds", None), P(None, ("clouds", "points")), P(), P(), P(), P(), P(), P())
    return jax.shard_map(
        program(mesh), mesh=mesh, in_specs=in_specs, out_specs=out_specs, check_vma=False
    )
```

```python
import functools
import math

import jax
import jax.numpy as jnp
from jax import lax
from jax.experimental import pallas as pl
from jax.experimental.pallas import tpu as pltpu
from jax.sharding import PartitionSpec as P

EPSILON = 1e-05
LOG2E = math.log2(math.e)
LN2 = math.log(2.0)
MESH = pl.DeviceIdType.MESH
F32 = jnp.float32
BF16 = jnp.bfloat16
LANES = 128
SUBLANES = 8
CHUNK = 256
MEMORY = 60 * 2**20
VMEM = pl.BlockSpec(memory_space=pltpu.VMEM)
SMEM = pl.BlockSpec(memory_space=pltpu.SMEM)
ANY = pl.BlockSpec(memory_space=pl.ANY)


def dot(left, right, dims):
    return lax.dot_general(
        left,
        right,
        (dims, ((), ())),
        precision=lax.Precision.HIGHEST,
        preferred_element_type=F32,
    )


def mm(left, right):
    return dot(left, right, ((1,), (0,)))


def mm_nt(left, right):
    return dot(left, right, ((1,), (1,)))


def mm_tn(left, right):
    return dot(left, right, ((0,), (0,)))


def mm_low(left, right):
    return lax.dot_general(
        left, right, (((1,), (0,)), ((), ())), preferred_element_type=F32
    )


def split(value):
    high = value.astype(BF16)
    low = (value - high.astype(F32)).astype(BF16)
    return high, low


def product(left, right, dims):
    def part(a, b):
        return lax.dot_general(a, b, (dims, ((), ())), preferred_element_type=F32)

    left_high, left_low = split(left)
    right_high, right_low = split(right)
    return part(left_high, right_high) + (part(left_high, right_low) + part(left_low, right_high))


def by(left, right):
    return product(left, right, ((1,), (0,)))


def by_t(left, right):
    return product(left, right, ((1,), (1,)))


def t_by(left, right):
    return product(left, right, ((0,), (0,)))


def thirds(value):
    high, rest = value.astype(BF16), value - value.astype(BF16).astype(F32)
    middle = rest.astype(BF16)
    return high, middle, (rest - middle.astype(F32)).astype(BF16)


def stacks(value, dim):
    high, middle, low = thirds(value)
    return [jnp.concatenate(parts, axis=dim) for parts in ((high, middle), (high, low))]


def weight_stacks(value, dim):
    high, middle, low = thirds(value)
    return [
        jnp.concatenate(parts, axis=dim)
        for parts in ((high, high), (middle, middle), (low, high))
    ]


def exact(left, right, dims):
    def part(a, b):
        return lax.dot_general(a, b, (dims, ((), ())), preferred_element_type=F32)

    return part(left[0], right[0]) + (part(left[0], right[1]) + part(left[1], right[2]))


def quad_stacks(value):
    high, middle, low = thirds(value)
    return [
        jnp.concatenate(parts, axis=0) for parts in ((high, high, middle, middle), (high, low))
    ]


def quad_weights(value):
    high, middle, low = thirds(value)
    return [
        jnp.concatenate(parts, axis=0) for parts in ((high, middle, high, middle), (low, high))
    ]


def exact_quad(left, right):
    def part(a, b):
        return lax.dot_general(a, b, (((0,), (0,)), ((), ())), preferred_element_type=F32)

    return part(left[0], right[0]) + part(left[1], right[1])


def over(count, step, body, times=1):
    def run(i, carry):
        for t in range(times):
            body(pl.multiple_of((i * times + t) * step, step))
        return carry

    lax.fori_loop(0, count // (step * times), run, 0)


def tree(values, join):
    values = list(values)
    while len(values) > 1:
        values = [
            join(values[i], values[i + 1]) if i + 1 < len(values) else values[i]
            for i in range(0, len(values), 2)
        ]
    return values[0]


def iota(shape, dim):
    return lax.broadcasted_iota(jnp.int32, shape, dim)


def signal_all(barrier, cores, total):
    me = lax.axis_index("clouds") * cores + lax.axis_index("points")

    def send(d, carry):
        t = lax.rem(me + d, total)
        pl.semaphore_signal(
            barrier,
            inc=1,
            device_id=(lax.div(t, cores), lax.rem(t, cores)),
            device_id_type=MESH,
        )
        return carry

    lax.fori_loop(1, total, send, 0)


def gather_start(own, slots, send_sem, recv_sem, cores, total):
    me = lax.axis_index("clouds") * cores + lax.axis_index("points")
    slots[me] = own[...]

    def send(d, carry):
        t = lax.rem(me + d, total)
        pltpu.make_async_remote_copy(
            src_ref=own,
            dst_ref=slots.at[me],
            send_sem=send_sem,
            recv_sem=recv_sem,
            device_id=(lax.div(t, cores), lax.rem(t, cores)),
            device_id_type=MESH,
        ).start()
        return carry

    lax.fori_loop(1, total, send, 0)


def gather_wait(slots, send_sem, recv_sem, total):
    others = slots.at[pl.ds(0, total - 1)]
    arrived = pltpu.make_async_remote_copy(
        src_ref=others,
        dst_ref=others,
        send_sem=send_sem,
        recv_sem=recv_sem,
        device_id=(lax.axis_index("clouds"), 1 - lax.axis_index("points")),
        device_id_type=MESH,
    )
    arrived.wait_recv()
    arrived.wait_send()


def slot_sum(slots, total):
    def add(i, carry):
        return carry + slots[i]

    return lax.fori_loop(1, total, add, slots[0])


def to_partner(source, target, sems, index):
    return pltpu.make_async_remote_copy(
        src_ref=source,
        dst_ref=target,
        send_sem=sems.at[0, index],
        recv_sem=sems.at[1, index],
        device_id=(lax.axis_index("clouds"), 1 - lax.axis_index("points")),
        device_id_type=MESH,
    )


def edge_pass(
    subs, block, depth, index, table, own_rows, out_hbm, held, ring, sems, outs, pending, after_block
):
    level_ref, share_ref, moment_ref, inverse_ref = outs
    per = SUBLANES // subs
    groups = own_rows.shape[0] // SUBLANES
    row = iota((SUBLANES, LANES), 0)
    mine = [(row >= subs * i) & (row < subs * (i + 1)) for i in range(per)]
    def fetch(group, slot):
        for k in range(depth):
            target = held[slot].at[k]
            for i in range(per):
                first = (k * per + i) * groups
                j = index.at[pl.ds(first, groups)][group]
                value = table[pl.ds(j, SUBLANES), :]
                if i == 0:
                    target[...] = value
                else:
                    pltpu.store(target, value, mask=mine[i])

    def work(group, slot, ring_slot, place):
        rows = pl.ds(pl.multiple_of(group * SUBLANES, SUBLANES), SUBLANES)
        peak = tree([held[slot][k] for k in range(depth)], jnp.maximum)
        top = own_rows[rows, :] + peak
        shift = jnp.maximum(top, 0.0)
        rest = jnp.maximum(jnp.exp2(-shift), 2.0**-100)
        under = jnp.maximum(jnp.minimum(top, 0.0), -100.0)
        offset = under - peak
        fifth = 0.2 * rest
        total, share, moment = [], [], []
        for k in range(depth):
            value = held[slot][k]
            power = value + offset
            grown = jnp.exp2(power)
            root = jnp.exp2((power - lax.log2(rest + grown)) * 0.2)
            weight = root * (fifth + grown)
            ring[ring_slot, place, k] = weight
            total.append(root)
            share.append(weight)
            moment.append(weight * value)
        total, share, moment = [
            functools.reduce(jnp.add, parts) for parts in (total, share, moment)
        ]
        mass = share + (0.8 * rest) * total
        inverse = 1.0 / mass
        level = 0.2 * (top - under) + 0.8 * shift + lax.log2(mass)
        level_ref[rows, :] = LN2 * level - math.log(depth)
        inverse_ref[rows, :] = inverse
        share_ref[rows, :] = share * inverse
        moment_ref[rows, :] = moment * inverse

    blocks = groups // block

    def push(b, slot):
        return pltpu.make_async_copy(
            ring.at[slot, pl.ds(0, block)], out_hbm.at[pl.ds(b * block, block)], sems.at[slot]
        )

    fetch(0, 0)

    def one_block(b, carry):
        ring_slot = lax.rem(b, 2)

        if pending is None:

            @pl.when(b >= 2)
            def _():
                push(b - 2, ring_slot).wait()

        else:

            @pl.when(b < 2)
            def _():
                pending(ring_slot).wait()

            @pl.when(b >= 2)
            def _():
                push(b - 2, ring_slot).wait()

        def several(t, inner):
            for unit in range(4):
                slot = unit % 2
                place = t * 4 + unit
                group = b * block + place
                work(group, slot, ring_slot, place)
                fetch(jnp.minimum(group + 1, groups - 1), 1 - slot)
            return inner

        lax.fori_loop(0, block // 4, several, 0)
        push(b, ring_slot).start()
        if after_block is not None:
            after_block(b)
        return carry

    lax.fori_loop(0, blocks, one_block, 0)
    return lambda slot: push(blocks - 2 + slot, slot)


def lanes_to_rows(value, width):
    return [value[:, i * LANES : (i + 1) * LANES] for i in range(width // LANES)]


def rows_to_lanes(rows):
    return rows[0] if len(rows) == 1 else jnp.concatenate(rows, axis=1)


def forward_kernel(
    sizes,
    feat,
    near,
    mask,
    index1_in,
    index2_in,
    lengths,
    weight1,
    gain1,
    bias1,
    weight2_in,
    gain2,
    bias2,
    pooled_grad,
    pooled,
    q1,
    q2,
    inverse1_out,
    share1_out,
    moment1_out,
    x1_out,
    away_own1_out,
    away_all1_out,
    counts_out,
    x2_out,
    push2_out,
    extra2_out,
    scales1,
    own2,
    grad_own2,
    scales2,
    known1,
    push2,
    extra2,
    index1,
    index2,
    weight2,
    inverse1,
    share1,
    moment1,
    x1,
    away_own1,
    away_all1,
    counts,
    x1_cm,
    tallies,
    lows,
    links,
    live,
    live_col,
    parts1,
    parts2,
    u1,
    v1,
    g1,
    table1,
    own_rows1,
    level1,
    other1,
    share_rows1,
    moment_rows1,
    table2,
    own_rows2,
    level2,
    share2,
    moment2,
    inverse2,
    x2,
    u2,
    v2,
    g2,
    u_parts,
    pool_parts,
    message,
    slots,
    held0,
    held1,
    ring,
    pair_sems,
    all_sems,
    ring_sems,
    load_sems,
    store_sems,
):
    cores, total = sizes
    points = feat.shape[1]
    cin = feat.shape[0]
    both = cores * points
    depth = near.shape[0]
    width1 = weight1.shape[0]
    width2 = gain2.shape[1]
    groups1, groups2 = points // SUBLANES, 2 * points // SUBLANES
    core = lax.axis_index("points")
    half = pl.multiple_of(core * points, points)
    barrier = pltpu.get_barrier_semaphore()
    signal_all(barrier, cores, total)
    loads = [
        pltpu.make_async_copy(source, target, load_sems.at[i])
        for i, (source, target) in enumerate(
            ((index1_in, index1), (index2_in, index2), (weight2_in, weight2))
        )
    ]
    for copy in loads:
        copy.start()
    late = [
        pltpu.make_async_copy(source, target, store_sems.at[8 + i])
        for i, (source, target) in enumerate(((push2, push2_out), (extra2, extra2_out)))
    ]
    stores = [
        pltpu.make_async_copy(source, target, store_sems.at[i])
        for i, (source, target) in enumerate(
            (
                (x1, x1_out),
                (counts, counts_out),
                (away_own1, away_own1_out),
                (away_all1, away_all1_out),
                (inverse1, inverse1_out),
                (share1, share1_out),
                (moment1, moment1_out),
                (x2, x2_out),
            )
        )
    ]

    live[...] = jnp.broadcast_to(mask[...].astype(F32), live.shape)
    row16 = iota((16, LANES), 0)
    one, none = jnp.ones((16, LANES), BF16), jnp.zeros((16, LANES), BF16)

    def build(columns, first):
        high_names, low_names = [], []
        for k in range(depth):
            name = near[k : k + 1, columns]
            high = jnp.where(mask[:, columns] > 0, lax.shift_right_logical(name, 7), -1)
            for names, value in ((high_names, high), (low_names, name & (LANES - 1))):
                names.append(jnp.broadcast_to(value, (16, LANES)).astype(jnp.int16))
        for s in range(0, LANES, 16):
            target = (row16 + s).astype(jnp.int16)
            for k in range(depth):
                lows[k, s : s + 16, :] = jnp.where(low_names[k] == target, one, none)

        def one_high(start):
            target = jnp.full((16, LANES), lax.shift_right_logical(start, 7), jnp.int32)
            target = target.astype(jnp.int16)
            meant = [jnp.where(name == target, one, none) for name in high_names]
            for s in range(0, LANES, 16):
                found = tree([meant[k] * lows[k, s : s + 16, :] for k in range(depth)], jnp.add)
                here = pl.ds(start + s, 16)
                links[here, columns] = found
                tallies[here, :] = found if first else tallies[here, :] + found

        over(both, LANES, one_high)

    tiles = points // LANES
    early = tiles - tiles // 4
    for tile in range(early):
        build(pl.ds(tile * LANES, LANES), tile == 0)
    x1_cm[core] = feat[...]
    pl.semaphore_wait(barrier, total - 1)
    swap = to_partner(feat, x1_cm.at[core], pair_sems, 0)
    swap.start()
    for tile in range(early, tiles):
        build(pl.ds(tile * LANES, LANES), tile == 0)
    live_col[...] = jnp.broadcast_to(jnp.transpose(live[...])[:, :1], live_col.shape)
    swap.wait()

    direct1 = weight1[:, :cin] - weight1[:, cin:]
    relative1 = weight1[:, cin:]
    for c in range(cores):

        def turn(start):
            x1[pl.ds(c * points + start, CHUNK), :] = jnp.transpose(
                x1_cm[c, :, pl.ds(start, CHUNK)]
            )

        over(points, CHUNK, turn, 2)
        value = x1_cm[c]
        high, low = split(value)
        lower = (value - high.astype(F32) - low.astype(F32)).astype(BF16)
        parts1[c, 0:cin, :] = high
        parts1[c, cin : 2 * cin, :] = low
        parts1[c, 2 * cin : 3 * cin, :] = lower

    direct_parts1 = quad_weights(jnp.transpose(direct1))
    relative_parts1 = quad_weights(jnp.transpose(relative1))

    def sums_near1(start):
        columns = pl.ds(start, CHUNK)
        value = mm_low(parts1[0], links[0:points, columns])
        for c in range(1, cores):
            value = value + mm_low(parts1[c], links[c * points : (c + 1) * points, columns])
        value = value[0:cin] + value[cin : 2 * cin] + value[2 * cin : 3 * cin]
        g1[columns, :] = exact_quad(quad_stacks(value), relative_parts1)

    over(points, CHUNK, sums_near1, 2)

    stores[0].start()
    ones = jnp.ones((LANES, LANES), BF16)

    def count_links(start):
        rows = pl.ds(start, CHUNK)
        counts[rows, :] = mm_low(tallies[rows, :], ones)

    over(both, CHUNK, count_links, 4)
    stores[1].start()

    live_sum = jnp.sum(live[0:1, :], axis=1, keepdims=True)
    mine = live_sum * depth

    def live_total(start, size, value):
        high, low = split(value)
        weights = live[:, start : start + size].astype(BF16)
        return (mm_low(weights, high) + mm_low(weights, low))[0:1]

    def statistics(u, v, g, width):
        for c in range(cores):

            def outer(start):
                left = quad_stacks(x1_cm[c, :, pl.ds(start, CHUNK)])
                v[pl.ds(c * points + start, CHUNK), :] = exact_quad(left, relative_parts1)

            over(points, CHUNK, outer, 2)

        def inner(start):
            rows = pl.ds(start, CHUNK)
            u[rows, :] = exact_quad(quad_stacks(x1_cm[core, :, rows]), direct_parts1)

        over(points, CHUNK, inner, 2)
        u_sum = live_total(0, points, u[...])
        g_sum = jnp.sum(g[...], axis=0, keepdims=True)
        u_mean = u_sum / live_sum
        v_mean = g_sum / mine
        centred = u[...] - u_mean
        spread = depth * centred * centred + 2.0 * centred * (g[...] - depth * v_mean)
        square = live_total(0, points, spread)
        weights = rows_to_lanes([counts[...]] * (width // LANES))
        away = v[...] - v_mean
        square = square + jnp.sum(weights * away * away, axis=0, keepdims=True)
        return depth * u_sum + g_sum, square, u_mean, v_mean

    def send_sums(use, rows):
        for i, value in enumerate(rows):
            message[use, i : i + 1, :] = value
        gather_start(
            message.at[use], slots.at[use], all_sems.at[0, use], all_sems.at[1, use], cores, total
        )

    def receive(use):
        gather_wait(slots.at[use], all_sems.at[0, use], all_sems.at[1, use], total)

    def combine(use, numbers, width):
        per = width // LANES
        count = numbers[0]
        for value in numbers[1:]:
            count = count + value

        def value_of(i, first):
            return rows_to_lanes([slots[use, i, first + h : first + h + 1, :] for h in range(per)])

        mean = value_of(0, 0)
        for i in range(1, total):
            mean = mean + value_of(i, 0)
        mean = mean / count
        square = None
        for i in range(total):
            gap = value_of(i, 0) / numbers[i] - mean
            term = value_of(i, per) + numbers[i] * gap * gap
            square = term if square is None else square + term
        return count, mean, square / count

    sums, square, u_mean1, v_mean1 = statistics(u1, v1, g1, width1)
    send_sums(0, [sums, square, jnp.broadcast_to(mine, (1, LANES)), jnp.zeros((1, LANES), F32)])

    for part, value in enumerate(split(u1[...] - u_mean1)):
        u_parts[:, part * LANES : (part + 1) * LANES] = value

    def shared1(start):
        rows = pl.ds(start, CHUNK)
        value = mm_low(links[rows, :], u_parts[:, 0 : 2 * LANES])
        away_all1[rows, :] = value[:, :LANES] + value[:, LANES:]

    over(both, CHUNK, shared1, 2)
    receive(0)
    numbers = [slots[0, i, 2:3, 0:1] for i in range(total)]
    count, mean1, variance1 = combine(0, numbers, width1)
    r1 = lax.rsqrt(variance1 + EPSILON)
    slope1 = gain1[...] * r1
    scales1[...] = jnp.concatenate(
        [slope1, r1, jnp.broadcast_to(count, (1, LANES)), jnp.zeros((5, LANES), F32)], axis=0
    )

    def fill1(start):
        rows = pl.ds(start, CHUNK)
        table1[pl.ds(SUBLANES + start, CHUNK), :] = (v1[rows, :] - v_mean1) * (slope1 * LOG2E)
        away_all1[rows, :] += counts[rows, :] * (v1[rows, :] - (mean1 - u_mean1))

    over(both, CHUNK, fill1, 2)

    def fill_own1(start):
        rows = pl.ds(start, CHUNK)
        value = (u1[rows, :] - (mean1 - v_mean1)) * (slope1 * LOG2E) + bias1[...] * LOG2E
        for s in range(0, CHUNK, groups1):
            here = pl.ds(lax.div(start, groups1) + s // groups1, groups1, stride=SUBLANES)
            own_rows1[here, :] = value[s : s + groups1]
        away_own1[rows, :] = depth * live_col[rows, :] * (u1[rows, :] - mean1) + g1[rows, :]

    over(points, CHUNK, fill_own1, 2)

    stores[2].start()
    stores[3].start()
    loads[0].wait()
    block1, block2 = groups1 // 4, ring.shape[1]
    block_rows = block1 * SUBLANES
    blocks1 = 4

    def hand_over(b):
        rows = pl.ds(pl.multiple_of(b * block_rows, block_rows), block_rows)
        return to_partner(level1.at[rows], other1.at[rows], pair_sems, 3 + b)

    pending = edge_pass(
        1,
        block1,
        depth,
        index1,
        table1,
        own_rows1,
        q1,
        (held0, held1),
        ring,
        ring_sems,
        (level1, share_rows1, moment_rows1, inverse1),
        None,
        lambda b: hand_over(b).start(),
    )

    inverse_gain1 = 1.0 / (gain1[...] * LOG2E)
    for i in range(SUBLANES):
        here = pl.ds(i, groups1, stride=SUBLANES)
        x2[pl.ds(half + i * groups1, groups1), :] = level1[here, :]
        offset = own_rows1[here, :] - bias1[...] * LOG2E
        rows = slice(i * groups1, (i + 1) * groups1)
        moment1[rows, :] = (share_rows1[here, :] * offset + moment_rows1[here, :]) * inverse_gain1
        share1[rows, :] = share_rows1[here, :]
    for copy in stores[4:7]:
        copy.start()
    loads[1].wait()
    loads[2].wait()
    for b in range(blocks1):
        hand_over(b).wait()
    other_half = pl.multiple_of((1 - core) * points, points)
    for i in range(SUBLANES):
        here = pl.ds(i, groups1, stride=SUBLANES)
        x2[pl.ds(other_half + i * groups1, groups1), :] = other1[here, :]
    stores[7].start()

    direct2 = weight2[:, :width1] - weight2[:, width1:]
    relative2 = weight2[:, width1:]

    direct_parts2 = weight_stacks(direct2, 1)
    relative_parts2 = weight_stacks(relative2, 1)

    def turn2(start):
        high, low = split(jnp.transpose(x2[pl.ds(start, CHUNK), :]))
        parts2[0:width1, pl.ds(start, CHUNK)] = high
        parts2[width1 : 2 * width1, pl.ds(start, CHUNK)] = low

    over(both, CHUNK, turn2, 4)

    def sums_near2(start):
        columns = pl.ds(start, CHUNK)
        value = mm_low(parts2[...], links[:, columns])
        value = value[0:width1] + value[width1 : 2 * width1]
        g2[columns, :] = exact(stacks(jnp.transpose(value), 1), relative_parts2, ((1,), (1,)))

    over(points, CHUNK, sums_near2, 2)

    def statistics2():
        def outer(start):
            rows = pl.ds(start, CHUNK)
            v2[rows, :] = exact(stacks(x2[rows, :], 1), relative_parts2, ((1,), (1,)))

        over(both, CHUNK, outer, 2)

        def inner(start):
            left = stacks(x2[pl.ds(half + start, CHUNK), :], 1)
            u2[pl.ds(start, CHUNK), :] = exact(left, direct_parts2, ((1,), (1,)))

        over(points, CHUNK, inner, 2)
        u_sum = jnp.zeros((1, width2), F32)
        g_sum = jnp.zeros((1, width2), F32)
        for s in range(0, points, CHUNK):
            u_sum = u_sum + live_total(s, CHUNK, u2[s : s + CHUNK, :])
            g_sum = g_sum + jnp.sum(g2[s : s + CHUNK, :], axis=0, keepdims=True)
        u_mean = u_sum / live_sum
        v_mean = g_sum / mine
        square = jnp.zeros((1, width2), F32)
        for s in range(0, points, CHUNK):
            centred = u2[s : s + CHUNK, :] - u_mean
            spread = depth * centred * centred + 2.0 * centred * (
                g2[s : s + CHUNK, :] - depth * v_mean
            )
            square = square + live_total(s, CHUNK, spread)

        def squares(i, carry):
            rows = pl.ds(pl.multiple_of(i * CHUNK, CHUNK), CHUNK)
            away = v2[rows, :] - v_mean
            weights = rows_to_lanes([counts[rows, :]] * (width2 // LANES))
            return carry + jnp.sum(weights * away * away, axis=0, keepdims=True)

        square = lax.fori_loop(0, both // CHUNK, squares, square)
        return depth * u_sum + g_sum, square, u_mean, v_mean

    sums, square, u_mean2, v_mean2 = statistics2()
    send_sums(1, lanes_to_rows(sums, width2) + lanes_to_rows(square, width2))
    for part, value in enumerate(split(u2[...] - u_mean2)):
        u_parts[:, part * width2 : (part + 1) * width2] = value

    def shared2(start):
        rows = pl.ds(start, CHUNK)
        extra2[rows, :] = mm_low(links[rows, :], u_parts[:, 0:width2]) + mm_low(
            links[rows, :], u_parts[:, width2:]
        )

    over(both, CHUNK, shared2, 2)
    receive(1)
    count, mean2, variance2 = combine(1, numbers, width2)
    r2 = lax.rsqrt(variance2 + EPSILON)
    slope2 = gain2[...] * r2
    scales2[...] = jnp.concatenate([slope2, jnp.zeros((7, width2), F32)], axis=0)

    def fill2(start):
        rows = pl.ds(start, CHUNK)
        value = (v2[rows, :] - v_mean2) * (slope2 * LOG2E)
        for h in range(2):
            table2[pl.ds(SUBLANES + 2 * start + h, CHUNK, stride=2), :] = value[
                :, h * LANES : (h + 1) * LANES
            ]

    over(both, CHUNK, fill2, 2)

    for i in range(SUBLANES // 2):
        rows = slice(i * groups2, (i + 1) * groups2)
        value = (u2[rows, :] - (mean2 - v_mean2)) * (slope2 * LOG2E) + bias2[...] * LOG2E
        for h in range(2):
            own_rows2[pl.ds(2 * i + h, groups2, stride=SUBLANES), :] = value[
                :, h * LANES : (h + 1) * LANES
            ]

    pending = edge_pass(
        2,
        block2,
        depth,
        index2,
        table2,
        own_rows2,
        q2,
        (held0, held1),
        ring,
        ring_sems,
        (level2, share2, moment2, inverse2),
        pending,
        None,
    )

    clouds = pooled_grad.shape[0]
    ends = [lengths[0]]
    for q in range(1, clouds):
        ends.append(ends[-1] + lengths[q])
    row = iota((SUBLANES, LANES), 0)
    odd = lax.rem(row, 2) == 1
    point_of_row = half + lax.div(row, 2) * groups2
    steps = level2.shape[0] // SUBLANES
    lowest = jnp.full((SUBLANES, LANES), -1e30, F32)
    zero = jnp.zeros((SUBLANES, LANES), F32)

    def past(t):
        position = point_of_row + t
        return [position >= ends[q] for q in range(clouds - 1)]

    def pick(after, values):
        value = values[0]
        for q in range(1, clouds):
            value = jnp.where(after[q - 1], values[q], value)
        return value

    def apart(after, value, none):
        out = []
        for q in range(clouds):
            kept = value if q == 0 else jnp.where(after[q - 1], value, none)
            out.append(kept if q == clouds - 1 else jnp.where(after[q], none, kept))
        return out

    def step_rows(t):
        return pl.ds(pl.multiple_of(t * SUBLANES, SUBLANES), SUBLANES)

    def by_parity(value, join):
        value = join(value, pltpu.roll(value, 2, 0))
        return join(value, pltpu.roll(value, 4, 0))

    def unrolled(body, state, times):
        def several(i, carry):
            for u in range(times):
                carry = body(i * times + u, carry)
            return carry

        return lax.fori_loop(0, steps // times, several, state)

    def peaks(t, carry):
        value = level2[step_rows(t), :]
        after = past(t)
        tops = [jnp.maximum(a, b) for a, b in zip(carry, apart(after, value, lowest))]
        adds = [a + b for a, b in zip(carry[clouds:], apart(after, value, zero))]
        return tuple(tops + adds)

    state = unrolled(peaks, (lowest,) * clouds + (zero,) * clouds, 8)
    peak = [by_parity(value, jnp.maximum) for value in state[:clouds]]
    sums = [by_parity(value, jnp.add) for value in state[clouds:]]

    def masses(t, carry):
        after = past(t)
        value = jnp.exp(level2[step_rows(t), :] - pick(after, peak))
        return tuple(a + b for a, b in zip(carry, apart(after, value, zero)))

    state = unrolled(masses, (zero,) * clouds, 8)
    mass = [by_parity(value, jnp.add) for value in state]
    for q in range(clouds):
        pool_parts[core, 3 * q] = peak[q]
        pool_parts[core, 3 * q + 1] = mass[q]
        pool_parts[core, 3 * q + 2] = sums[q]
    here = pool_parts.at[core]
    swap = to_partner(here, here, pair_sems, 2)
    swap.start()
    swap.wait()

    level, grad_level, grad_mean = [], [], []
    for q in range(clouds):
        top = pool_parts[0, 3 * q]
        for c in range(1, cores):
            top = jnp.maximum(top, pool_parts[c, 3 * q])
        whole, sum_all = zero, zero
        for c in range(cores):
            whole = whole + pool_parts[c, 3 * q + 1] * jnp.exp(pool_parts[c, 3 * q] - top)
            sum_all = sum_all + pool_parts[c, 3 * q + 2]
        level.append(top + jnp.log(whole))
        size = jnp.full((SUBLANES, LANES), lengths[q].astype(F32), F32)
        first = level[q] - jnp.log(size)
        second = sum_all / size
        for h in range(2):
            pooled[q : q + 1, h * LANES : (h + 1) * LANES] = first[h : h + 1]
            pooled[q : q + 1, (2 + h) * LANES : (3 + h) * LANES] = second[h : h + 1]
        given = [pooled_grad[q : q + 1, h * LANES : (h + 1) * LANES] for h in range(4)]
        grad_level.append(jnp.where(odd, given[1], given[0]))
        grad_mean.append(jnp.where(odd, given[3], given[2]) / size)

    slope_rows, bias_rows = [], []
    for ref_value, target in ((gain2[...], slope_rows), (bias2[...], bias_rows)):
        low_half, high_half = lanes_to_rows(ref_value * LOG2E, width2)
        target.append(jnp.where(odd, high_half, low_half))
    inverse_gain = 1.0 / slope_rows[0]
    bias_row = bias_rows[0]

    def gradient(t, carry):
        rows = step_rows(t)
        after = past(t)
        value = pick(after, grad_level) * jnp.exp(level2[rows, :] - pick(after, level))
        value = value + pick(after, grad_mean)
        push2[rows, :] = value * inverse2[rows, :]
        share = share2[rows, :]
        moment = (share * (own_rows2[rows, :] - bias_row) + moment2[rows, :]) * inverse_gain
        given = value * share
        share2[rows, :] = given
        return carry[0] + given, carry[1] + value * moment

    state = unrolled(gradient, (zero, zero), 8)
    grad_beta, grad_gamma = [by_parity(value, jnp.add) for value in state]
    late[0].start()
    send_sums(2, [grad_beta[0:1], grad_beta[1:2], grad_gamma[0:1], grad_gamma[1:2]])

    known1[...] = jnp.zeros(known1.shape, F32)

    def known(start):
        near_rows = pl.ds(start, CHUNK)
        known1[0, cin:, :] += t_by(x1[near_rows, :], away_all1[near_rows, :])
        known1[1, cin:, :] += t_by(x1[near_rows, :], counts[near_rows, :])

    over(both, CHUNK, known, 2)

    def known_own(start):
        rows = pl.ds(start, CHUNK)
        here = x1[pl.ds(half + start, CHUNK), :]
        known1[0, 0:cin, :] += t_by(here, away_own1[rows, :])
        known1[1, 0:cin, :] += t_by(here, depth * live_col[rows, :])

    over(points, CHUNK, known_own, 2)
    for i in range(2):
        known1[i, cin:, :] -= known1[i, 0:cin, :]
    receive(2)
    sums = slot_sum(slots.at[2], total)
    grad_beta = rows_to_lanes([sums[0:1], sums[1:2]])
    grad_gamma = rows_to_lanes([sums[2:3], sums[3:4]])
    scales2[1:2, :] = grad_beta
    scales2[2:3, :] = grad_gamma
    outer_scale = slope2 / count
    gamma_scale = outer_scale * grad_gamma * r2
    beta_scale = outer_scale * grad_beta

    def extra(start):
        rows = pl.ds(start, CHUNK)
        weights = rows_to_lanes([counts[rows, :]] * 2)
        away = extra2[rows, :] + weights * (v2[rows, :] - (mean2 - u_mean2))
        extra2[rows, :] = weights * beta_scale + away * gamma_scale

    over(both, CHUNK, extra, 2)
    late[1].start()
    grad_own2[...] = jnp.zeros(grad_own2.shape, F32)

    for i in range(SUBLANES // 2):
        rows = slice(i * groups2, (i + 1) * groups2)
        weights = rows_to_lanes([live_col[rows, :]] * 2)
        given = rows_to_lanes(
            [share2[pl.ds(2 * i + h, groups2, stride=SUBLANES), :] for h in range(2)]
        )
        away = depth * weights * (u2[rows, :] - mean2) + g2[rows, :]
        value = given * slope2 - (depth * weights * beta_scale + away * gamma_scale)
        own2[rows, :] = by(value, direct2)
        grad_own2[...] += t_by(x2[pl.ds(half + i * groups2, groups2), :], value)
    for copy in stores + late + [pending(0), pending(1)]:
        copy.wait()


def scatter_loop(subs, depth, index, q_hbm, ring, sems, push, sums, clear):
    per = SUBLANES // subs
    groups = q_hbm.shape[0]
    slots, block = ring.shape[0], ring.shape[1]
    blocks = groups // block
    row = iota((SUBLANES, LANES), 0)
    mine = [(row >= subs * i) & (row < subs * (i + 1)) for i in range(per)]
    ways = len(sums) // per

    def pull(b):
        slot = lax.rem(b, slots)
        return pltpu.make_async_copy(
            q_hbm.at[pl.ds(b * block, block)], ring.at[slot], sems.at[slot]
        )

    for b in range(slots - 1):
        pull(b).start()
    clear()

    def one_block(b, carry):
        @pl.when(b + slots - 1 < blocks)
        def _():
            pull(b + slots - 1).start()

        pull(b).wait()
        slot = lax.rem(b, slots)

        def one_group(place, inner):
            group = b * block + place
            rows = pl.ds(pl.multiple_of(group * SUBLANES, SUBLANES), SUBLANES)
            given = push[rows, :]

            for k in range(depth):
                value = ring[slot, place, k] * given
                for i in range(per):
                    j = index.at[pl.ds((k * per + i) * groups, groups)][group]
                    target = sums[i * ways + k % ways].at[pl.ds(j, SUBLANES), :]
                    pltpu.store(target, target[...] + value, mask=mine[i])
            return inner

        lax.fori_loop(0, block, one_group, 0)
        return carry

    lax.fori_loop(0, blocks, one_block, 0)


def clear(sums):
    rows = sums[0].shape[0]
    zero = jnp.zeros((SUBLANES, LANES), F32)

    def rows32(start):
        for ref in sums:
            for s in range(0, 4 * SUBLANES, SUBLANES):
                ref[pl.ds(start + s, SUBLANES), :] = zero

    over(rows, 4 * SUBLANES, rows32)
    for s in range(rows // 32 * 32, rows, SUBLANES):
        for ref in sums:
            ref[s : s + SUBLANES, :] = zero


def scatter2_kernel(
    depth,
    index_in,
    q_hbm,
    push_in,
    x2_in,
    weight_in,
    scales,
    extra_in,
    kept,
    sent,
    grad_near,
    index,
    push,
    x2,
    weight,
    extra,
    ring,
    load_sems,
    ring_sems,
    *sums,
):
    loads = [
        pltpu.make_async_copy(source, target, load_sems.at[i])
        for i, (source, target) in enumerate(
            ((index_in, index), (push_in, push), (x2_in, x2), (weight_in, weight), (extra_in, extra))
        )
    ]

    def prepare():
        for copy in loads[2:]:
            copy.start()
        clear(sums)
        loads[0].wait()
        loads[1].wait()

    for copy in loads[:2]:
        copy.start()
    scatter_loop(2, depth, index, q_hbm, ring, ring_sems, push, sums, prepare)
    for copy in loads[2:]:
        copy.wait()
    points, width = kept.shape
    relative = weight[:, width:]
    core = lax.axis_index("points")
    grad_near[...] = jnp.zeros(grad_near.shape, F32)
    for part, out in ((1 - core, sent), (core, kept)):

        def finish(start):
            first = pl.multiple_of(part * points + start, CHUNK)
            rows = pl.ds(first, CHUNK)
            halves = []
            for h in range(2):
                here = pl.ds(SUBLANES + 2 * first + h, CHUNK, stride=2)
                halves.append(tree([ref[here, :] for ref in sums], jnp.add))
            value = rows_to_lanes(halves) * scales[0:1, :] - extra[rows, :]
            out[pl.ds(start, CHUNK), :] = by(value, relative)
            grad_near[...] += t_by(x2[rows, :], value)

        over(points, CHUNK, finish, 2)


def scatter1_kernel(
    depth,
    index_in,
    q_hbm,
    own,
    kept,
    other,
    inverse,
    share,
    moment,
    near,
    given,
    parts,
    index,
    push,
    ring,
    load_sems,
    ring_sems,
    *sums,
):
    load = pltpu.make_async_copy(index_in, index, load_sems.at[0])
    load.start()

    def prepare():
        clear(sums)
        groups = own.shape[0] // SUBLANES
        grad_beta = jnp.zeros((1, LANES), F32)
        grad_gamma = jnp.zeros((1, LANES), F32)
        for i in range(SUBLANES):
            here = pl.ds(i, groups, stride=SUBLANES)
            rows = slice(i * groups, (i + 1) * groups)
            grad = own[rows, :] + kept[rows, :] + other[rows, :]
            push[here, :] = grad * inverse[here, :]
            weighted = grad * share[rows, :]
            given[rows, :] = weighted
            grad_beta = grad_beta + jnp.sum(weighted, axis=0, keepdims=True)
            grad_gamma = grad_gamma + jnp.sum(grad * moment[rows, :], axis=0, keepdims=True)
        parts[...] = jnp.concatenate([grad_beta, grad_gamma], axis=0)
        load.wait()

    scatter_loop(1, depth, index, q_hbm, ring, ring_sems, push, sums, prepare)

    def finish(start):
        here = pl.ds(SUBLANES + start, CHUNK)
        near[pl.ds(start, CHUNK), :] = tree([ref[here, :] for ref in sums], jnp.add)

    over(near.shape[0], CHUNK, finish, 2)


def last_kernel(
    sizes,
    depth,
    near1_in,
    given1_in,
    parts,
    x1_in,
    away_own1_in,
    away_all1_in,
    counts_in,
    scales1,
    mask,
    weight1,
    grad_own2_in,
    grad_near2_in,
    known1_in,
    from_own,
    from_near,
    norm1,
    whole1,
    whole2,
    near1,
    given1,
    x1,
    away_own1,
    away_all1,
    counts,
    grad_own2,
    grad_near2,
    known1,
    slots,
    flat1,
    flat2,
    pushed,
    arrived,
    halved1,
    halved2,
    landed1,
    landed2,
    reduced1,
    reduced2,
    all1,
    all2,
    small_sems,
    pair_sems,
    ring_sems,
    load_sems,
):
    cores, chips = sizes
    total = cores * chips
    points = given1.shape[0]
    cin = x1.shape[1]
    width1 = weight1.shape[0]
    core = lax.axis_index("points")
    chip = lax.axis_index("clouds")
    half = pl.multiple_of(core * points, points)
    barrier = pltpu.get_barrier_semaphore()
    signal_all(barrier, cores, total)
    loads = [
        pltpu.make_async_copy(source, target, load_sems.at[i])
        for i, (source, target) in enumerate(
            (
                (x1_in, x1),
                (near1_in, near1),
                (given1_in, given1),
                (known1_in, known1),
                (grad_own2_in, grad_own2),
                (grad_near2_in, grad_near2),
                (counts_in, counts),
                (away_all1_in, away_all1),
                (away_own1_in, away_own1),
            )
        )
    ]
    for copy in loads:
        copy.start()

    def chip_copy(d, source, target, use):
        return pltpu.make_async_remote_copy(
            src_ref=source,
            dst_ref=target,
            send_sem=ring_sems.at[0, use],
            recv_sem=ring_sems.at[1, use],
            device_id=(lax.rem(chip + d, chips), core),
            device_id_type=MESH,
        )

    class Summed:
        def __init__(self, flat, halved, landed, reduced, whole, first):
            self.flat, self.halved, self.landed = flat, halved, landed
            self.reduced, self.whole, self.first = reduced, whole, first
            self.swap = to_partner(flat.at[1 - core], halved, pair_sems, first)
            here = whole.at[core]
            self.back = to_partner(here, here, pair_sems, first + 1)

        def scatter(self):
            self.swap.wait()
            self.flat[core] += self.halved[...]
            self.landed[chip] = self.flat[core, chip]

            def send(d, carry):
                source = self.flat.at[core, lax.rem(chip + d, chips)]
                chip_copy(d, source, self.landed.at[chip], self.first).start()
                return carry

            lax.fori_loop(1, chips, send, 0)

        def wait(self, ref, use):
            others = ref.at[pl.ds(0, chips - 1)]
            arrival = chip_copy(1, others, others, use)
            arrival.wait_recv()
            arrival.wait_send()

        def spread(self, change):
            self.wait(self.landed, self.first)
            self.reduced[...] = change(slot_sum(self.landed, chips))
            self.whole[core, chip] = self.reduced[...]

            def send(d, carry):
                chip_copy(d, self.reduced, self.whole.at[core, chip], self.first + 1).start()
                return carry

            lax.fori_loop(1, chips, send, 0)

        def finish(self):
            self.wait(self.whole.at[core], self.first + 1)
            self.back.start()

    sum1 = Summed(flat1, halved1, landed1, reduced1, all1, 0)
    sum2 = Summed(flat2, halved2, landed2, reduced2, all2, 2)
    direct1 = weight1[:, :cin] - weight1[:, cin:]
    relative1 = weight1[:, cin:]
    slope = scales1[0:1, :]
    r1 = scales1[1:2, :]
    outer_scale = slope / scales1[2:3, :]

    pieces = [(n // chips, n % chips) for n in range(total)]
    size1 = -(-2 * cin // total)
    size2 = reduced2.shape[0]
    blocks2 = 4 * LANES // size2
    for copy in loads[:6]:
        copy.wait()

    def sums_of(count, base, values):
        def add(i, carry):
            start = pl.multiple_of(i * CHUNK, CHUNK)
            rows = pl.ds(start, CHUNK)
            return carry + t_by(x1[pl.ds(base + start, CHUNK), :], values[rows, :])

        return lax.fori_loop(0, count // CHUNK, add, jnp.zeros((cin, width1), F32))

    grad_own1 = sums_of(points, half, given1) * slope
    grad_near1 = sums_of(cores * points, 0, near1) * slope
    summed = [
        jnp.concatenate([grad_own1, grad_near1 - grad_own1], axis=0),
        known1[0],
        known1[1],
    ]
    flat1[...] = jnp.zeros(flat1.shape, F32)
    for n, (c, place) in enumerate(pieces):
        if n * size1 < 2 * cin:
            for i, value in enumerate(summed):
                flat1[c, place, i * size1 : (i + 1) * size1, :] = value[
                    n * size1 : (n + 1) * size1
                ]
    flat2[...] = jnp.zeros(flat2.shape, F32)
    for n, (c, place) in enumerate(pieces[:blocks2]):
        block, row = divmod(n * size2, LANES)
        columns = slice(block % 2 * LANES, (block % 2 + 1) * LANES)
        value = grad_own2[row : row + size2, columns]
        if block >= 2:
            value = grad_near2[row : row + size2, columns] - value
        flat2[c, place] = value

    pl.semaphore_wait(barrier, total - 1)
    sum1.swap.start()
    sum2.swap.start()
    gather_start(parts, slots, small_sems.at[0], small_sems.at[1], cores, total)
    sum1.scatter()
    sum2.scatter()
    for copy in loads[6:]:
        copy.wait()
    gather_wait(slots, small_sems.at[0], small_sems.at[1], total)
    sums = slot_sum(slots, total)
    norm1[...] = sums
    beta_scale = outer_scale * sums[0:1]
    gamma_scale = outer_scale * sums[1:2] * r1

    def corrected(value):
        main, gamma_part, beta_part = [
            value[i * size1 : (i + 1) * size1] for i in range(3)
        ]
        main = main - (gamma_part * gamma_scale + beta_part * beta_scale)
        if size1 == SUBLANES:
            return main
        return jnp.concatenate([main, jnp.zeros((SUBLANES - size1, LANES), F32)], axis=0)

    sum1.spread(corrected)
    sum2.spread(lambda value: value)
    for c in range(cores):

        def push(start):
            rows = pl.ds(c * points + start, CHUNK)
            value = near1[rows, :] * slope
            value = value - (counts[rows, :] * beta_scale + away_all1[rows, :] * gamma_scale)
            pushed[c, :, pl.ds(start, CHUNK)] = jnp.transpose(by(value, relative1))

        over(points, CHUNK, push, 2)
    swap = to_partner(pushed.at[1 - core], arrived, pair_sems, 4)
    swap.start()

    def own(start):
        rows = pl.ds(start, CHUNK)
        weights = jnp.broadcast_to(mask[:, rows].astype(F32), (SUBLANES, CHUNK))
        weights = jnp.transpose(weights)[:, :1]
        value = given1[rows, :] * slope
        value = value - (depth * weights * beta_scale + away_own1[rows, :] * gamma_scale)
        from_own[:, rows] = jnp.transpose(by(value, direct1)) + pushed[core, :, rows]

    over(points, CHUNK, own, 2)
    sum1.finish()
    sum2.finish()
    swap.wait()
    from_near[...] = arrived[...]
    sum1.back.wait()
    whole1[...] = all1[...]
    sum2.back.wait()
    whole2[...] = all2[...]


def finish_kernel(
    from_own,
    from_near,
    norm1,
    whole1,
    whole2,
    scales2,
    pooled_in,
    pooled,
    grad_features,
    grad_weight1,
    grad_gain1,
    grad_bias1,
    grad_weight2,
    grad_gain2,
    grad_bias2,
):
    pooled[...] = pooled_in[...]
    grad_features[...] = from_own[...] + from_near[...]
    cores, chips = whole1.shape[:2]
    cin = from_own.shape[0]
    size1 = -(-2 * cin // (cores * chips))
    rows1 = [whole1[n // chips, n % chips, 0:size1, :] for n in range(2 * cin // size1)]
    grad_weight1[...] = jnp.transpose(jnp.concatenate(rows1, axis=0))
    size2 = whole2.shape[2]
    grad_bias1[...] = norm1[0:1, :]
    grad_gain1[...] = norm1[1:2, :]
    for h in range(2):
        rows = slice(h * LANES, (h + 1) * LANES)
        for part in range(2):
            first = (2 * part + h) * LANES // size2
            block = [
                whole2[n // chips, n % chips] for n in range(first, first + LANES // size2)
            ]
            grad_weight2[rows, part * LANES : (part + 1) * LANES] = jnp.transpose(
                jnp.concatenate(block, axis=0)
            )
    grad_bias2[...] = scales2[1:2, :]
    grad_gain2[...] = scales2[2:3, :]


def shaped(*shape):
    return jax.ShapeDtypeStruct(shape, F32)


def scratch(*shape, dtype=F32):
    return pltpu.VMEM(shape, dtype)


def program(mesh):
    cores, chips = mesh.shape["points"], mesh.shape["clouds"]
    total = cores * chips

    def on_device(
        features,
        lengths,
        mask,
        neighbours,
        first_layer_weight,
        first_norm_gain,
        first_norm_bias,
        second_layer_weight,
        second_norm_gain,
        second_norm_bias,
        pooled_grad,
    ):
        cin, points = features.shape
        depth = neighbours.shape[0]
        width1, width2 = first_layer_weight.shape[0], second_layer_weight.shape[0]
        both = cores * points
        clouds = lengths.shape[0]
        mask_row = mask[None, :]
        groups1, groups2 = points // SUBLANES, points // 4

        def layout(subs, groups):
            place = jnp.arange(points, dtype=jnp.int32) // groups
            return (neighbours * subs + (SUBLANES - subs * place)).reshape(-1)

        index1, index2 = layout(1, groups1), layout(2, groups2)
        block = 32
        outs = pl.pallas_call(
            functools.partial(forward_kernel, (cores, total)),
            out_shape=[
                shaped(clouds, 2 * width2),
                shaped(groups1, depth, SUBLANES, LANES),
                shaped(groups2, depth, SUBLANES, LANES),
                shaped(points, width1),
                shaped(points, width1),
                shaped(points, width1),
                shaped(both, cin),
                shaped(points, width1),
                shaped(both, width1),
                shaped(both, LANES),
                shaped(both, width1),
                shaped(2 * points, LANES),
                shaped(both, width2),
                shaped(SUBLANES, width1),
                shaped(points, width1),
                shaped(width1, width2),
                shaped(SUBLANES, width2),
                shaped(2, 2 * cin, width1),
            ],
            in_specs=[VMEM] * 3 + [ANY] * 2 + [SMEM] + [VMEM] * 3 + [ANY] + [VMEM] * 3,
            out_specs=[VMEM] + [ANY] * 12 + [VMEM] * 5,
            scratch_shapes=[
                scratch(2 * points, LANES),
                scratch(both, width2),
                pltpu.SMEM((depth * points,), jnp.int32),
                pltpu.SMEM((depth * points,), jnp.int32),
                scratch(width2, 2 * width1),
                scratch(points, width1),
                scratch(points, width1),
                scratch(points, width1),
                scratch(both, cin),
                scratch(points, width1),
                scratch(both, width1),
                scratch(both, LANES),
                scratch(cores, cin, points),
                scratch(both, LANES, dtype=BF16),
                scratch(depth, LANES, LANES, dtype=BF16),
                scratch(both, points, dtype=BF16),
                scratch(SUBLANES, points),
                scratch(points, LANES),
                scratch(cores, 3 * cin, points, dtype=BF16),
                scratch(2 * width1, both, dtype=BF16),
                scratch(points, width1),
                scratch(both, width1),
                scratch(points, width1),
                scratch(both + 2 * SUBLANES, LANES),
                scratch(points, LANES),
                scratch(points, LANES),
                scratch(points, LANES),
                scratch(points, LANES),
                scratch(points, LANES),
                scratch(2 * both + 2 * SUBLANES, LANES),
                scratch(2 * points, LANES),
                scratch(2 * points, LANES),
                scratch(2 * points, LANES),
                scratch(2 * points, LANES),
                scratch(2 * points, LANES),
                scratch(both, width1),
                scratch(points, width2),
                scratch(both, width2),
                scratch(points, width2),
                scratch(points, 2 * width2, dtype=BF16),
                scratch(cores, 3 * clouds, SUBLANES, LANES),
                scratch(3, 4, LANES),
                scratch(3, total, 4, LANES),
                scratch(depth, SUBLANES, LANES),
                scratch(depth, SUBLANES, LANES),
                scratch(2, 2 * block, depth, SUBLANES, LANES),
                pltpu.SemaphoreType.DMA((2, 7)),
                pltpu.SemaphoreType.DMA((2, 3)),
                pltpu.SemaphoreType.DMA((2,)),
                pltpu.SemaphoreType.DMA((3,)),
                pltpu.SemaphoreType.DMA((10,)),
            ],
            compiler_params=pltpu.CompilerParams(
                collective_id=1, has_side_effects=True, vmem_limit_bytes=MEMORY
            ),
            name="forward",
        )(
            features,
            neighbours,
            mask_row,
            index1,
            index2,
            lengths,
            first_layer_weight,
            first_norm_gain[None, :],
            first_norm_bias[None, :],
            second_layer_weight,
            second_norm_gain[None, :],
            second_norm_bias[None, :],
            pooled_grad,
        )
        (
            pooled,
            q1,
            q2,
            inverse1,
            share1,
            moment1,
            x1,
            away_own1,
            away_all1,
            counts,
            x2,
            push2,
            extra2,
            scales1,
            own2,
            grad_own2,
            scales2,
            known1,
        ) = outs

        ring = scratch(3, block, depth, SUBLANES, LANES)
        kept, sent, grad_near2 = pl.pallas_call(
            functools.partial(scatter2_kernel, depth),
            out_shape=[shaped(points, width1), shaped(points, width1), shaped(width1, width2)],
            in_specs=[ANY] * 5 + [VMEM, ANY],
            out_specs=[VMEM] * 3,
            scratch_shapes=[
                pltpu.SMEM((depth * points,), jnp.int32),
                scratch(2 * points, LANES),
                scratch(both, width1),
                scratch(width2, 2 * width1),
                scratch(both, width2),
                ring,
                pltpu.SemaphoreType.DMA((5,)),
                pltpu.SemaphoreType.DMA((3,)),
            ]
            + [scratch(2 * both + 2 * SUBLANES, LANES)] * 12,
            compiler_params=pltpu.CompilerParams(vmem_limit_bytes=MEMORY),
            name="scatter2",
        )(index2, q2, push2, x2, second_layer_weight, scales2, extra2)
        other = lax.ppermute(sent, "points", [(0, 1), (1, 0)])

        near1, given1, parts = pl.pallas_call(
            functools.partial(scatter1_kernel, depth),
            out_shape=[shaped(both, width1), shaped(points, width1), shaped(2, width1)],
            in_specs=[ANY] * 2 + [VMEM] * 6,
            out_specs=[VMEM] * 3,
            scratch_shapes=[
                pltpu.SMEM((depth * points,), jnp.int32),
                scratch(points, width1),
                ring,
                pltpu.SemaphoreType.DMA((1,)),
                pltpu.SemaphoreType.DMA((3,)),
            ]
            + [scratch(both + 2 * SUBLANES, LANES)] * (SUBLANES * 2),
            compiler_params=pltpu.CompilerParams(vmem_limit_bytes=MEMORY),
            name="scatter1",
        )(index1, q1, own2, kept, other, inverse1, share1, moment1)

        size1 = -(-2 * cin // total)
        size2 = -(-4 * LANES // (total * SUBLANES)) * SUBLANES
        stacked1 = -(-3 * size1 // SUBLANES) * SUBLANES
        padded1 = -(-size1 // SUBLANES) * SUBLANES
        from_own, from_near, norm1, whole1, whole2 = pl.pallas_call(
            functools.partial(last_kernel, (cores, chips), depth),
            out_shape=[
                shaped(cin, points),
                shaped(cin, points),
                shaped(2, width1),
                shaped(cores, chips, padded1, LANES),
                shaped(cores, chips, size2, LANES),
            ],
            in_specs=[ANY] * 2 + [VMEM] + [ANY] * 4 + [VMEM] * 3 + [ANY] * 3,
            out_specs=[VMEM] * 5,
            scratch_shapes=[
                scratch(both, width1),
                scratch(points, width1),
                scratch(both, cin),
                scratch(points, width1),
                scratch(both, width1),
                scratch(both, LANES),
                scratch(width1, width2),
                scratch(width1, width2),
                scratch(2, 2 * cin, width1),
                scratch(total, 2, LANES),
                scratch(cores, chips, stacked1, LANES),
                scratch(cores, chips, size2, LANES),
                scratch(cores, cin, points),
                scratch(cin, points),
                scratch(chips, stacked1, LANES),
                scratch(chips, size2, LANES),
                scratch(chips, stacked1, LANES),
                scratch(chips, size2, LANES),
                scratch(padded1, LANES),
                scratch(size2, LANES),
                scratch(cores, chips, padded1, LANES),
                scratch(cores, chips, size2, LANES),
                pltpu.SemaphoreType.DMA((2,)),
                pltpu.SemaphoreType.DMA((2, 5)),
                pltpu.SemaphoreType.DMA((2, 4)),
                pltpu.SemaphoreType.DMA((9,)),
            ],
            compiler_params=pltpu.CompilerParams(
                collective_id=2, has_side_effects=True, vmem_limit_bytes=MEMORY
            ),
            name="last",
        )(
            near1,
            given1,
            parts,
            x1,
            away_own1,
            away_all1,
            counts,
            scales1,
            mask_row,
            first_layer_weight,
            grad_own2,
            grad_near2,
            known1,
        )
        outs = pl.pallas_call(
            finish_kernel,
            out_shape=[
                shaped(clouds, 2 * width2),
                shaped(cin, points),
                shaped(width1, 2 * cin),
                shaped(1, width1),
                shaped(1, width1),
                shaped(width2, 2 * width1),
                shaped(1, width2),
                shaped(1, width2),
            ],
            in_specs=[VMEM] * 7,
            out_specs=[VMEM] * 8,
            compiler_params=pltpu.CompilerParams(vmem_limit_bytes=MEMORY),
            name="finish",
        )(
            from_own,
            from_near,
            norm1,
            whole1,
            whole2,
            scales2,
            pooled,
        )
        return tuple(
            value.reshape(-1) if value.shape[0] == 1 else value for value in outs
        )

    return on_device


def solution(mesh):
    in_specs = (
        P(None, ("clouds", "points")),
        P("clouds"),
        P(("clouds", "points")),
        P(None, ("clouds", "points")),
        P(),
        P(),
        P(),
        P(),
        P(),
        P(),
        P("clouds", None),
    )
    out_specs = (P("clouds", None), P(None, ("clouds", "points")), P(), P(), P(), P(), P(), P())
    return jax.shard_map(
        program(mesh), mesh=mesh, in_specs=in_specs, out_specs=out_specs, check_vma=False
    )
```

```python
import functools
import math

import jax
import jax.numpy as jnp
from jax import lax
from jax.experimental import pallas as pl
from jax.experimental.pallas import tpu as pltpu
from jax.sharding import PartitionSpec as P

EPSILON = 1e-05
LOG2E = math.log2(math.e)
LN2 = math.log(2.0)
MESH = pl.DeviceIdType.MESH
F32 = jnp.float32
BF16 = jnp.bfloat16
LANES = 128
SUBLANES = 8
CHUNK = 256
MEMORY = 60 * 2**20
VMEM = pl.BlockSpec(memory_space=pltpu.VMEM)
SMEM = pl.BlockSpec(memory_space=pltpu.SMEM)
ANY = pl.BlockSpec(memory_space=pl.ANY)


def dot(left, right, dims):
    return lax.dot_general(
        left,
        right,
        (dims, ((), ())),
        precision=lax.Precision.HIGHEST,
        preferred_element_type=F32,
    )


def mm(left, right):
    return dot(left, right, ((1,), (0,)))


def mm_nt(left, right):
    return dot(left, right, ((1,), (1,)))


def mm_tn(left, right):
    return dot(left, right, ((0,), (0,)))


def mm_low(left, right):
    return lax.dot_general(
        left, right, (((1,), (0,)), ((), ())), preferred_element_type=F32
    )


def split(value):
    high = value.astype(BF16)
    low = (value - high.astype(F32)).astype(BF16)
    return high, low


def product(left, right, dims):
    def part(a, b):
        return lax.dot_general(a, b, (dims, ((), ())), preferred_element_type=F32)

    left_high, left_low = split(left)
    right_high, right_low = split(right)
    return part(left_high, right_high) + (part(left_high, right_low) + part(left_low, right_high))


def by(left, right):
    return product(left, right, ((1,), (0,)))


def by_t(left, right):
    return product(left, right, ((1,), (1,)))


def t_by(left, right):
    return product(left, right, ((0,), (0,)))


def thirds(value):
    high, rest = value.astype(BF16), value - value.astype(BF16).astype(F32)
    middle = rest.astype(BF16)
    return high, middle, (rest - middle.astype(F32)).astype(BF16)


def stacks(value, dim):
    high, middle, low = thirds(value)
    return [jnp.concatenate(parts, axis=dim) for parts in ((high, middle), (high, low))]


def weight_stacks(value, dim):
    high, middle, low = thirds(value)
    return [
        jnp.concatenate(parts, axis=dim)
        for parts in ((high, high), (middle, middle), (low, high))
    ]


def exact(left, right, dims):
    def part(a, b):
        return lax.dot_general(a, b, (dims, ((), ())), preferred_element_type=F32)

    return part(left[0], right[0]) + (part(left[0], right[1]) + part(left[1], right[2]))


def quad_stacks(value):
    high, middle, low = thirds(value)
    return [
        jnp.concatenate(parts, axis=0) for parts in ((high, high, middle, middle), (high, low))
    ]


def quad_weights(value):
    high, middle, low = thirds(value)
    return [
        jnp.concatenate(parts, axis=0) for parts in ((high, middle, high, middle), (low, high))
    ]


def exact_quad(left, right):
    def part(a, b):
        return lax.dot_general(a, b, (((0,), (0,)), ((), ())), preferred_element_type=F32)

    return part(left[0], right[0]) + part(left[1], right[1])


def over(count, step, body, times=1):
    def run(i, carry):
        for t in range(times):
            body(pl.multiple_of((i * times + t) * step, step))
        return carry

    lax.fori_loop(0, count // (step * times), run, 0)


def tree(values, join):
    values = list(values)
    while len(values) > 1:
        values = [
            join(values[i], values[i + 1]) if i + 1 < len(values) else values[i]
            for i in range(0, len(values), 2)
        ]
    return values[0]


def iota(shape, dim):
    return lax.broadcasted_iota(jnp.int32, shape, dim)


def signal_all(barrier, cores, total):
    me = lax.axis_index("clouds") * cores + lax.axis_index("points")

    def send(d, carry):
        t = lax.rem(me + d, total)
        pl.semaphore_signal(
            barrier,
            inc=1,
            device_id=(lax.div(t, cores), lax.rem(t, cores)),
            device_id_type=MESH,
        )
        return carry

    lax.fori_loop(1, total, send, 0)


def gather_start(own, slots, send_sem, recv_sem, cores, total):
    me = lax.axis_index("clouds") * cores + lax.axis_index("points")
    slots[me] = own[...]

    def send(d, carry):
        t = lax.rem(me + d, total)
        pltpu.make_async_remote_copy(
            src_ref=own,
            dst_ref=slots.at[me],
            send_sem=send_sem,
            recv_sem=recv_sem,
            device_id=(lax.div(t, cores), lax.rem(t, cores)),
            device_id_type=MESH,
        ).start()
        return carry

    lax.fori_loop(1, total, send, 0)


def gather_wait(slots, send_sem, recv_sem, total):
    others = slots.at[pl.ds(0, total - 1)]
    arrived = pltpu.make_async_remote_copy(
        src_ref=others,
        dst_ref=others,
        send_sem=send_sem,
        recv_sem=recv_sem,
        device_id=(lax.axis_index("clouds"), 1 - lax.axis_index("points")),
        device_id_type=MESH,
    )
    arrived.wait_recv()
    arrived.wait_send()


def slot_sum(slots, total):
    def add(i, carry):
        return carry + slots[i]

    return lax.fori_loop(1, total, add, slots[0])


def to_partner(source, target, sems, index):
    return pltpu.make_async_remote_copy(
        src_ref=source,
        dst_ref=target,
        send_sem=sems.at[0, index],
        recv_sem=sems.at[1, index],
        device_id=(lax.axis_index("clouds"), 1 - lax.axis_index("points")),
        device_id_type=MESH,
    )


def edge_pass(
    subs, block, depth, index, table, own_rows, out_hbm, held, ring, sems, outs, pending, after_block
):
    level_ref, share_ref, moment_ref, inverse_ref = outs
    per = SUBLANES // subs
    groups = own_rows.shape[0] // SUBLANES
    row = iota((SUBLANES, LANES), 0)
    mine = [(row >= subs * i) & (row < subs * (i + 1)) for i in range(per)]
    def fetch(group, slot):
        for k in range(depth):
            target = held[slot].at[k]
            for i in range(per):
                first = (k * per + i) * groups
                j = index.at[pl.ds(first, groups)][group]
                value = table[pl.ds(j, SUBLANES), :]
                if i == 0:
                    target[...] = value
                else:
                    pltpu.store(target, value, mask=mine[i])

    def work(group, slot, ring_slot, place):
        rows = pl.ds(pl.multiple_of(group * SUBLANES, SUBLANES), SUBLANES)
        peak = tree([held[slot][k] for k in range(depth)], jnp.maximum)
        top = own_rows[rows, :] + peak
        shift = jnp.maximum(top, 0.0)
        rest = jnp.maximum(jnp.exp2(-shift), 2.0**-100)
        under = jnp.maximum(jnp.minimum(top, 0.0), -100.0)
        offset = under - peak
        fifth = 0.2 * rest
        total, share, moment = [], [], []
        for k in range(depth):
            value = held[slot][k]
            power = value + offset
            grown = jnp.exp2(power)
            root = jnp.exp2((power - lax.log2(rest + grown)) * 0.2)
            weight = root * (fifth + grown)
            ring[ring_slot, place, k] = weight
            total.append(root)
            share.append(weight)
            moment.append(weight * value)
        total, share, moment = [
            functools.reduce(jnp.add, parts) for parts in (total, share, moment)
        ]
        mass = share + (0.8 * rest) * total
        inverse = 1.0 / mass
        level = 0.2 * (top - under) + 0.8 * shift + lax.log2(mass)
        level_ref[rows, :] = LN2 * level - math.log(depth)
        inverse_ref[rows, :] = inverse
        share_ref[rows, :] = share * inverse
        moment_ref[rows, :] = moment * inverse

    blocks = groups // block

    def push(b, slot):
        return pltpu.make_async_copy(
            ring.at[slot, pl.ds(0, block)], out_hbm.at[pl.ds(b * block, block)], sems.at[slot]
        )

    fetch(0, 0)

    def one_block(b, carry):
        ring_slot = lax.rem(b, 2)

        if pending is None:

            @pl.when(b >= 2)
            def _():
                push(b - 2, ring_slot).wait()

        else:

            @pl.when(b < 2)
            def _():
                pending(ring_slot).wait()

            @pl.when(b >= 2)
            def _():
                push(b - 2, ring_slot).wait()

        def several(t, inner):
            for unit in range(4):
                slot = unit % 2
                place = t * 4 + unit
                group = b * block + place
                work(group, slot, ring_slot, place)
                fetch(jnp.minimum(group + 1, groups - 1), 1 - slot)
            return inner

        lax.fori_loop(0, block // 4, several, 0)
        push(b, ring_slot).start()
        if after_block is not None:
            after_block(b)
        return carry

    lax.fori_loop(0, blocks, one_block, 0)
    return lambda slot: push(blocks - 2 + slot, slot)


def lanes_to_rows(value, width):
    return [value[:, i * LANES : (i + 1) * LANES] for i in range(width // LANES)]


def rows_to_lanes(rows):
    return rows[0] if len(rows) == 1 else jnp.concatenate(rows, axis=1)


def forward_kernel(
    sizes,
    feat,
    near,
    mask,
    index1_in,
    index2_in,
    lengths,
    weight1,
    gain1,
    bias1,
    weight2_in,
    gain2,
    bias2,
    pooled_grad,
    pooled,
    q1,
    q2,
    inverse1_out,
    share1_out,
    moment1_out,
    x1_out,
    away_own1_out,
    away_all1_out,
    counts_out,
    x2_out,
    push2_out,
    extra2_out,
    scales1,
    own2,
    grad_own2,
    scales2,
    known1,
    push2,
    extra2,
    index1,
    index2,
    weight2,
    inverse1,
    share1,
    moment1,
    x1,
    away_own1,
    away_all1,
    counts,
    x1_cm,
    tallies,
    lows,
    links,
    live,
    live_col,
    parts1,
    parts2,
    u1,
    v1,
    g1,
    table1,
    own_rows1,
    level1,
    other1,
    share_rows1,
    moment_rows1,
    table2,
    own_rows2,
    level2,
    share2,
    moment2,
    inverse2,
    x2,
    u2,
    v2,
    g2,
    u_parts,
    pool_parts,
    message,
    slots,
    held0,
    held1,
    ring,
    pair_sems,
    all_sems,
    ring_sems,
    load_sems,
    store_sems,
):
    cores, total = sizes
    points = feat.shape[1]
    cin = feat.shape[0]
    both = cores * points
    depth = near.shape[0]
    width1 = weight1.shape[0]
    width2 = gain2.shape[1]
    groups1, groups2 = points // SUBLANES, 2 * points // SUBLANES
    core = lax.axis_index("points")
    half = pl.multiple_of(core * points, points)
    barrier = pltpu.get_barrier_semaphore()
    signal_all(barrier, cores, total)
    loads = [
        pltpu.make_async_copy(source, target, load_sems.at[i])
        for i, (source, target) in enumerate(
            ((index1_in, index1), (index2_in, index2), (weight2_in, weight2))
        )
    ]
    for copy in loads:
        copy.start()
    late = [
        pltpu.make_async_copy(source, target, store_sems.at[8 + i])
        for i, (source, target) in enumerate(((push2, push2_out), (extra2, extra2_out)))
    ]
    stores = [
        pltpu.make_async_copy(source, target, store_sems.at[i])
        for i, (source, target) in enumerate(
            (
                (x1, x1_out),
                (counts, counts_out),
                (away_own1, away_own1_out),
                (away_all1, away_all1_out),
                (inverse1, inverse1_out),
                (share1, share1_out),
                (moment1, moment1_out),
                (x2, x2_out),
            )
        )
    ]

    live[...] = jnp.broadcast_to(mask[...].astype(F32), live.shape)
    row16 = iota((16, LANES), 0)
    one, none = jnp.ones((16, LANES), BF16), jnp.zeros((16, LANES), BF16)

    def build(columns, first):
        high_names, low_names = [], []
        for k in range(depth):
            name = near[k : k + 1, columns]
            high = jnp.where(mask[:, columns] > 0, lax.shift_right_logical(name, 7), -1)
            for names, value in ((high_names, high), (low_names, name & (LANES - 1))):
                names.append(jnp.broadcast_to(value, (16, LANES)).astype(jnp.int16))
        for s in range(0, LANES, 16):
            target = (row16 + s).astype(jnp.int16)
            for k in range(depth):
                lows[k, s : s + 16, :] = jnp.where(low_names[k] == target, one, none)

        def one_high(start):
            target = jnp.full((16, LANES), lax.shift_right_logical(start, 7), jnp.int32)
            target = target.astype(jnp.int16)
            meant = [jnp.where(name == target, one, none) for name in high_names]
            for s in range(0, LANES, 16):
                found = tree([meant[k] * lows[k, s : s + 16, :] for k in range(depth)], jnp.add)
                here = pl.ds(start + s, 16)
                links[here, columns] = found
                tallies[here, :] = found if first else tallies[here, :] + found

        over(both, LANES, one_high)

    tiles = points // LANES
    early = tiles - tiles // 4
    for tile in range(early):
        build(pl.ds(tile * LANES, LANES), tile == 0)
    x1_cm[core] = feat[...]
    pl.semaphore_wait(barrier, total - 1)
    swap = to_partner(feat, x1_cm.at[core], pair_sems, 0)
    swap.start()
    for tile in range(early, tiles):
        build(pl.ds(tile * LANES, LANES), tile == 0)
    live_col[...] = jnp.broadcast_to(jnp.transpose(live[...])[:, :1], live_col.shape)
    swap.wait()

    direct1 = weight1[:, :cin] - weight1[:, cin:]
    relative1 = weight1[:, cin:]
    for c in range(cores):

        def turn(start):
            x1[pl.ds(c * points + start, CHUNK), :] = jnp.transpose(
                x1_cm[c, :, pl.ds(start, CHUNK)]
            )

        over(points, CHUNK, turn, 2)
        value = x1_cm[c]
        high, low = split(value)
        lower = (value - high.astype(F32) - low.astype(F32)).astype(BF16)
        parts1[c, 0:cin, :] = high
        parts1[c, cin : 2 * cin, :] = low
        parts1[c, 2 * cin : 3 * cin, :] = lower

    direct_parts1 = quad_weights(jnp.transpose(direct1))
    relative_parts1 = quad_weights(jnp.transpose(relative1))

    def sums_near1(start):
        columns = pl.ds(start, CHUNK)
        value = mm_low(parts1[0], links[0:points, columns])
        for c in range(1, cores):
            value = value + mm_low(parts1[c], links[c * points : (c + 1) * points, columns])
        value = value[0:cin] + value[cin : 2 * cin] + value[2 * cin : 3 * cin]
        g1[columns, :] = exact_quad(quad_stacks(value), relative_parts1)

    over(points, CHUNK, sums_near1, 2)

    stores[0].start()
    ones = jnp.ones((LANES, LANES), BF16)

    def count_links(start):
        rows = pl.ds(start, CHUNK)
        counts[rows, :] = mm_low(tallies[rows, :], ones)

    over(both, CHUNK, count_links, 4)
    stores[1].start()

    live_sum = jnp.sum(live[0:1, :], axis=1, keepdims=True)
    mine = live_sum * depth

    def fold(count, size, body, state):
        def several(i, carry):
            for t in range(2):
                carry = body(pl.multiple_of((i * 2 + t) * size, size), carry)
            return carry

        return lax.fori_loop(0, count // (2 * size), several, state)

    def column_sum(value):
        rows = [value[s : s + SUBLANES] for s in range(0, value.shape[0], SUBLANES)]
        return tree(rows, jnp.add)

    def statistics(u, v, g, width):
        per = width // LANES
        zeros = jnp.zeros((SUBLANES, width), F32)

        def first(start, carry):
            rows = pl.ds(start, CHUNK)
            weights = rows_to_lanes([live_col[rows, :]] * per)
            return carry[0] + column_sum(weights * u[rows, :]), carry[1] + column_sum(g[rows, :])

        u_sum, g_sum = fold(points, CHUNK, first, (zeros, zeros))
        u_sum = jnp.sum(u_sum, axis=0, keepdims=True)
        g_sum = jnp.sum(g_sum, axis=0, keepdims=True)
        u_mean = u_sum / live_sum
        v_mean = g_sum / mine

        def second(start, carry):
            rows = pl.ds(start, CHUNK)
            weights = rows_to_lanes([live_col[rows, :]] * per)
            centred = weights * (u[rows, :] - u_mean)
            spread = depth * centred + 2.0 * (g[rows, :] - depth * v_mean)
            return carry + column_sum(centred * spread)

        def third(start, carry):
            rows = pl.ds(start, CHUNK)
            away = v[rows, :] - v_mean
            weights = rows_to_lanes([counts[rows, :]] * per)
            return carry + column_sum(weights * away * away)

        square = fold(points, CHUNK, second, zeros)
        square = fold(both, CHUNK, third, square)
        square = jnp.sum(square, axis=0, keepdims=True)
        return depth * u_sum + g_sum, square, u_mean, v_mean

    for c in range(cores):

        def outer(start):
            left = quad_stacks(x1_cm[c, :, pl.ds(start, CHUNK)])
            v1[pl.ds(c * points + start, CHUNK), :] = exact_quad(left, relative_parts1)

        over(points, CHUNK, outer, 2)

    def inner(start):
        rows = pl.ds(start, CHUNK)
        u1[rows, :] = exact_quad(quad_stacks(x1_cm[core, :, rows]), direct_parts1)

    over(points, CHUNK, inner, 2)

    def send_sums(use, rows):
        for i, value in enumerate(rows):
            message[use, i : i + 1, :] = value
        gather_start(
            message.at[use], slots.at[use], all_sems.at[0, use], all_sems.at[1, use], cores, total
        )

    def receive(use):
        gather_wait(slots.at[use], all_sems.at[0, use], all_sems.at[1, use], total)

    def combine(use, numbers, width):
        per = width // LANES
        count = numbers[0]
        for value in numbers[1:]:
            count = count + value

        def value_of(i, first):
            return rows_to_lanes([slots[use, i, first + h : first + h + 1, :] for h in range(per)])

        mean = value_of(0, 0)
        for i in range(1, total):
            mean = mean + value_of(i, 0)
        mean = mean / count
        square = None
        for i in range(total):
            gap = value_of(i, 0) / numbers[i] - mean
            term = value_of(i, per) + numbers[i] * gap * gap
            square = term if square is None else square + term
        return count, mean, square / count

    sums, square, u_mean1, v_mean1 = statistics(u1, v1, g1, width1)
    send_sums(0, [sums, square, jnp.broadcast_to(mine, (1, LANES)), jnp.zeros((1, LANES), F32)])

    for part, value in enumerate(split(u1[...] - u_mean1)):
        u_parts[:, part * LANES : (part + 1) * LANES] = value

    def shared1(start):
        rows = pl.ds(start, CHUNK)
        value = mm_low(links[rows, :], u_parts[:, 0 : 2 * LANES])
        away_all1[rows, :] = value[:, :LANES] + value[:, LANES:]

    over(both, CHUNK, shared1, 2)
    receive(0)
    numbers = [slots[0, i, 2:3, 0:1] for i in range(total)]
    count, mean1, variance1 = combine(0, numbers, width1)
    r1 = lax.rsqrt(variance1 + EPSILON)
    slope1 = gain1[...] * r1
    scales1[...] = jnp.concatenate(
        [slope1, r1, jnp.broadcast_to(count, (1, LANES)), jnp.zeros((5, LANES), F32)], axis=0
    )

    def fill1(start):
        rows = pl.ds(start, CHUNK)
        table1[pl.ds(SUBLANES + start, CHUNK), :] = (v1[rows, :] - v_mean1) * (slope1 * LOG2E)

    over(both, CHUNK, fill1, 2)

    def fill_own1(start):
        rows = pl.ds(start, CHUNK)
        value = (u1[rows, :] - (mean1 - v_mean1)) * (slope1 * LOG2E) + bias1[...] * LOG2E
        for s in range(0, CHUNK, groups1):
            here = pl.ds(lax.div(start, groups1) + s // groups1, groups1, stride=SUBLANES)
            own_rows1[here, :] = value[s : s + groups1]

    over(points, CHUNK, fill_own1, 2)

    loads[0].wait()
    block1, block2 = groups1 // 4, ring.shape[1]
    block_rows = block1 * SUBLANES
    blocks1 = 4

    def hand_over(b):
        rows = pl.ds(pl.multiple_of(b * block_rows, block_rows), block_rows)
        return to_partner(level1.at[rows], other1.at[rows], pair_sems, 3 + b)

    pending = edge_pass(
        1,
        block1,
        depth,
        index1,
        table1,
        own_rows1,
        q1,
        (held0, held1),
        ring,
        ring_sems,
        (level1, share_rows1, moment_rows1, inverse1),
        None,
        lambda b: hand_over(b).start(),
    )

    for i in range(SUBLANES):
        here = pl.ds(i, groups1, stride=SUBLANES)
        x2[pl.ds(half + i * groups1, groups1), :] = level1[here, :]
    loads[1].wait()
    loads[2].wait()
    direct2 = weight2[:, :width1] - weight2[:, width1:]
    relative2 = weight2[:, width1:]
    direct_parts2 = weight_stacks(direct2, 1)
    relative_parts2 = weight_stacks(relative2, 1)
    other_half = pl.multiple_of((1 - core) * points, points)

    def outer2(base):
        def chunk(start):
            rows = pl.ds(base + start, CHUNK)
            value = x2[rows, :]
            high, low = split(jnp.transpose(value))
            parts2[0:width1, rows] = high
            parts2[width1 : 2 * width1, rows] = low
            v2[rows, :] = exact(stacks(value, 1), relative_parts2, ((1,), (1,)))

        over(points, CHUNK, chunk, 2)

    def inner2(start):
        left = stacks(x2[pl.ds(half + start, CHUNK), :], 1)
        u2[pl.ds(start, CHUNK), :] = exact(left, direct_parts2, ((1,), (1,)))

    over(points, CHUNK, inner2, 2)
    outer2(half)
    for b in range(blocks1):
        hand_over(b).wait()
    for i in range(SUBLANES):
        here = pl.ds(i, groups1, stride=SUBLANES)
        x2[pl.ds(other_half + i * groups1, groups1), :] = other1[here, :]
    stores[7].start()
    outer2(other_half)

    def sums_near2(start):
        columns = pl.ds(start, CHUNK)
        value = mm_low(parts2[...], links[:, columns])
        value = value[0:width1] + value[width1 : 2 * width1]
        g2[columns, :] = exact(stacks(jnp.transpose(value), 1), relative_parts2, ((1,), (1,)))

    over(points, CHUNK, sums_near2, 2)

    sums, square, u_mean2, v_mean2 = statistics(u2, v2, g2, width2)
    send_sums(1, lanes_to_rows(sums, width2) + lanes_to_rows(square, width2))
    for part, value in enumerate(split(u2[...] - u_mean2)):
        u_parts[:, part * width2 : (part + 1) * width2] = value

    def shared2(start):
        rows = pl.ds(start, CHUNK)
        extra2[rows, :] = mm_low(links[rows, :], u_parts[:, 0:width2]) + mm_low(
            links[rows, :], u_parts[:, width2:]
        )

    over(both, CHUNK, shared2, 2)

    def away1(start):
        rows = pl.ds(start, CHUNK)
        away_all1[rows, :] += counts[rows, :] * (v1[rows, :] - (mean1 - u_mean1))

    over(both, CHUNK, away1, 2)
    inverse_gain1 = 1.0 / (gain1[...] * LOG2E)
    for i in range(SUBLANES):
        here = pl.ds(i, groups1, stride=SUBLANES)
        rows = slice(i * groups1, (i + 1) * groups1)
        offset = own_rows1[here, :] - bias1[...] * LOG2E
        moment1[rows, :] = (share_rows1[here, :] * offset + moment_rows1[here, :]) * inverse_gain1
        share1[rows, :] = share_rows1[here, :]
        away_own1[rows, :] = depth * live_col[rows, :] * (u1[rows, :] - mean1) + g1[rows, :]
    for copy in stores[2:7]:
        copy.start()
    receive(1)
    count, mean2, variance2 = combine(1, numbers, width2)
    r2 = lax.rsqrt(variance2 + EPSILON)
    slope2 = gain2[...] * r2
    scales2[...] = jnp.concatenate([slope2, jnp.zeros((7, width2), F32)], axis=0)

    def fill2(start):
        rows = pl.ds(start, CHUNK)
        value = (v2[rows, :] - v_mean2) * (slope2 * LOG2E)
        for h in range(2):
            table2[pl.ds(SUBLANES + 2 * start + h, CHUNK, stride=2), :] = value[
                :, h * LANES : (h + 1) * LANES
            ]

    over(both, CHUNK, fill2, 2)

    for i in range(SUBLANES // 2):
        rows = slice(i * groups2, (i + 1) * groups2)
        value = (u2[rows, :] - (mean2 - v_mean2)) * (slope2 * LOG2E) + bias2[...] * LOG2E
        for h in range(2):
            own_rows2[pl.ds(2 * i + h, groups2, stride=SUBLANES), :] = value[
                :, h * LANES : (h + 1) * LANES
            ]

    pending = edge_pass(
        2,
        block2,
        depth,
        index2,
        table2,
        own_rows2,
        q2,
        (held0, held1),
        ring,
        ring_sems,
        (level2, share2, moment2, inverse2),
        pending,
        None,
    )

    clouds = pooled_grad.shape[0]
    ends = [lengths[0]]
    for q in range(1, clouds):
        ends.append(ends[-1] + lengths[q])
    row = iota((SUBLANES, LANES), 0)
    odd = lax.rem(row, 2) == 1
    point_of_row = half + lax.div(row, 2) * groups2
    steps = level2.shape[0] // SUBLANES
    lowest = jnp.full((SUBLANES, LANES), -1e30, F32)
    zero = jnp.zeros((SUBLANES, LANES), F32)

    def past(t):
        position = point_of_row + t
        return [position >= ends[q] for q in range(clouds - 1)]

    def pick(after, values):
        value = values[0]
        for q in range(1, clouds):
            value = jnp.where(after[q - 1], values[q], value)
        return value

    def apart(after, value, none):
        out = []
        for q in range(clouds):
            kept = value if q == 0 else jnp.where(after[q - 1], value, none)
            out.append(kept if q == clouds - 1 else jnp.where(after[q], none, kept))
        return out

    def step_rows(t):
        return pl.ds(pl.multiple_of(t * SUBLANES, SUBLANES), SUBLANES)

    def by_parity(value, join):
        value = join(value, pltpu.roll(value, 2, 0))
        return join(value, pltpu.roll(value, 4, 0))

    def unrolled(body, state, times):
        def several(i, carry):
            for u in range(times):
                carry = body(i * times + u, carry)
            return carry

        return lax.fori_loop(0, steps // times, several, state)

    def peaks(t, carry):
        value = level2[step_rows(t), :]
        after = past(t)
        tops = [jnp.maximum(a, b) for a, b in zip(carry, apart(after, value, lowest))]
        adds = [a + b for a, b in zip(carry[clouds:], apart(after, value, zero))]
        return tuple(tops + adds)

    state = unrolled(peaks, (lowest,) * clouds + (zero,) * clouds, 8)
    peak = [by_parity(value, jnp.maximum) for value in state[:clouds]]
    sums = [by_parity(value, jnp.add) for value in state[clouds:]]

    def masses(t, carry):
        after = past(t)
        value = jnp.exp(level2[step_rows(t), :] - pick(after, peak))
        return tuple(a + b for a, b in zip(carry, apart(after, value, zero)))

    state = unrolled(masses, (zero,) * clouds, 8)
    mass = [by_parity(value, jnp.add) for value in state]
    for q in range(clouds):
        pool_parts[core, 3 * q] = peak[q]
        pool_parts[core, 3 * q + 1] = mass[q]
        pool_parts[core, 3 * q + 2] = sums[q]
    here = pool_parts.at[core]
    swap = to_partner(here, here, pair_sems, 2)
    swap.start()
    swap.wait()

    level, grad_level, grad_mean = [], [], []
    for q in range(clouds):
        top = pool_parts[0, 3 * q]
        for c in range(1, cores):
            top = jnp.maximum(top, pool_parts[c, 3 * q])
        whole, sum_all = zero, zero
        for c in range(cores):
            whole = whole + pool_parts[c, 3 * q + 1] * jnp.exp(pool_parts[c, 3 * q] - top)
            sum_all = sum_all + pool_parts[c, 3 * q + 2]
        level.append(top + jnp.log(whole))
        size = jnp.full((SUBLANES, LANES), lengths[q].astype(F32), F32)
        first = level[q] - jnp.log(size)
        second = sum_all / size
        for h in range(2):
            pooled[q : q + 1, h * LANES : (h + 1) * LANES] = first[h : h + 1]
            pooled[q : q + 1, (2 + h) * LANES : (3 + h) * LANES] = second[h : h + 1]
        given = [pooled_grad[q : q + 1, h * LANES : (h + 1) * LANES] for h in range(4)]
        grad_level.append(jnp.where(odd, given[1], given[0]))
        grad_mean.append(jnp.where(odd, given[3], given[2]) / size)

    slope_rows, bias_rows = [], []
    for ref_value, target in ((gain2[...], slope_rows), (bias2[...], bias_rows)):
        low_half, high_half = lanes_to_rows(ref_value * LOG2E, width2)
        target.append(jnp.where(odd, high_half, low_half))
    inverse_gain = 1.0 / slope_rows[0]
    bias_row = bias_rows[0]

    def gradient(t, carry):
        rows = step_rows(t)
        after = past(t)
        value = pick(after, grad_level) * jnp.exp(level2[rows, :] - pick(after, level))
        value = value + pick(after, grad_mean)
        push2[rows, :] = value * inverse2[rows, :]
        share = share2[rows, :]
        moment = (share * (own_rows2[rows, :] - bias_row) + moment2[rows, :]) * inverse_gain
        given = value * share
        share2[rows, :] = given
        return carry[0] + given, carry[1] + value * moment

    state = unrolled(gradient, (zero, zero), 8)
    grad_beta, grad_gamma = [by_parity(value, jnp.add) for value in state]
    late[0].start()
    send_sums(2, [grad_beta[0:1], grad_beta[1:2], grad_gamma[0:1], grad_gamma[1:2]])

    known1[...] = jnp.zeros(known1.shape, F32)

    def known(start):
        near_rows = pl.ds(start, CHUNK)
        known1[0, cin:, :] += t_by(x1[near_rows, :], away_all1[near_rows, :])
        known1[1, cin:, :] += t_by(x1[near_rows, :], counts[near_rows, :])

    over(both, CHUNK, known, 2)

    def known_own(start):
        rows = pl.ds(start, CHUNK)
        here = x1[pl.ds(half + start, CHUNK), :]
        known1[0, 0:cin, :] += t_by(here, away_own1[rows, :])
        known1[1, 0:cin, :] += t_by(here, depth * live_col[rows, :])

    over(points, CHUNK, known_own, 2)
    for i in range(2):
        known1[i, cin:, :] -= known1[i, 0:cin, :]

    main = jnp.zeros(grad_own2.shape, F32)
    away_sum = jnp.zeros(grad_own2.shape, F32)
    live_x = jnp.zeros((width1, LANES), F32)
    for i in range(SUBLANES // 2):
        rows = slice(i * groups2, (i + 1) * groups2)
        here = x2[pl.ds(half + i * groups2, groups2), :]
        weights = rows_to_lanes([live_col[rows, :]] * 2)
        u2[rows, :] = depth * weights * (u2[rows, :] - mean2) + g2[rows, :]
        given = rows_to_lanes(
            [share2[pl.ds(2 * i + h, groups2, stride=SUBLANES), :] for h in range(2)]
        )
        g2[rows, :] = given * slope2
        main = main + t_by(here, g2[rows, :])
        away_sum = away_sum + t_by(here, u2[rows, :])
        live_x = live_x + t_by(here, depth * live_col[rows, :])
    receive(2)
    sums = slot_sum(slots.at[2], total)
    grad_beta = rows_to_lanes([sums[0:1], sums[1:2]])
    grad_gamma = rows_to_lanes([sums[2:3], sums[3:4]])
    scales2[1:2, :] = grad_beta
    scales2[2:3, :] = grad_gamma
    outer_scale = slope2 / count
    gamma_scale = outer_scale * grad_gamma * r2
    beta_scale = outer_scale * grad_beta

    def extra(start):
        rows = pl.ds(start, CHUNK)
        weights = rows_to_lanes([counts[rows, :]] * 2)
        away = extra2[rows, :] + weights * (v2[rows, :] - (mean2 - u_mean2))
        extra2[rows, :] = weights * beta_scale + away * gamma_scale

    over(both, CHUNK, extra, 2)
    late[1].start()
    grad_own2[...] = main - (
        rows_to_lanes([live_x] * 2) * beta_scale + away_sum * gamma_scale
    )

    def own(start):
        rows = pl.ds(start, CHUNK)
        weights = rows_to_lanes([live_col[rows, :]] * 2)
        value = g2[rows, :] - (depth * weights * beta_scale + u2[rows, :] * gamma_scale)
        own2[rows, :] = by(value, direct2)

    over(points, CHUNK, own, 2)
    for copy in stores + late + [pending(0), pending(1)]:
        copy.wait()


def scatter_loop(subs, depth, index, q_hbm, ring, sems, push, sums, clear):
    per = SUBLANES // subs
    groups = q_hbm.shape[0]
    slots, block = ring.shape[0], ring.shape[1]
    blocks = groups // block
    row = iota((SUBLANES, LANES), 0)
    mine = [(row >= subs * i) & (row < subs * (i + 1)) for i in range(per)]
    ways = len(sums) // per

    def pull(b):
        slot = lax.rem(b, slots)
        return pltpu.make_async_copy(
            q_hbm.at[pl.ds(b * block, block)], ring.at[slot], sems.at[slot]
        )

    for b in range(slots - 1):
        pull(b).start()
    clear()

    def one_block(b, carry):
        @pl.when(b + slots - 1 < blocks)
        def _():
            pull(b + slots - 1).start()

        pull(b).wait()
        slot = lax.rem(b, slots)

        def one_group(place, inner):
            group = b * block + place
            rows = pl.ds(pl.multiple_of(group * SUBLANES, SUBLANES), SUBLANES)
            given = push[rows, :]

            for k in range(depth):
                value = ring[slot, place, k] * given
                for i in range(per):
                    j = index.at[pl.ds((k * per + i) * groups, groups)][group]
                    target = sums[i * ways + k % ways].at[pl.ds(j, SUBLANES), :]
                    pltpu.store(target, target[...] + value, mask=mine[i])
            return inner

        lax.fori_loop(0, block, one_group, 0)
        return carry

    lax.fori_loop(0, blocks, one_block, 0)


def clear(sums):
    rows = sums[0].shape[0]
    zero = jnp.zeros((SUBLANES, LANES), F32)

    def rows32(start):
        for ref in sums:
            for s in range(0, 4 * SUBLANES, SUBLANES):
                ref[pl.ds(start + s, SUBLANES), :] = zero

    over(rows, 4 * SUBLANES, rows32)
    for s in range(rows // 32 * 32, rows, SUBLANES):
        for ref in sums:
            ref[s : s + SUBLANES, :] = zero


def scatter2_kernel(
    depth,
    index_in,
    q_hbm,
    push_in,
    x2_in,
    weight_in,
    scales,
    extra_in,
    kept,
    sent,
    grad_near,
    index,
    push,
    x2,
    weight,
    extra,
    ring,
    load_sems,
    ring_sems,
    *sums,
):
    loads = [
        pltpu.make_async_copy(source, target, load_sems.at[i])
        for i, (source, target) in enumerate(
            ((index_in, index), (push_in, push), (x2_in, x2), (weight_in, weight), (extra_in, extra))
        )
    ]

    def prepare():
        for copy in loads[2:]:
            copy.start()
        clear(sums)
        loads[0].wait()
        loads[1].wait()

    for copy in loads[:2]:
        copy.start()
    scatter_loop(2, depth, index, q_hbm, ring, ring_sems, push, sums, prepare)
    for copy in loads[2:]:
        copy.wait()
    points, width = kept.shape
    relative = weight[:, width:]
    core = lax.axis_index("points")
    grad_near[...] = jnp.zeros(grad_near.shape, F32)
    for part, out in ((1 - core, sent), (core, kept)):

        def finish(start):
            first = pl.multiple_of(part * points + start, CHUNK)
            rows = pl.ds(first, CHUNK)
            halves = []
            for h in range(2):
                here = pl.ds(SUBLANES + 2 * first + h, CHUNK, stride=2)
                halves.append(tree([ref[here, :] for ref in sums], jnp.add))
            value = rows_to_lanes(halves) * scales[0:1, :] - extra[rows, :]
            out[pl.ds(start, CHUNK), :] = by(value, relative)
            grad_near[...] += t_by(x2[rows, :], value)

        over(points, CHUNK, finish, 2)


def scatter1_kernel(
    depth,
    index_in,
    q_hbm,
    own,
    kept,
    other,
    inverse,
    share,
    moment,
    near_out,
    given_out,
    parts,
    near,
    given,
    index,
    push,
    ring,
    load_sems,
    ring_sems,
    store_sems,
    *sums,
):
    load = pltpu.make_async_copy(index_in, index, load_sems.at[0])
    load.start()
    quarter = near.shape[0] // 4
    stores = [pltpu.make_async_copy(given, given_out, store_sems.at[0])]
    for i in range(4):
        rows = pl.ds(i * quarter, quarter)
        stores.append(
            pltpu.make_async_copy(near.at[rows], near_out.at[rows], store_sems.at[1 + i])
        )

    def prepare():
        clear(sums)
        groups = own.shape[0] // SUBLANES
        grad_beta = jnp.zeros((1, LANES), F32)
        grad_gamma = jnp.zeros((1, LANES), F32)
        for i in range(SUBLANES):
            here = pl.ds(i, groups, stride=SUBLANES)
            rows = slice(i * groups, (i + 1) * groups)
            grad = own[rows, :] + kept[rows, :] + other[rows, :]
            push[here, :] = grad * inverse[here, :]
            weighted = grad * share[rows, :]
            given[rows, :] = weighted
            grad_beta = grad_beta + jnp.sum(weighted, axis=0, keepdims=True)
            grad_gamma = grad_gamma + jnp.sum(grad * moment[rows, :], axis=0, keepdims=True)
        parts[...] = jnp.concatenate([grad_beta, grad_gamma], axis=0)
        stores[0].start()
        load.wait()

    scatter_loop(1, depth, index, q_hbm, ring, ring_sems, push, sums, prepare)

    for i in range(4):

        def finish(start):
            first = i * quarter + start
            here = pl.ds(SUBLANES + first, CHUNK)
            near[pl.ds(first, CHUNK), :] = tree([ref[here, :] for ref in sums], jnp.add)

        over(quarter, CHUNK, finish)
        stores[1 + i].start()
    for copy in stores:
        copy.wait()


def last_kernel(
    sizes,
    depth,
    near1_in,
    given1_in,
    parts,
    x1_in,
    away_own1_in,
    away_all1_in,
    counts_in,
    scales1,
    mask,
    weight1,
    grad_own2_in,
    grad_near2_in,
    known1_in,
    from_own,
    norm1,
    whole1,
    whole2,
    near1,
    given1,
    x1,
    away_own1,
    away_all1,
    counts,
    grad_own2,
    grad_near2,
    known1,
    slots,
    flat1,
    flat2,
    pushed,
    arrived,
    halved1,
    halved2,
    landed1,
    landed2,
    reduced1,
    reduced2,
    all1,
    all2,
    small_sems,
    pair_sems,
    ring_sems,
    load_sems,
):
    cores, chips = sizes
    total = cores * chips
    points = given1.shape[0]
    cin = x1.shape[1]
    width1 = weight1.shape[0]
    core = lax.axis_index("points")
    chip = lax.axis_index("clouds")
    half = pl.multiple_of(core * points, points)
    barrier = pltpu.get_barrier_semaphore()
    signal_all(barrier, cores, total)
    loads = [
        pltpu.make_async_copy(source, target, load_sems.at[i])
        for i, (source, target) in enumerate(
            (
                (x1_in, x1),
                (near1_in, near1),
                (given1_in, given1),
                (known1_in, known1),
                (grad_own2_in, grad_own2),
                (grad_near2_in, grad_near2),
                (counts_in, counts),
                (away_all1_in, away_all1),
                (away_own1_in, away_own1),
            )
        )
    ]
    for copy in loads:
        copy.start()

    def chip_copy(d, source, target, use):
        return pltpu.make_async_remote_copy(
            src_ref=source,
            dst_ref=target,
            send_sem=ring_sems.at[0, use],
            recv_sem=ring_sems.at[1, use],
            device_id=(lax.rem(chip + d, chips), core),
            device_id_type=MESH,
        )

    class Summed:
        def __init__(self, flat, halved, landed, reduced, whole, first):
            self.flat, self.halved, self.landed = flat, halved, landed
            self.reduced, self.whole, self.first = reduced, whole, first
            self.swap = to_partner(flat.at[1 - core], halved, pair_sems, first)
            here = whole.at[core]
            self.back = to_partner(here, here, pair_sems, first + 1)

        def scatter(self):
            self.swap.wait()
            self.flat[core] += self.halved[...]
            self.landed[chip] = self.flat[core, chip]

            def send(d, carry):
                source = self.flat.at[core, lax.rem(chip + d, chips)]
                chip_copy(d, source, self.landed.at[chip], self.first).start()
                return carry

            lax.fori_loop(1, chips, send, 0)

        def wait(self, ref, use):
            others = ref.at[pl.ds(0, chips - 1)]
            arrival = chip_copy(1, others, others, use)
            arrival.wait_recv()
            arrival.wait_send()

        def spread(self, change):
            self.wait(self.landed, self.first)
            self.reduced[...] = change(slot_sum(self.landed, chips))
            self.whole[core, chip] = self.reduced[...]

            def send(d, carry):
                chip_copy(d, self.reduced, self.whole.at[core, chip], self.first + 1).start()
                return carry

            lax.fori_loop(1, chips, send, 0)

        def finish(self):
            self.wait(self.whole.at[core], self.first + 1)
            self.back.start()

    sum1 = Summed(flat1, halved1, landed1, reduced1, all1, 0)
    sum2 = Summed(flat2, halved2, landed2, reduced2, all2, 2)
    direct1 = weight1[:, :cin] - weight1[:, cin:]
    relative1 = weight1[:, cin:]
    slope = scales1[0:1, :]
    r1 = scales1[1:2, :]
    outer_scale = slope / scales1[2:3, :]

    pieces = [(n // chips, n % chips) for n in range(total)]
    size1 = -(-2 * cin // total)
    size2 = reduced2.shape[0]
    blocks2 = 4 * LANES // size2
    for copy in loads[:6]:
        copy.wait()

    def sums_of(count, base, values):
        def add(i, carry):
            start = pl.multiple_of(i * CHUNK, CHUNK)
            rows = pl.ds(start, CHUNK)
            return carry + t_by(x1[pl.ds(base + start, CHUNK), :], values[rows, :])

        return lax.fori_loop(0, count // CHUNK, add, jnp.zeros((cin, width1), F32))

    grad_own1 = sums_of(points, half, given1) * slope
    grad_near1 = sums_of(cores * points, 0, near1) * slope
    summed = [
        jnp.concatenate([grad_own1, grad_near1 - grad_own1], axis=0),
        known1[0],
        known1[1],
    ]
    flat1[...] = jnp.zeros(flat1.shape, F32)
    for n, (c, place) in enumerate(pieces):
        if n * size1 < 2 * cin:
            for i, value in enumerate(summed):
                flat1[c, place, i * size1 : (i + 1) * size1, :] = value[
                    n * size1 : (n + 1) * size1
                ]
    flat2[...] = jnp.zeros(flat2.shape, F32)
    for n, (c, place) in enumerate(pieces[:blocks2]):
        block, row = divmod(n * size2, LANES)
        columns = slice(block % 2 * LANES, (block % 2 + 1) * LANES)
        value = grad_own2[row : row + size2, columns]
        if block >= 2:
            value = grad_near2[row : row + size2, columns] - value
        flat2[c, place] = value

    pl.semaphore_wait(barrier, total - 1)
    sum1.swap.start()
    sum2.swap.start()
    gather_start(parts, slots, small_sems.at[0], small_sems.at[1], cores, total)
    sum1.scatter()
    sum2.scatter()
    for copy in loads[6:]:
        copy.wait()
    gather_wait(slots, small_sems.at[0], small_sems.at[1], total)
    sums = slot_sum(slots, total)
    norm1[...] = sums
    beta_scale = outer_scale * sums[0:1]
    gamma_scale = outer_scale * sums[1:2] * r1

    def corrected(value):
        main, gamma_part, beta_part = [
            value[i * size1 : (i + 1) * size1] for i in range(3)
        ]
        main = main - (gamma_part * gamma_scale + beta_part * beta_scale)
        if size1 == SUBLANES:
            return main
        return jnp.concatenate([main, jnp.zeros((SUBLANES - size1, LANES), F32)], axis=0)

    sum1.spread(corrected)
    sum2.spread(lambda value: value)
    for c in range(cores):

        def push(start):
            rows = pl.ds(c * points + start, CHUNK)
            value = near1[rows, :] * slope
            value = value - (counts[rows, :] * beta_scale + away_all1[rows, :] * gamma_scale)
            pushed[c, :, pl.ds(start, CHUNK)] = jnp.transpose(by(value, relative1))

        over(points, CHUNK, push, 2)
    swap = to_partner(pushed.at[1 - core], arrived, pair_sems, 4)
    swap.start()

    def own(start):
        rows = pl.ds(start, CHUNK)
        weights = jnp.broadcast_to(mask[:, rows].astype(F32), (SUBLANES, CHUNK))
        weights = jnp.transpose(weights)[:, :1]
        value = given1[rows, :] * slope
        value = value - (depth * weights * beta_scale + away_own1[rows, :] * gamma_scale)
        from_own[:, rows] = jnp.transpose(by(value, direct1)) + pushed[core, :, rows]

    over(points, CHUNK, own, 2)
    sum1.finish()
    sum2.finish()
    swap.wait()
    from_own[...] += arrived[...]
    sum1.back.wait()
    whole1[...] = all1[...]
    sum2.back.wait()
    whole2[...] = all2[...]


def finish_kernel(
    from_own,
    norm1,
    whole1,
    whole2,
    scales2,
    pooled_in,
    pooled,
    grad_features,
    grad_weight1,
    grad_gain1,
    grad_bias1,
    grad_weight2,
    grad_gain2,
    grad_bias2,
):
    pooled[...] = pooled_in[...]
    grad_features[...] = from_own[...]
    cores, chips = whole1.shape[:2]
    cin = from_own.shape[0]
    size1 = -(-2 * cin // (cores * chips))
    rows1 = [whole1[n // chips, n % chips, 0:size1, :] for n in range(2 * cin // size1)]
    grad_weight1[...] = jnp.transpose(jnp.concatenate(rows1, axis=0))
    size2 = whole2.shape[2]
    grad_bias1[...] = norm1[0:1, :]
    grad_gain1[...] = norm1[1:2, :]
    for h in range(2):
        rows = slice(h * LANES, (h + 1) * LANES)
        for part in range(2):
            first = (2 * part + h) * LANES // size2
            block = [
                whole2[n // chips, n % chips] for n in range(first, first + LANES // size2)
            ]
            grad_weight2[rows, part * LANES : (part + 1) * LANES] = jnp.transpose(
                jnp.concatenate(block, axis=0)
            )
    grad_bias2[...] = scales2[1:2, :]
    grad_gain2[...] = scales2[2:3, :]


def shaped(*shape):
    return jax.ShapeDtypeStruct(shape, F32)


def scratch(*shape, dtype=F32):
    return pltpu.VMEM(shape, dtype)


def program(mesh):
    cores, chips = mesh.shape["points"], mesh.shape["clouds"]
    total = cores * chips

    def on_device(
        features,
        lengths,
        mask,
        neighbours,
        first_layer_weight,
        first_norm_gain,
        first_norm_bias,
        second_layer_weight,
        second_norm_gain,
        second_norm_bias,
        pooled_grad,
    ):
        cin, points = features.shape
        depth = neighbours.shape[0]
        width1, width2 = first_layer_weight.shape[0], second_layer_weight.shape[0]
        both = cores * points
        clouds = lengths.shape[0]
        mask_row = mask[None, :]
        groups1, groups2 = points // SUBLANES, points // 4

        def layout(subs, groups):
            place = jnp.arange(points, dtype=jnp.int32) // groups
            return (neighbours * subs + (SUBLANES - subs * place)).reshape(-1)

        index1, index2 = layout(1, groups1), layout(2, groups2)
        block = 32
        outs = pl.pallas_call(
            functools.partial(forward_kernel, (cores, total)),
            out_shape=[
                shaped(clouds, 2 * width2),
                shaped(groups1, depth, SUBLANES, LANES),
                shaped(groups2, depth, SUBLANES, LANES),
                shaped(points, width1),
                shaped(points, width1),
                shaped(points, width1),
                shaped(both, cin),
                shaped(points, width1),
                shaped(both, width1),
                shaped(both, LANES),
                shaped(both, width1),
                shaped(2 * points, LANES),
                shaped(both, width2),
                shaped(SUBLANES, width1),
                shaped(points, width1),
                shaped(width1, width2),
                shaped(SUBLANES, width2),
                shaped(2, 2 * cin, width1),
            ],
            in_specs=[VMEM] * 3 + [ANY] * 2 + [SMEM] + [VMEM] * 3 + [ANY] + [VMEM] * 3,
            out_specs=[VMEM] + [ANY] * 12 + [VMEM] * 5,
            scratch_shapes=[
                scratch(2 * points, LANES),
                scratch(both, width2),
                pltpu.SMEM((depth * points,), jnp.int32),
                pltpu.SMEM((depth * points,), jnp.int32),
                scratch(width2, 2 * width1),
                scratch(points, width1),
                scratch(points, width1),
                scratch(points, width1),
                scratch(both, cin),
                scratch(points, width1),
                scratch(both, width1),
                scratch(both, LANES),
                scratch(cores, cin, points),
                scratch(both, LANES, dtype=BF16),
                scratch(depth, LANES, LANES, dtype=BF16),
                scratch(both, points, dtype=BF16),
                scratch(SUBLANES, points),
                scratch(points, LANES),
                scratch(cores, 3 * cin, points, dtype=BF16),
                scratch(2 * width1, both, dtype=BF16),
                scratch(points, width1),
                scratch(both, width1),
                scratch(points, width1),
                scratch(both + 2 * SUBLANES, LANES),
                scratch(points, LANES),
                scratch(points, LANES),
                scratch(points, LANES),
                scratch(points, LANES),
                scratch(points, LANES),
                scratch(2 * both + 2 * SUBLANES, LANES),
                scratch(2 * points, LANES),
                scratch(2 * points, LANES),
                scratch(2 * points, LANES),
                scratch(2 * points, LANES),
                scratch(2 * points, LANES),
                scratch(both, width1),
                scratch(points, width2),
                scratch(both, width2),
                scratch(points, width2),
                scratch(points, 2 * width2, dtype=BF16),
                scratch(cores, 3 * clouds, SUBLANES, LANES),
                scratch(3, 4, LANES),
                scratch(3, total, 4, LANES),
                scratch(depth, SUBLANES, LANES),
                scratch(depth, SUBLANES, LANES),
                scratch(2, 2 * block, depth, SUBLANES, LANES),
                pltpu.SemaphoreType.DMA((2, 7)),
                pltpu.SemaphoreType.DMA((2, 3)),
                pltpu.SemaphoreType.DMA((2,)),
                pltpu.SemaphoreType.DMA((3,)),
                pltpu.SemaphoreType.DMA((10,)),
            ],
            compiler_params=pltpu.CompilerParams(
                collective_id=1, has_side_effects=True, vmem_limit_bytes=MEMORY
            ),
            name="forward",
        )(
            features,
            neighbours,
            mask_row,
            index1,
            index2,
            lengths,
            first_layer_weight,
            first_norm_gain[None, :],
            first_norm_bias[None, :],
            second_layer_weight,
            second_norm_gain[None, :],
            second_norm_bias[None, :],
            pooled_grad,
        )
        (
            pooled,
            q1,
            q2,
            inverse1,
            share1,
            moment1,
            x1,
            away_own1,
            away_all1,
            counts,
            x2,
            push2,
            extra2,
            scales1,
            own2,
            grad_own2,
            scales2,
            known1,
        ) = outs

        ring = scratch(3, block, depth, SUBLANES, LANES)
        kept, sent, grad_near2 = pl.pallas_call(
            functools.partial(scatter2_kernel, depth),
            out_shape=[shaped(points, width1), shaped(points, width1), shaped(width1, width2)],
            in_specs=[ANY] * 5 + [VMEM, ANY],
            out_specs=[VMEM] * 3,
            scratch_shapes=[
                pltpu.SMEM((depth * points,), jnp.int32),
                scratch(2 * points, LANES),
                scratch(both, width1),
                scratch(width2, 2 * width1),
                scratch(both, width2),
                ring,
                pltpu.SemaphoreType.DMA((5,)),
                pltpu.SemaphoreType.DMA((3,)),
            ]
            + [scratch(2 * both + 2 * SUBLANES, LANES)] * 12,
            compiler_params=pltpu.CompilerParams(vmem_limit_bytes=MEMORY),
            name="scatter2",
        )(index2, q2, push2, x2, second_layer_weight, scales2, extra2)
        other = lax.ppermute(sent, "points", [(0, 1), (1, 0)])

        near1, given1, parts = pl.pallas_call(
            functools.partial(scatter1_kernel, depth),
            out_shape=[shaped(both, width1), shaped(points, width1), shaped(2, width1)],
            in_specs=[ANY] * 2 + [VMEM] * 6,
            out_specs=[ANY] * 2 + [VMEM],
            scratch_shapes=[
                scratch(both, width1),
                scratch(points, width1),
                pltpu.SMEM((depth * points,), jnp.int32),
                scratch(points, width1),
                ring,
                pltpu.SemaphoreType.DMA((1,)),
                pltpu.SemaphoreType.DMA((3,)),
                pltpu.SemaphoreType.DMA((5,)),
            ]
            + [scratch(both + 2 * SUBLANES, LANES)] * (SUBLANES * 2),
            compiler_params=pltpu.CompilerParams(vmem_limit_bytes=MEMORY),
            name="scatter1",
        )(index1, q1, own2, kept, other, inverse1, share1, moment1)

        size1 = -(-2 * cin // total)
        size2 = -(-4 * LANES // (total * SUBLANES)) * SUBLANES
        stacked1 = -(-3 * size1 // SUBLANES) * SUBLANES
        padded1 = -(-size1 // SUBLANES) * SUBLANES
        from_own, norm1, whole1, whole2 = pl.pallas_call(
            functools.partial(last_kernel, (cores, chips), depth),
            out_shape=[
                shaped(cin, points),
                shaped(2, width1),
                shaped(cores, chips, padded1, LANES),
                shaped(cores, chips, size2, LANES),
            ],
            in_specs=[ANY] * 2 + [VMEM] + [ANY] * 4 + [VMEM] * 3 + [ANY] * 3,
            out_specs=[VMEM] * 4,
            scratch_shapes=[
                scratch(both, width1),
                scratch(points, width1),
                scratch(both, cin),
                scratch(points, width1),
                scratch(both, width1),
                scratch(both, LANES),
                scratch(width1, width2),
                scratch(width1, width2),
                scratch(2, 2 * cin, width1),
                scratch(total, 2, LANES),
                scratch(cores, chips, stacked1, LANES),
                scratch(cores, chips, size2, LANES),
                scratch(cores, cin, points),
                scratch(cin, points),
                scratch(chips, stacked1, LANES),
                scratch(chips, size2, LANES),
                scratch(chips, stacked1, LANES),
                scratch(chips, size2, LANES),
                scratch(padded1, LANES),
                scratch(size2, LANES),
                scratch(cores, chips, padded1, LANES),
                scratch(cores, chips, size2, LANES),
                pltpu.SemaphoreType.DMA((2,)),
                pltpu.SemaphoreType.DMA((2, 5)),
                pltpu.SemaphoreType.DMA((2, 4)),
                pltpu.SemaphoreType.DMA((9,)),
            ],
            compiler_params=pltpu.CompilerParams(
                collective_id=2, has_side_effects=True, vmem_limit_bytes=MEMORY
            ),
            name="last",
        )(
            near1,
            given1,
            parts,
            x1,
            away_own1,
            away_all1,
            counts,
            scales1,
            mask_row,
            first_layer_weight,
            grad_own2,
            grad_near2,
            known1,
        )
        outs = pl.pallas_call(
            finish_kernel,
            out_shape=[
                shaped(clouds, 2 * width2),
                shaped(cin, points),
                shaped(width1, 2 * cin),
                shaped(1, width1),
                shaped(1, width1),
                shaped(width2, 2 * width1),
                shaped(1, width2),
                shaped(1, width2),
            ],
            in_specs=[VMEM] * 6,
            out_specs=[VMEM] * 8,
            compiler_params=pltpu.CompilerParams(vmem_limit_bytes=MEMORY),
            name="finish",
        )(
            from_own,
            norm1,
            whole1,
            whole2,
            scales2,
            pooled,
        )
        return tuple(
            value.reshape(-1) if value.shape[0] == 1 else value for value in outs
        )

    return on_device


def solution(mesh):
    in_specs = (
        P(None, ("clouds", "points")),
        P("clouds"),
        P(("clouds", "points")),
        P(None, ("clouds", "points")),
        P(),
        P(),
        P(),
        P(),
        P(),
        P(),
        P("clouds", None),
    )
    out_specs = (P("clouds", None), P(None, ("clouds", "points")), P(), P(), P(), P(), P(), P())
    return jax.shard_map(
        program(mesh), mesh=mesh, in_specs=in_specs, out_specs=out_specs, check_vma=False
    )
```

```python
import functools
import math

import jax
import jax.numpy as jnp
from jax import lax
from jax.experimental import pallas as pl
from jax.experimental.pallas import tpu as pltpu
from jax.sharding import PartitionSpec as P

EPSILON = 1e-05
LOG2E = math.log2(math.e)
LN2 = math.log(2.0)
MESH = pl.DeviceIdType.MESH
F32 = jnp.float32
BF16 = jnp.bfloat16
LANES = 128
SUBLANES = 8
CHUNK = 256
MEMORY = 60 * 2**20
VMEM = pl.BlockSpec(memory_space=pltpu.VMEM)
SMEM = pl.BlockSpec(memory_space=pltpu.SMEM)
ANY = pl.BlockSpec(memory_space=pl.ANY)


def dot(left, right, dims):
    return lax.dot_general(
        left,
        right,
        (dims, ((), ())),
        precision=lax.Precision.HIGHEST,
        preferred_element_type=F32,
    )


def mm(left, right):
    return dot(left, right, ((1,), (0,)))


def mm_nt(left, right):
    return dot(left, right, ((1,), (1,)))


def mm_tn(left, right):
    return dot(left, right, ((0,), (0,)))


def mm_low(left, right):
    return lax.dot_general(
        left, right, (((1,), (0,)), ((), ())), preferred_element_type=F32
    )


def split(value):
    high = value.astype(BF16)
    low = (value - high.astype(F32)).astype(BF16)
    return high, low


def product(left, right, dims):
    def part(a, b):
        return lax.dot_general(a, b, (dims, ((), ())), preferred_element_type=F32)

    left_high, left_low = split(left)
    right_high, right_low = split(right)
    return part(left_high, right_high) + (part(left_high, right_low) + part(left_low, right_high))


def by(left, right):
    return product(left, right, ((1,), (0,)))


def by_t(left, right):
    return product(left, right, ((1,), (1,)))


def t_by(left, right):
    return product(left, right, ((0,), (0,)))


def thirds(value):
    high, rest = value.astype(BF16), value - value.astype(BF16).astype(F32)
    middle = rest.astype(BF16)
    return high, middle, (rest - middle.astype(F32)).astype(BF16)


def stacks(value, dim):
    high, middle, low = thirds(value)
    return [jnp.concatenate(parts, axis=dim) for parts in ((high, middle), (high, low))]


def weight_stacks(value, dim):
    high, middle, low = thirds(value)
    return [
        jnp.concatenate(parts, axis=dim)
        for parts in ((high, high), (middle, middle), (low, high))
    ]


def exact(left, right, dims):
    def part(a, b):
        return lax.dot_general(a, b, (dims, ((), ())), preferred_element_type=F32)

    return part(left[0], right[0]) + (part(left[0], right[1]) + part(left[1], right[2]))


def quad_stacks(value):
    high, middle, low = thirds(value)
    return [
        jnp.concatenate(parts, axis=0) for parts in ((high, high, middle, middle), (high, low))
    ]


def quad_weights(value):
    high, middle, low = thirds(value)
    return [
        jnp.concatenate(parts, axis=0) for parts in ((high, middle, high, middle), (low, high))
    ]


def exact_quad(left, right):
    def part(a, b):
        return lax.dot_general(a, b, (((0,), (0,)), ((), ())), preferred_element_type=F32)

    return part(left[0], right[0]) + part(left[1], right[1])


def over(count, step, body, times=1):
    def run(i, carry):
        for t in range(times):
            body(pl.multiple_of((i * times + t) * step, step))
        return carry

    lax.fori_loop(0, count // (step * times), run, 0)


def tree(values, join):
    values = list(values)
    while len(values) > 1:
        values = [
            join(values[i], values[i + 1]) if i + 1 < len(values) else values[i]
            for i in range(0, len(values), 2)
        ]
    return values[0]


def iota(shape, dim):
    return lax.broadcasted_iota(jnp.int32, shape, dim)


def signal_all(barrier, cores, total):
    me = lax.axis_index("clouds") * cores + lax.axis_index("points")

    def send(d, carry):
        t = lax.rem(me + d, total)
        pl.semaphore_signal(
            barrier,
            inc=1,
            device_id=(lax.div(t, cores), lax.rem(t, cores)),
            device_id_type=MESH,
        )
        return carry

    lax.fori_loop(1, total, send, 0)


def gather_start(own, slots, send_sem, recv_sem, cores, total):
    me = lax.axis_index("clouds") * cores + lax.axis_index("points")
    slots[me] = own[...]

    def send(d, carry):
        t = lax.rem(me + d, total)
        pltpu.make_async_remote_copy(
            src_ref=own,
            dst_ref=slots.at[me],
            send_sem=send_sem,
            recv_sem=recv_sem,
            device_id=(lax.div(t, cores), lax.rem(t, cores)),
            device_id_type=MESH,
        ).start()
        return carry

    lax.fori_loop(1, total, send, 0)


def gather_wait(slots, send_sem, recv_sem, total):
    others = slots.at[pl.ds(0, total - 1)]
    arrived = pltpu.make_async_remote_copy(
        src_ref=others,
        dst_ref=others,
        send_sem=send_sem,
        recv_sem=recv_sem,
        device_id=(lax.axis_index("clouds"), 1 - lax.axis_index("points")),
        device_id_type=MESH,
    )
    arrived.wait_recv()
    arrived.wait_send()


def slot_sum(slots, total):
    def add(i, carry):
        return carry + slots[i]

    return lax.fori_loop(1, total, add, slots[0])


def to_partner(source, target, sems, index):
    return pltpu.make_async_remote_copy(
        src_ref=source,
        dst_ref=target,
        send_sem=sems.at[0, index],
        recv_sem=sems.at[1, index],
        device_id=(lax.axis_index("clouds"), 1 - lax.axis_index("points")),
        device_id_type=MESH,
    )


def edge_pass(
    subs, block, depth, index, table, own_rows, out_hbm, held, ring, sems, outs, pending, after_block
):
    level_ref, share_ref, moment_ref, inverse_ref = outs
    per = SUBLANES // subs
    groups = own_rows.shape[0] // SUBLANES
    row = iota((SUBLANES, LANES), 0)
    mine = [(row >= subs * i) & (row < subs * (i + 1)) for i in range(per)]
    def fetch(group, slot):
        for k in range(depth):
            target = held[slot].at[k]
            for i in range(per):
                first = (k * per + i) * groups
                j = index.at[pl.ds(first, groups)][group]
                value = table[pl.ds(j, SUBLANES), :]
                if i == 0:
                    target[...] = value
                else:
                    pltpu.store(target, value, mask=mine[i])

    def work(group, slot, ring_slot, place):
        rows = pl.ds(pl.multiple_of(group * SUBLANES, SUBLANES), SUBLANES)
        peak = tree([held[slot][k] for k in range(depth)], jnp.maximum)
        top = own_rows[rows, :] + peak
        shift = jnp.maximum(top, 0.0)
        rest = jnp.maximum(jnp.exp2(-shift), 2.0**-100)
        under = jnp.maximum(jnp.minimum(top, 0.0), -100.0)
        offset = under - peak
        fifth = 0.2 * rest
        total, share, moment = [], [], []
        for k in range(depth):
            value = held[slot][k]
            power = value + offset
            grown = jnp.exp2(power)
            root = jnp.exp2((power - lax.log2(rest + grown)) * 0.2)
            weight = root * (fifth + grown)
            ring[ring_slot, place, k] = weight
            total.append(root)
            share.append(weight)
            moment.append(weight * value)
        total, share, moment = [
            functools.reduce(jnp.add, parts) for parts in (total, share, moment)
        ]
        mass = share + (0.8 * rest) * total
        inverse = 1.0 / mass
        level = 0.2 * (top - under) + 0.8 * shift + lax.log2(mass)
        level_ref[rows, :] = LN2 * level - math.log(depth)
        inverse_ref[rows, :] = inverse
        share_ref[rows, :] = share * inverse
        moment_ref[rows, :] = moment * inverse

    blocks = groups // block

    def push(b, slot):
        return pltpu.make_async_copy(
            ring.at[slot, pl.ds(0, block)], out_hbm.at[pl.ds(b * block, block)], sems.at[slot]
        )

    fetch(0, 0)

    def one_block(b, carry):
        ring_slot = lax.rem(b, 2)

        if pending is None:

            @pl.when(b >= 2)
            def _():
                push(b - 2, ring_slot).wait()

        else:

            @pl.when(b < 2)
            def _():
                pending(ring_slot).wait()

            @pl.when(b >= 2)
            def _():
                push(b - 2, ring_slot).wait()

        def several(t, inner):
            for unit in range(4):
                slot = unit % 2
                place = t * 4 + unit
                group = b * block + place
                work(group, slot, ring_slot, place)
                fetch(jnp.minimum(group + 1, groups - 1), 1 - slot)
            return inner

        lax.fori_loop(0, block // 4, several, 0)
        push(b, ring_slot).start()
        if after_block is not None:
            after_block(b)
        return carry

    lax.fori_loop(0, blocks, one_block, 0)
    return lambda slot: push(blocks - 2 + slot, slot)


def lanes_to_rows(value, width):
    return [value[:, i * LANES : (i + 1) * LANES] for i in range(width // LANES)]


def rows_to_lanes(rows):
    return rows[0] if len(rows) == 1 else jnp.concatenate(rows, axis=1)


def forward_kernel(
    sizes,
    feat,
    near,
    mask,
    indices,
    lengths,
    weight1,
    gain1,
    bias1,
    weight2_in,
    gain2,
    bias2,
    pooled_grad,
    pooled,
    q1,
    q2,
    inverse1_out,
    share1_out,
    moment1_out,
    x1_out,
    away_own1_out,
    away_all1_out,
    counts_out,
    x2_out,
    push2_out,
    extra2_out,
    scales1,
    own2,
    grad_own2,
    scales2,
    known1,
    push2,
    extra2,
    index1,
    index2,
    weight2,
    inverse1,
    share1,
    moment1,
    x1,
    away_own1,
    away_all1,
    counts,
    x1_cm,
    tallies,
    lows,
    links,
    live,
    live_col,
    parts1,
    parts2,
    u1,
    v1,
    g1,
    table1,
    own_rows1,
    level1,
    other1,
    share_rows1,
    moment_rows1,
    table2,
    own_rows2,
    level2,
    share2,
    moment2,
    inverse2,
    x2,
    u2,
    v2,
    g2,
    u_parts,
    pool_parts,
    message,
    slots,
    held0,
    held1,
    ring,
    pair_sems,
    all_sems,
    ring_sems,
    load_sems,
    store_sems,
):
    cores, total = sizes
    points = feat.shape[1]
    cin = feat.shape[0]
    both = cores * points
    depth = near.shape[0]
    width1 = weight1.shape[0]
    width2 = gain2.shape[1]
    groups1, groups2 = points // SUBLANES, 2 * points // SUBLANES
    core = lax.axis_index("points")
    half = pl.multiple_of(core * points, points)
    barrier = pltpu.get_barrier_semaphore()
    signal_all(barrier, cores, total)
    loads = [
        pltpu.make_async_copy(source, target, load_sems.at[i])
        for i, (source, target) in enumerate(
            (
                (indices.at[pl.ds(0, depth * points)], index1),
                (indices.at[pl.ds(depth * points, depth * points)], index2),
                (weight2_in, weight2),
            )
        )
    ]
    for copy in loads:
        copy.start()
    late = [
        pltpu.make_async_copy(source, target, store_sems.at[8 + i])
        for i, (source, target) in enumerate(((push2, push2_out), (extra2, extra2_out)))
    ]
    stores = [
        pltpu.make_async_copy(source, target, store_sems.at[i])
        for i, (source, target) in enumerate(
            (
                (x1, x1_out),
                (counts, counts_out),
                (away_own1, away_own1_out),
                (away_all1, away_all1_out),
                (inverse1, inverse1_out),
                (share1, share1_out),
                (moment1, moment1_out),
                (x2, x2_out),
            )
        )
    ]

    live[...] = jnp.broadcast_to(mask[...].astype(F32), live.shape)
    row16 = iota((16, LANES), 0)
    one, none = jnp.ones((16, LANES), BF16), jnp.zeros((16, LANES), BF16)

    def build(columns, first):
        high_names, low_names = [], []
        for k in range(depth):
            name = near[k : k + 1, columns]
            high = jnp.where(mask[:, columns] > 0, lax.shift_right_logical(name, 7), -1)
            for names, value in ((high_names, high), (low_names, name & (LANES - 1))):
                names.append(jnp.broadcast_to(value, (16, LANES)).astype(jnp.int16))
        for s in range(0, LANES, 16):
            target = (row16 + s).astype(jnp.int16)
            for k in range(depth):
                lows[k, s : s + 16, :] = jnp.where(low_names[k] == target, one, none)

        def one_high(start):
            target = jnp.full((16, LANES), lax.shift_right_logical(start, 7), jnp.int32)
            target = target.astype(jnp.int16)
            meant = [jnp.where(name == target, one, none) for name in high_names]
            for s in range(0, LANES, 16):
                found = tree([meant[k] * lows[k, s : s + 16, :] for k in range(depth)], jnp.add)
                here = pl.ds(start + s, 16)
                links[here, columns] = found
                tallies[here, :] = found if first else tallies[here, :] + found

        over(both, LANES, one_high)

    tiles = points // LANES
    early = tiles - tiles // 4
    for tile in range(early):
        build(pl.ds(tile * LANES, LANES), tile == 0)
    x1_cm[core] = feat[...]
    pl.semaphore_wait(barrier, total - 1)
    swap = to_partner(feat, x1_cm.at[core], pair_sems, 0)
    swap.start()
    for tile in range(early, tiles):
        build(pl.ds(tile * LANES, LANES), tile == 0)
    live_col[...] = jnp.broadcast_to(jnp.transpose(live[...])[:, :1], live_col.shape)
    swap.wait()

    direct1 = weight1[:, :cin] - weight1[:, cin:]
    relative1 = weight1[:, cin:]
    for c in range(cores):

        def turn(start):
            x1[pl.ds(c * points + start, CHUNK), :] = jnp.transpose(
                x1_cm[c, :, pl.ds(start, CHUNK)]
            )

        over(points, CHUNK, turn, 2)
        value = x1_cm[c]
        high, low = split(value)
        lower = (value - high.astype(F32) - low.astype(F32)).astype(BF16)
        parts1[c, 0:cin, :] = high
        parts1[c, cin : 2 * cin, :] = low
        parts1[c, 2 * cin : 3 * cin, :] = lower

    direct_parts1 = quad_weights(jnp.transpose(direct1))
    relative_parts1 = quad_weights(jnp.transpose(relative1))

    def sums_near1(start):
        columns = pl.ds(start, CHUNK)
        value = mm_low(parts1[0], links[0:points, columns])
        for c in range(1, cores):
            value = value + mm_low(parts1[c], links[c * points : (c + 1) * points, columns])
        value = value[0:cin] + value[cin : 2 * cin] + value[2 * cin : 3 * cin]
        g1[columns, :] = exact_quad(quad_stacks(value), relative_parts1)

    over(points, CHUNK, sums_near1, 2)

    stores[0].start()
    ones = jnp.ones((LANES, LANES), BF16)

    def count_links(start):
        rows = pl.ds(start, CHUNK)
        counts[rows, :] = mm_low(tallies[rows, :], ones)

    over(both, CHUNK, count_links, 4)
    stores[1].start()

    live_sum = jnp.sum(live[0:1, :], axis=1, keepdims=True)
    mine = live_sum * depth

    def fold(count, size, body, state):
        def several(i, carry):
            for t in range(2):
                carry = body(pl.multiple_of((i * 2 + t) * size, size), carry)
            return carry

        return lax.fori_loop(0, count // (2 * size), several, state)

    def column_sum(value):
        rows = [value[s : s + SUBLANES] for s in range(0, value.shape[0], SUBLANES)]
        return tree(rows, jnp.add)

    def statistics(u, v, g, width):
        per = width // LANES
        zeros = jnp.zeros((SUBLANES, width), F32)

        def first(start, carry):
            rows = pl.ds(start, CHUNK)
            weights = rows_to_lanes([live_col[rows, :]] * per)
            return carry[0] + column_sum(weights * u[rows, :]), carry[1] + column_sum(g[rows, :])

        u_sum, g_sum = fold(points, CHUNK, first, (zeros, zeros))
        u_sum = jnp.sum(u_sum, axis=0, keepdims=True)
        g_sum = jnp.sum(g_sum, axis=0, keepdims=True)
        u_mean = u_sum / live_sum
        v_mean = g_sum / mine

        def second(start, carry):
            rows = pl.ds(start, CHUNK)
            weights = rows_to_lanes([live_col[rows, :]] * per)
            centred = weights * (u[rows, :] - u_mean)
            spread = depth * centred + 2.0 * (g[rows, :] - depth * v_mean)
            return carry + column_sum(centred * spread)

        def third(start, carry):
            rows = pl.ds(start, CHUNK)
            away = v[rows, :] - v_mean
            weights = rows_to_lanes([counts[rows, :]] * per)
            return carry + column_sum(weights * away * away)

        square = fold(points, CHUNK, second, zeros)
        square = fold(both, CHUNK, third, square)
        square = jnp.sum(square, axis=0, keepdims=True)
        return depth * u_sum + g_sum, square, u_mean, v_mean

    for c in range(cores):

        def outer(start):
            left = quad_stacks(x1_cm[c, :, pl.ds(start, CHUNK)])
            v1[pl.ds(c * points + start, CHUNK), :] = exact_quad(left, relative_parts1)

        over(points, CHUNK, outer, 2)

    def inner(start):
        rows = pl.ds(start, CHUNK)
        u1[rows, :] = exact_quad(quad_stacks(x1_cm[core, :, rows]), direct_parts1)

    over(points, CHUNK, inner, 2)

    def send_sums(use, rows):
        for i, value in enumerate(rows):
            message[use, i : i + 1, :] = value
        gather_start(
            message.at[use], slots.at[use], all_sems.at[0, use], all_sems.at[1, use], cores, total
        )

    def receive(use):
        gather_wait(slots.at[use], all_sems.at[0, use], all_sems.at[1, use], total)

    def combine(use, numbers, width):
        per = width // LANES
        count = numbers[0]
        for value in numbers[1:]:
            count = count + value

        def value_of(i, first):
            return rows_to_lanes([slots[use, i, first + h : first + h + 1, :] for h in range(per)])

        mean = value_of(0, 0)
        for i in range(1, total):
            mean = mean + value_of(i, 0)
        mean = mean / count
        square = None
        for i in range(total):
            gap = value_of(i, 0) / numbers[i] - mean
            term = value_of(i, per) + numbers[i] * gap * gap
            square = term if square is None else square + term
        return count, mean, square / count

    sums, square, u_mean1, v_mean1 = statistics(u1, v1, g1, width1)
    send_sums(0, [sums, square, jnp.broadcast_to(mine, (1, LANES)), jnp.zeros((1, LANES), F32)])

    for part, value in enumerate(split(u1[...] - u_mean1)):
        u_parts[:, part * LANES : (part + 1) * LANES] = value

    def shared1(start):
        rows = pl.ds(start, CHUNK)
        value = mm_low(links[rows, :], u_parts[:, 0 : 2 * LANES])
        away_all1[rows, :] = value[:, :LANES] + value[:, LANES:]

    over(both, CHUNK, shared1, 2)
    receive(0)
    numbers = [slots[0, i, 2:3, 0:1] for i in range(total)]
    count, mean1, variance1 = combine(0, numbers, width1)
    r1 = lax.rsqrt(variance1 + EPSILON)
    slope1 = gain1[...] * r1
    scales1[...] = jnp.concatenate(
        [slope1, r1, jnp.broadcast_to(count, (1, LANES)), jnp.zeros((5, LANES), F32)], axis=0
    )

    def fill1(start):
        rows = pl.ds(start, CHUNK)
        table1[pl.ds(SUBLANES + start, CHUNK), :] = (v1[rows, :] - v_mean1) * (slope1 * LOG2E)

    over(both, CHUNK, fill1, 2)

    def fill_own1(start):
        rows = pl.ds(start, CHUNK)
        value = (u1[rows, :] - (mean1 - v_mean1)) * (slope1 * LOG2E) + bias1[...] * LOG2E
        for s in range(0, CHUNK, groups1):
            here = pl.ds(lax.div(start, groups1) + s // groups1, groups1, stride=SUBLANES)
            own_rows1[here, :] = value[s : s + groups1]

    over(points, CHUNK, fill_own1, 2)

    loads[0].wait()
    block1, block2 = groups1 // 4, ring.shape[1]
    block_rows = block1 * SUBLANES
    blocks1 = 4

    def hand_over(b):
        rows = pl.ds(pl.multiple_of(b * block_rows, block_rows), block_rows)
        return to_partner(level1.at[rows], other1.at[rows], pair_sems, 3 + b)

    pending = edge_pass(
        1,
        block1,
        depth,
        index1,
        table1,
        own_rows1,
        q1,
        (held0, held1),
        ring,
        ring_sems,
        (level1, share_rows1, moment_rows1, inverse1),
        None,
        lambda b: hand_over(b).start(),
    )

    for i in range(SUBLANES):
        here = pl.ds(i, groups1, stride=SUBLANES)
        x2[pl.ds(half + i * groups1, groups1), :] = level1[here, :]
    loads[1].wait()
    loads[2].wait()
    direct2 = weight2[:, :width1] - weight2[:, width1:]
    relative2 = weight2[:, width1:]
    direct_parts2 = weight_stacks(direct2, 1)
    relative_parts2 = weight_stacks(relative2, 1)
    other_half = pl.multiple_of((1 - core) * points, points)

    def outer2(base):
        def chunk(start):
            rows = pl.ds(base + start, CHUNK)
            value = x2[rows, :]
            high, low = split(jnp.transpose(value))
            parts2[0:width1, rows] = high
            parts2[width1 : 2 * width1, rows] = low
            v2[rows, :] = exact(stacks(value, 1), relative_parts2, ((1,), (1,)))

        over(points, CHUNK, chunk, 2)

    def inner2(start):
        left = stacks(x2[pl.ds(half + start, CHUNK), :], 1)
        u2[pl.ds(start, CHUNK), :] = exact(left, direct_parts2, ((1,), (1,)))

    over(points, CHUNK, inner2, 2)
    outer2(half)
    for b in range(blocks1):
        hand_over(b).wait()
    for i in range(SUBLANES):
        here = pl.ds(i, groups1, stride=SUBLANES)
        x2[pl.ds(other_half + i * groups1, groups1), :] = other1[here, :]
    stores[7].start()
    outer2(other_half)

    def sums_near2(start):
        columns = pl.ds(start, CHUNK)
        value = mm_low(parts2[...], links[:, columns])
        value = value[0:width1] + value[width1 : 2 * width1]
        g2[columns, :] = exact(stacks(jnp.transpose(value), 1), relative_parts2, ((1,), (1,)))

    over(points, CHUNK, sums_near2, 2)

    sums, square, u_mean2, v_mean2 = statistics(u2, v2, g2, width2)
    send_sums(1, lanes_to_rows(sums, width2) + lanes_to_rows(square, width2))
    for part, value in enumerate(split(u2[...] - u_mean2)):
        u_parts[:, part * width2 : (part + 1) * width2] = value

    def shared2(start):
        rows = pl.ds(start, CHUNK)
        extra2[rows, :] = mm_low(links[rows, :], u_parts[:, 0:width2]) + mm_low(
            links[rows, :], u_parts[:, width2:]
        )

    over(both, CHUNK, shared2, 2)

    def away1(start):
        rows = pl.ds(start, CHUNK)
        away_all1[rows, :] += counts[rows, :] * (v1[rows, :] - (mean1 - u_mean1))

    over(both, CHUNK, away1, 2)
    inverse_gain1 = 1.0 / (gain1[...] * LOG2E)
    for i in range(SUBLANES):
        here = pl.ds(i, groups1, stride=SUBLANES)
        rows = slice(i * groups1, (i + 1) * groups1)
        offset = own_rows1[here, :] - bias1[...] * LOG2E
        moment1[rows, :] = (share_rows1[here, :] * offset + moment_rows1[here, :]) * inverse_gain1
        share1[rows, :] = share_rows1[here, :]
        away_own1[rows, :] = depth * live_col[rows, :] * (u1[rows, :] - mean1) + g1[rows, :]
    for copy in stores[2:7]:
        copy.start()
    receive(1)
    count, mean2, variance2 = combine(1, numbers, width2)
    r2 = lax.rsqrt(variance2 + EPSILON)
    slope2 = gain2[...] * r2
    scales2[...] = jnp.concatenate([slope2, jnp.zeros((7, width2), F32)], axis=0)

    def fill2(start):
        rows = pl.ds(start, CHUNK)
        value = (v2[rows, :] - v_mean2) * (slope2 * LOG2E)
        for h in range(2):
            table2[pl.ds(SUBLANES + 2 * start + h, CHUNK, stride=2), :] = value[
                :, h * LANES : (h + 1) * LANES
            ]

    over(both, CHUNK, fill2, 2)

    for i in range(SUBLANES // 2):
        rows = slice(i * groups2, (i + 1) * groups2)
        value = (u2[rows, :] - (mean2 - v_mean2)) * (slope2 * LOG2E) + bias2[...] * LOG2E
        for h in range(2):
            own_rows2[pl.ds(2 * i + h, groups2, stride=SUBLANES), :] = value[
                :, h * LANES : (h + 1) * LANES
            ]

    pending = edge_pass(
        2,
        block2,
        depth,
        index2,
        table2,
        own_rows2,
        q2,
        (held0, held1),
        ring,
        ring_sems,
        (level2, share2, moment2, inverse2),
        pending,
        None,
    )

    clouds = pooled_grad.shape[0]
    ends = [lengths[0]]
    for q in range(1, clouds):
        ends.append(ends[-1] + lengths[q])
    row = iota((SUBLANES, LANES), 0)
    odd = lax.rem(row, 2) == 1
    point_of_row = half + lax.div(row, 2) * groups2
    steps = level2.shape[0] // SUBLANES
    lowest = jnp.full((SUBLANES, LANES), -1e30, F32)
    zero = jnp.zeros((SUBLANES, LANES), F32)

    def past(t):
        position = point_of_row + t
        return [position >= ends[q] for q in range(clouds - 1)]

    def pick(after, values):
        value = values[0]
        for q in range(1, clouds):
            value = jnp.where(after[q - 1], values[q], value)
        return value

    def apart(after, value, none):
        out = []
        for q in range(clouds):
            kept = value if q == 0 else jnp.where(after[q - 1], value, none)
            out.append(kept if q == clouds - 1 else jnp.where(after[q], none, kept))
        return out

    def step_rows(t):
        return pl.ds(pl.multiple_of(t * SUBLANES, SUBLANES), SUBLANES)

    def by_parity(value, join):
        value = join(value, pltpu.roll(value, 2, 0))
        return join(value, pltpu.roll(value, 4, 0))

    def unrolled(body, state, times):
        def several(i, carry):
            for u in range(times):
                carry = body(i * times + u, carry)
            return carry

        return lax.fori_loop(0, steps // times, several, state)

    def peaks(t, carry):
        value = level2[step_rows(t), :]
        after = past(t)
        tops = [jnp.maximum(a, b) for a, b in zip(carry, apart(after, value, lowest))]
        adds = [a + b for a, b in zip(carry[clouds:], apart(after, value, zero))]
        return tuple(tops + adds)

    state = unrolled(peaks, (lowest,) * clouds + (zero,) * clouds, 8)
    peak = [by_parity(value, jnp.maximum) for value in state[:clouds]]
    sums = [by_parity(value, jnp.add) for value in state[clouds:]]

    def masses(t, carry):
        after = past(t)
        value = jnp.exp(level2[step_rows(t), :] - pick(after, peak))
        return tuple(a + b for a, b in zip(carry, apart(after, value, zero)))

    state = unrolled(masses, (zero,) * clouds, 8)
    mass = [by_parity(value, jnp.add) for value in state]
    for q in range(clouds):
        pool_parts[core, 3 * q] = peak[q]
        pool_parts[core, 3 * q + 1] = mass[q]
        pool_parts[core, 3 * q + 2] = sums[q]
    here = pool_parts.at[core]
    swap = to_partner(here, here, pair_sems, 2)
    swap.start()
    swap.wait()

    level, grad_level, grad_mean = [], [], []
    for q in range(clouds):
        top = pool_parts[0, 3 * q]
        for c in range(1, cores):
            top = jnp.maximum(top, pool_parts[c, 3 * q])
        whole, sum_all = zero, zero
        for c in range(cores):
            whole = whole + pool_parts[c, 3 * q + 1] * jnp.exp(pool_parts[c, 3 * q] - top)
            sum_all = sum_all + pool_parts[c, 3 * q + 2]
        level.append(top + jnp.log(whole))
        size = jnp.full((SUBLANES, LANES), lengths[q].astype(F32), F32)
        first = level[q] - jnp.log(size)
        second = sum_all / size
        for h in range(2):
            pooled[q : q + 1, h * LANES : (h + 1) * LANES] = first[h : h + 1]
            pooled[q : q + 1, (2 + h) * LANES : (3 + h) * LANES] = second[h : h + 1]
        given = [pooled_grad[q : q + 1, h * LANES : (h + 1) * LANES] for h in range(4)]
        grad_level.append(jnp.where(odd, given[1], given[0]))
        grad_mean.append(jnp.where(odd, given[3], given[2]) / size)

    slope_rows, bias_rows = [], []
    for ref_value, target in ((gain2[...], slope_rows), (bias2[...], bias_rows)):
        low_half, high_half = lanes_to_rows(ref_value * LOG2E, width2)
        target.append(jnp.where(odd, high_half, low_half))
    inverse_gain = 1.0 / slope_rows[0]
    bias_row = bias_rows[0]

    def gradient(t, carry):
        rows = step_rows(t)
        after = past(t)
        value = pick(after, grad_level) * jnp.exp(level2[rows, :] - pick(after, level))
        value = value + pick(after, grad_mean)
        push2[rows, :] = value * inverse2[rows, :]
        share = share2[rows, :]
        moment = (share * (own_rows2[rows, :] - bias_row) + moment2[rows, :]) * inverse_gain
        given = value * share
        share2[rows, :] = given
        return carry[0] + given, carry[1] + value * moment

    state = unrolled(gradient, (zero, zero), 8)
    grad_beta, grad_gamma = [by_parity(value, jnp.add) for value in state]
    late[0].start()
    send_sums(2, [grad_beta[0:1], grad_beta[1:2], grad_gamma[0:1], grad_gamma[1:2]])

    known1[...] = jnp.zeros(known1.shape, F32)

    def known(start):
        near_rows = pl.ds(start, CHUNK)
        known1[0, cin:, :] += t_by(x1[near_rows, :], away_all1[near_rows, :])
        known1[1, cin:, :] += t_by(x1[near_rows, :], counts[near_rows, :])

    over(both, CHUNK, known, 2)

    def known_own(start):
        rows = pl.ds(start, CHUNK)
        here = x1[pl.ds(half + start, CHUNK), :]
        known1[0, 0:cin, :] += t_by(here, away_own1[rows, :])
        known1[1, 0:cin, :] += t_by(here, depth * live_col[rows, :])

    over(points, CHUNK, known_own, 2)
    for i in range(2):
        known1[i, cin:, :] -= known1[i, 0:cin, :]

    main = jnp.zeros(grad_own2.shape, F32)
    away_sum = jnp.zeros(grad_own2.shape, F32)
    live_x = jnp.zeros((width1, LANES), F32)
    for i in range(SUBLANES // 2):
        rows = slice(i * groups2, (i + 1) * groups2)
        here = x2[pl.ds(half + i * groups2, groups2), :]
        weights = rows_to_lanes([live_col[rows, :]] * 2)
        u2[rows, :] = depth * weights * (u2[rows, :] - mean2) + g2[rows, :]
        given = rows_to_lanes(
            [share2[pl.ds(2 * i + h, groups2, stride=SUBLANES), :] for h in range(2)]
        )
        g2[rows, :] = given * slope2
        main = main + t_by(here, g2[rows, :])
        away_sum = away_sum + t_by(here, u2[rows, :])
        live_x = live_x + t_by(here, depth * live_col[rows, :])
    receive(2)
    sums = slot_sum(slots.at[2], total)
    grad_beta = rows_to_lanes([sums[0:1], sums[1:2]])
    grad_gamma = rows_to_lanes([sums[2:3], sums[3:4]])
    scales2[1:2, :] = grad_beta
    scales2[2:3, :] = grad_gamma
    outer_scale = slope2 / count
    gamma_scale = outer_scale * grad_gamma * r2
    beta_scale = outer_scale * grad_beta

    def extra(start):
        rows = pl.ds(start, CHUNK)
        weights = rows_to_lanes([counts[rows, :]] * 2)
        away = extra2[rows, :] + weights * (v2[rows, :] - (mean2 - u_mean2))
        extra2[rows, :] = weights * beta_scale + away * gamma_scale

    over(both, CHUNK, extra, 2)
    late[1].start()
    grad_own2[...] = main - (
        rows_to_lanes([live_x] * 2) * beta_scale + away_sum * gamma_scale
    )

    def own(start):
        rows = pl.ds(start, CHUNK)
        weights = rows_to_lanes([live_col[rows, :]] * 2)
        value = g2[rows, :] - (depth * weights * beta_scale + u2[rows, :] * gamma_scale)
        own2[rows, :] = by(value, direct2)

    over(points, CHUNK, own, 2)
    for copy in stores + late + [pending(0), pending(1)]:
        copy.wait()


def scatter_loop(subs, depth, index, q_hbm, ring, sems, push, sums, clear):
    per = SUBLANES // subs
    groups = q_hbm.shape[0]
    slots, block = ring.shape[0], ring.shape[1]
    blocks = groups // block
    row = iota((SUBLANES, LANES), 0)
    mine = [(row >= subs * i) & (row < subs * (i + 1)) for i in range(per)]
    ways = len(sums) // per

    def pull(b):
        slot = lax.rem(b, slots)
        return pltpu.make_async_copy(
            q_hbm.at[pl.ds(b * block, block)], ring.at[slot], sems.at[slot]
        )

    for b in range(slots - 1):
        pull(b).start()
    clear()

    def one_block(b, carry):
        @pl.when(b + slots - 1 < blocks)
        def _():
            pull(b + slots - 1).start()

        pull(b).wait()
        slot = lax.rem(b, slots)

        def one_group(place):
            group = b * block + place
            rows = pl.ds(pl.multiple_of(group * SUBLANES, SUBLANES), SUBLANES)
            given = push[rows, :]

            for k in range(depth):
                value = ring[slot, place, k] * given
                for i in range(per):
                    j = index.at[pl.ds((k * per + i) * groups, groups)][group]
                    target = sums[i * ways + k % ways].at[pl.ds(j, SUBLANES), :]
                    pltpu.store(target, target[...] + value, mask=mine[i])

        def two_groups(t, inner):
            for u in range(2):
                one_group(t * 2 + u)
            return inner

        lax.fori_loop(0, block // 2, two_groups, 0)
        return carry

    lax.fori_loop(0, blocks, one_block, 0)


def clear(sums):
    rows = sums[0].shape[0]
    zero = jnp.zeros((SUBLANES, LANES), F32)

    def rows32(start):
        for ref in sums:
            for s in range(0, 4 * SUBLANES, SUBLANES):
                ref[pl.ds(start + s, SUBLANES), :] = zero

    over(rows, 4 * SUBLANES, rows32)
    for s in range(rows // 32 * 32, rows, SUBLANES):
        for ref in sums:
            ref[s : s + SUBLANES, :] = zero


def scatter2_kernel(
    depth,
    index_in,
    q_hbm,
    push_in,
    x2_in,
    weight_in,
    scales,
    extra_in,
    kept,
    sent,
    grad_near,
    index,
    push,
    x2,
    weight,
    extra,
    ring,
    load_sems,
    ring_sems,
    *sums,
):
    loads = [
        pltpu.make_async_copy(source, target, load_sems.at[i])
        for i, (source, target) in enumerate(
            ((index_in.at[pl.ds(index.shape[0], index.shape[0])], index), (push_in, push), (x2_in, x2), (weight_in, weight), (extra_in, extra))
        )
    ]

    def prepare():
        for copy in loads[2:]:
            copy.start()
        clear(sums)
        loads[0].wait()
        loads[1].wait()

    for copy in loads[:2]:
        copy.start()
    scatter_loop(2, depth, index, q_hbm, ring, ring_sems, push, sums, prepare)
    for copy in loads[2:]:
        copy.wait()
    points, width = kept.shape
    relative = weight[:, width:]
    core = lax.axis_index("points")
    grad_near[...] = jnp.zeros(grad_near.shape, F32)
    for part, out in ((1 - core, sent), (core, kept)):

        def finish(start):
            first = pl.multiple_of(part * points + start, CHUNK)
            rows = pl.ds(first, CHUNK)
            halves = []
            for h in range(2):
                here = pl.ds(SUBLANES + 2 * first + h, CHUNK, stride=2)
                halves.append(tree([ref[here, :] for ref in sums], jnp.add))
            value = rows_to_lanes(halves) * scales[0:1, :] - extra[rows, :]
            out[pl.ds(start, CHUNK), :] = by(value, relative)
            grad_near[...] += t_by(x2[rows, :], value)

        over(points, CHUNK, finish, 2)


def scatter1_kernel(
    depth,
    index_in,
    q_hbm,
    own,
    kept,
    other,
    inverse,
    share,
    moment,
    near_out,
    given_out,
    parts,
    near,
    given,
    index,
    push,
    ring,
    load_sems,
    ring_sems,
    store_sems,
    *sums,
):
    first_half = index_in.at[pl.ds(0, index.shape[0])]
    load = pltpu.make_async_copy(first_half, index, load_sems.at[0])
    load.start()
    quarter = near.shape[0] // 4
    stores = [pltpu.make_async_copy(given, given_out, store_sems.at[0])]
    for i in range(4):
        rows = pl.ds(i * quarter, quarter)
        stores.append(
            pltpu.make_async_copy(near.at[rows], near_out.at[rows], store_sems.at[1 + i])
        )

    def prepare():
        clear(sums)
        groups = own.shape[0] // SUBLANES
        grad_beta = jnp.zeros((1, LANES), F32)
        grad_gamma = jnp.zeros((1, LANES), F32)
        for i in range(SUBLANES):
            here = pl.ds(i, groups, stride=SUBLANES)
            rows = slice(i * groups, (i + 1) * groups)
            grad = own[rows, :] + kept[rows, :] + other[rows, :]
            push[here, :] = grad * inverse[here, :]
            weighted = grad * share[rows, :]
            given[rows, :] = weighted
            grad_beta = grad_beta + jnp.sum(weighted, axis=0, keepdims=True)
            grad_gamma = grad_gamma + jnp.sum(grad * moment[rows, :], axis=0, keepdims=True)
        parts[...] = jnp.concatenate([grad_beta, grad_gamma], axis=0)
        stores[0].start()
        load.wait()

    scatter_loop(1, depth, index, q_hbm, ring, ring_sems, push, sums, prepare)

    for i in range(4):

        def finish(start):
            first = i * quarter + start
            here = pl.ds(SUBLANES + first, CHUNK)
            near[pl.ds(first, CHUNK), :] = tree([ref[here, :] for ref in sums], jnp.add)

        over(quarter, CHUNK, finish)
        stores[1 + i].start()
    for copy in stores:
        copy.wait()


def last_kernel(
    sizes,
    depth,
    near1_in,
    given1_in,
    parts,
    x1_in,
    away_own1_in,
    away_all1_in,
    counts_in,
    scales1,
    mask,
    weight1,
    grad_own2_in,
    grad_near2_in,
    known1_in,
    from_own,
    norm1,
    whole1,
    whole2,
    near1,
    given1,
    x1,
    away_own1,
    away_all1,
    counts,
    grad_own2,
    grad_near2,
    known1,
    slots,
    flat1,
    flat2,
    pushed,
    arrived,
    halved1,
    halved2,
    landed1,
    landed2,
    reduced1,
    reduced2,
    all1,
    all2,
    small_sems,
    pair_sems,
    ring_sems,
    load_sems,
):
    cores, chips = sizes
    total = cores * chips
    points = given1.shape[0]
    cin = x1.shape[1]
    width1 = weight1.shape[0]
    core = lax.axis_index("points")
    chip = lax.axis_index("clouds")
    half = pl.multiple_of(core * points, points)
    barrier = pltpu.get_barrier_semaphore()
    signal_all(barrier, cores, total)
    loads = [
        pltpu.make_async_copy(source, target, load_sems.at[i])
        for i, (source, target) in enumerate(
            (
                (x1_in, x1),
                (near1_in, near1),
                (given1_in, given1),
                (known1_in, known1),
                (grad_own2_in, grad_own2),
                (grad_near2_in, grad_near2),
                (counts_in, counts),
                (away_all1_in, away_all1),
                (away_own1_in, away_own1),
            )
        )
    ]
    for copy in loads:
        copy.start()

    def chip_copy(d, source, target, use):
        return pltpu.make_async_remote_copy(
            src_ref=source,
            dst_ref=target,
            send_sem=ring_sems.at[0, use],
            recv_sem=ring_sems.at[1, use],
            device_id=(lax.rem(chip + d, chips), core),
            device_id_type=MESH,
        )

    class Summed:
        def __init__(self, flat, halved, landed, reduced, whole, first):
            self.flat, self.halved, self.landed = flat, halved, landed
            self.reduced, self.whole, self.first = reduced, whole, first
            self.swap = to_partner(flat.at[1 - core], halved, pair_sems, first)
            here = whole.at[core]
            self.back = to_partner(here, here, pair_sems, first + 1)

        def scatter(self):
            self.swap.wait()
            self.flat[core] += self.halved[...]
            self.landed[chip] = self.flat[core, chip]

            def send(d, carry):
                source = self.flat.at[core, lax.rem(chip + d, chips)]
                chip_copy(d, source, self.landed.at[chip], self.first).start()
                return carry

            lax.fori_loop(1, chips, send, 0)

        def wait(self, ref, use):
            others = ref.at[pl.ds(0, chips - 1)]
            arrival = chip_copy(1, others, others, use)
            arrival.wait_recv()
            arrival.wait_send()

        def spread(self, change):
            self.wait(self.landed, self.first)
            self.reduced[...] = change(slot_sum(self.landed, chips))
            self.whole[core, chip] = self.reduced[...]

            def send(d, carry):
                chip_copy(d, self.reduced, self.whole.at[core, chip], self.first + 1).start()
                return carry

            lax.fori_loop(1, chips, send, 0)

        def finish(self):
            self.wait(self.whole.at[core], self.first + 1)
            self.back.start()

    sum1 = Summed(flat1, halved1, landed1, reduced1, all1, 0)
    sum2 = Summed(flat2, halved2, landed2, reduced2, all2, 2)
    direct1 = weight1[:, :cin] - weight1[:, cin:]
    relative1 = weight1[:, cin:]
    slope = scales1[0:1, :]
    r1 = scales1[1:2, :]
    outer_scale = slope / scales1[2:3, :]

    pieces = [(n // chips, n % chips) for n in range(total)]
    size1 = -(-2 * cin // total)
    size2 = reduced2.shape[0]
    blocks2 = 4 * LANES // size2
    for copy in loads[:6]:
        copy.wait()

    def sums_of(count, base, values):
        def add(i, carry):
            start = pl.multiple_of(i * CHUNK, CHUNK)
            rows = pl.ds(start, CHUNK)
            return carry + t_by(x1[pl.ds(base + start, CHUNK), :], values[rows, :])

        return lax.fori_loop(0, count // CHUNK, add, jnp.zeros((cin, width1), F32))

    grad_own1 = sums_of(points, half, given1) * slope
    grad_near1 = sums_of(cores * points, 0, near1) * slope
    summed = [
        jnp.concatenate([grad_own1, grad_near1 - grad_own1], axis=0),
        known1[0],
        known1[1],
    ]
    flat1[...] = jnp.zeros(flat1.shape, F32)
    for n, (c, place) in enumerate(pieces):
        if n * size1 < 2 * cin:
            for i, value in enumerate(summed):
                flat1[c, place, i * size1 : (i + 1) * size1, :] = value[
                    n * size1 : (n + 1) * size1
                ]
    flat2[...] = jnp.zeros(flat2.shape, F32)
    for n, (c, place) in enumerate(pieces[:blocks2]):
        block, row = divmod(n * size2, LANES)
        columns = slice(block % 2 * LANES, (block % 2 + 1) * LANES)
        value = grad_own2[row : row + size2, columns]
        if block >= 2:
            value = grad_near2[row : row + size2, columns] - value
        flat2[c, place] = value

    pl.semaphore_wait(barrier, total - 1)
    sum1.swap.start()
    sum2.swap.start()
    gather_start(parts, slots, small_sems.at[0], small_sems.at[1], cores, total)
    sum1.scatter()
    sum2.scatter()
    for copy in loads[6:]:
        copy.wait()
    gather_wait(slots, small_sems.at[0], small_sems.at[1], total)
    sums = slot_sum(slots, total)
    norm1[...] = sums
    beta_scale = outer_scale * sums[0:1]
    gamma_scale = outer_scale * sums[1:2] * r1

    def corrected(value):
        main, gamma_part, beta_part = [
            value[i * size1 : (i + 1) * size1] for i in range(3)
        ]
        main = main - (gamma_part * gamma_scale + beta_part * beta_scale)
        if size1 == SUBLANES:
            return main
        return jnp.concatenate([main, jnp.zeros((SUBLANES - size1, LANES), F32)], axis=0)

    sum1.spread(corrected)
    sum2.spread(lambda value: value)
    for c in range(cores):

        def push(start):
            rows = pl.ds(c * points + start, CHUNK)
            value = near1[rows, :] * slope
            value = value - (counts[rows, :] * beta_scale + away_all1[rows, :] * gamma_scale)
            pushed[c, :, pl.ds(start, CHUNK)] = jnp.transpose(by(value, relative1))

        over(points, CHUNK, push, 2)
    swap = to_partner(pushed.at[1 - core], arrived, pair_sems, 4)
    swap.start()

    def own(start):
        rows = pl.ds(start, CHUNK)
        weights = jnp.broadcast_to(mask[:, rows].astype(F32), (SUBLANES, CHUNK))
        weights = jnp.transpose(weights)[:, :1]
        value = given1[rows, :] * slope
        value = value - (depth * weights * beta_scale + away_own1[rows, :] * gamma_scale)
        from_own[:, rows] = jnp.transpose(by(value, direct1)) + pushed[core, :, rows]

    over(points, CHUNK, own, 2)
    sum1.finish()
    sum2.finish()
    swap.wait()
    from_own[...] += arrived[...]
    sum1.back.wait()
    whole1[...] = all1[...]
    sum2.back.wait()
    whole2[...] = all2[...]


def finish_kernel(
    from_own,
    norm1,
    whole1,
    whole2,
    scales2,
    pooled_in,
    pooled,
    grad_features,
    grad_weight1,
    grad_gain1,
    grad_bias1,
    grad_weight2,
    grad_gain2,
    grad_bias2,
):
    pooled[...] = pooled_in[...]
    grad_features[...] = from_own[...]
    cores, chips = whole1.shape[:2]
    cin = from_own.shape[0]
    size1 = -(-2 * cin // (cores * chips))
    rows1 = [whole1[n // chips, n % chips, 0:size1, :] for n in range(2 * cin // size1)]
    grad_weight1[...] = jnp.transpose(jnp.concatenate(rows1, axis=0))
    size2 = whole2.shape[2]
    grad_bias1[...] = norm1[0:1, :]
    grad_gain1[...] = norm1[1:2, :]
    for h in range(2):
        rows = slice(h * LANES, (h + 1) * LANES)
        for part in range(2):
            first = (2 * part + h) * LANES // size2
            block = [
                whole2[n // chips, n % chips] for n in range(first, first + LANES // size2)
            ]
            grad_weight2[rows, part * LANES : (part + 1) * LANES] = jnp.transpose(
                jnp.concatenate(block, axis=0)
            )
    grad_bias2[...] = scales2[1:2, :]
    grad_gain2[...] = scales2[2:3, :]


def shaped(*shape):
    return jax.ShapeDtypeStruct(shape, F32)


def scratch(*shape, dtype=F32):
    return pltpu.VMEM(shape, dtype)


def program(mesh):
    cores, chips = mesh.shape["points"], mesh.shape["clouds"]
    total = cores * chips

    def on_device(
        features,
        lengths,
        mask,
        neighbours,
        first_layer_weight,
        first_norm_gain,
        first_norm_bias,
        second_layer_weight,
        second_norm_gain,
        second_norm_bias,
        pooled_grad,
    ):
        cin, points = features.shape
        depth = neighbours.shape[0]
        width1, width2 = first_layer_weight.shape[0], second_layer_weight.shape[0]
        both = cores * points
        clouds = lengths.shape[0]
        mask_row = mask[None, :]
        groups1, groups2 = points // SUBLANES, points // 4

        def layout(subs, groups):
            place = jnp.arange(points, dtype=jnp.int32) // groups
            return neighbours * subs + (SUBLANES - subs * place)

        indices = jnp.concatenate([layout(1, groups1), layout(2, groups2)]).reshape(-1)
        block = 32
        outs = pl.pallas_call(
            functools.partial(forward_kernel, (cores, total)),
            out_shape=[
                shaped(clouds, 2 * width2),
                shaped(groups1, depth, SUBLANES, LANES),
                shaped(groups2, depth, SUBLANES, LANES),
                shaped(points, width1),
                shaped(points, width1),
                shaped(points, width1),
                shaped(both, cin),
                shaped(points, width1),
                shaped(both, width1),
                shaped(both, LANES),
                shaped(both, width1),
                shaped(2 * points, LANES),
                shaped(both, width2),
                shaped(SUBLANES, width1),
                shaped(points, width1),
                shaped(width1, width2),
                shaped(SUBLANES, width2),
                shaped(2, 2 * cin, width1),
            ],
            in_specs=[VMEM] * 3 + [ANY] + [SMEM] + [VMEM] * 3 + [ANY] + [VMEM] * 3,
            out_specs=[VMEM] + [ANY] * 12 + [VMEM] * 5,
            scratch_shapes=[
                scratch(2 * points, LANES),
                scratch(both, width2),
                pltpu.SMEM((depth * points,), jnp.int32),
                pltpu.SMEM((depth * points,), jnp.int32),
                scratch(width2, 2 * width1),
                scratch(points, width1),
                scratch(points, width1),
                scratch(points, width1),
                scratch(both, cin),
                scratch(points, width1),
                scratch(both, width1),
                scratch(both, LANES),
                scratch(cores, cin, points),
                scratch(both, LANES, dtype=BF16),
                scratch(depth, LANES, LANES, dtype=BF16),
                scratch(both, points, dtype=BF16),
                scratch(SUBLANES, points),
                scratch(points, LANES),
                scratch(cores, 3 * cin, points, dtype=BF16),
                scratch(2 * width1, both, dtype=BF16),
                scratch(points, width1),
                scratch(both, width1),
                scratch(points, width1),
                scratch(both + 2 * SUBLANES, LANES),
                scratch(points, LANES),
                scratch(points, LANES),
                scratch(points, LANES),
                scratch(points, LANES),
                scratch(points, LANES),
                scratch(2 * both + 2 * SUBLANES, LANES),
                scratch(2 * points, LANES),
                scratch(2 * points, LANES),
                scratch(2 * points, LANES),
                scratch(2 * points, LANES),
                scratch(2 * points, LANES),
                scratch(both, width1),
                scratch(points, width2),
                scratch(both, width2),
                scratch(points, width2),
                scratch(points, 2 * width2, dtype=BF16),
                scratch(cores, 3 * clouds, SUBLANES, LANES),
                scratch(3, 4, LANES),
                scratch(3, total, 4, LANES),
                scratch(depth, SUBLANES, LANES),
                scratch(depth, SUBLANES, LANES),
                scratch(2, 2 * block, depth, SUBLANES, LANES),
                pltpu.SemaphoreType.DMA((2, 7)),
                pltpu.SemaphoreType.DMA((2, 3)),
                pltpu.SemaphoreType.DMA((2,)),
                pltpu.SemaphoreType.DMA((3,)),
                pltpu.SemaphoreType.DMA((10,)),
            ],
            compiler_params=pltpu.CompilerParams(
                collective_id=1, has_side_effects=True, vmem_limit_bytes=MEMORY
            ),
            name="forward",
        )(
            features,
            neighbours,
            mask_row,
            indices,
            lengths,
            first_layer_weight,
            first_norm_gain[None, :],
            first_norm_bias[None, :],
            second_layer_weight,
            second_norm_gain[None, :],
            second_norm_bias[None, :],
            pooled_grad,
        )
        (
            pooled,
            q1,
            q2,
            inverse1,
            share1,
            moment1,
            x1,
            away_own1,
            away_all1,
            counts,
            x2,
            push2,
            extra2,
            scales1,
            own2,
            grad_own2,
            scales2,
            known1,
        ) = outs

        ring = scratch(3, block, depth, SUBLANES, LANES)
        kept, sent, grad_near2 = pl.pallas_call(
            functools.partial(scatter2_kernel, depth),
            out_shape=[shaped(points, width1), shaped(points, width1), shaped(width1, width2)],
            in_specs=[ANY] * 5 + [VMEM, ANY],
            out_specs=[VMEM] * 3,
            scratch_shapes=[
                pltpu.SMEM((depth * points,), jnp.int32),
                scratch(2 * points, LANES),
                scratch(both, width1),
                scratch(width2, 2 * width1),
                scratch(both, width2),
                ring,
                pltpu.SemaphoreType.DMA((5,)),
                pltpu.SemaphoreType.DMA((3,)),
            ]
            + [scratch(2 * both + 2 * SUBLANES, LANES)] * 12,
            compiler_params=pltpu.CompilerParams(vmem_limit_bytes=MEMORY),
            name="scatter2",
        )(indices, q2, push2, x2, second_layer_weight, scales2, extra2)
        other = lax.ppermute(sent, "points", [(0, 1), (1, 0)])

        near1, given1, parts = pl.pallas_call(
            functools.partial(scatter1_kernel, depth),
            out_shape=[shaped(both, width1), shaped(points, width1), shaped(2, width1)],
            in_specs=[ANY] * 2 + [VMEM] * 6,
            out_specs=[ANY] * 2 + [VMEM],
            scratch_shapes=[
                scratch(both, width1),
                scratch(points, width1),
                pltpu.SMEM((depth * points,), jnp.int32),
                scratch(points, width1),
                ring,
                pltpu.SemaphoreType.DMA((1,)),
                pltpu.SemaphoreType.DMA((3,)),
                pltpu.SemaphoreType.DMA((5,)),
            ]
            + [scratch(both + 2 * SUBLANES, LANES)] * (SUBLANES * 2),
            compiler_params=pltpu.CompilerParams(vmem_limit_bytes=MEMORY),
            name="scatter1",
        )(indices, q1, own2, kept, other, inverse1, share1, moment1)

        size1 = -(-2 * cin // total)
        size2 = -(-4 * LANES // (total * SUBLANES)) * SUBLANES
        stacked1 = -(-3 * size1 // SUBLANES) * SUBLANES
        padded1 = -(-size1 // SUBLANES) * SUBLANES
        from_own, norm1, whole1, whole2 = pl.pallas_call(
            functools.partial(last_kernel, (cores, chips), depth),
            out_shape=[
                shaped(cin, points),
                shaped(2, width1),
                shaped(cores, chips, padded1, LANES),
                shaped(cores, chips, size2, LANES),
            ],
            in_specs=[ANY] * 2 + [VMEM] + [ANY] * 4 + [VMEM] * 3 + [ANY] * 3,
            out_specs=[VMEM] * 4,
            scratch_shapes=[
                scratch(both, width1),
                scratch(points, width1),
                scratch(both, cin),
                scratch(points, width1),
                scratch(both, width1),
                scratch(both, LANES),
                scratch(width1, width2),
                scratch(width1, width2),
                scratch(2, 2 * cin, width1),
                scratch(total, 2, LANES),
                scratch(cores, chips, stacked1, LANES),
                scratch(cores, chips, size2, LANES),
                scratch(cores, cin, points),
                scratch(cin, points),
                scratch(chips, stacked1, LANES),
                scratch(chips, size2, LANES),
                scratch(chips, stacked1, LANES),
                scratch(chips, size2, LANES),
                scratch(padded1, LANES),
                scratch(size2, LANES),
                scratch(cores, chips, padded1, LANES),
                scratch(cores, chips, size2, LANES),
                pltpu.SemaphoreType.DMA((2,)),
                pltpu.SemaphoreType.DMA((2, 5)),
                pltpu.SemaphoreType.DMA((2, 4)),
                pltpu.SemaphoreType.DMA((9,)),
            ],
            compiler_params=pltpu.CompilerParams(
                collective_id=2, has_side_effects=True, vmem_limit_bytes=MEMORY
            ),
            name="last",
        )(
            near1,
            given1,
            parts,
            x1,
            away_own1,
            away_all1,
            counts,
            scales1,
            mask_row,
            first_layer_weight,
            grad_own2,
            grad_near2,
            known1,
        )
        outs = pl.pallas_call(
            finish_kernel,
            out_shape=[
                shaped(clouds, 2 * width2),
                shaped(cin, points),
                shaped(width1, 2 * cin),
                shaped(1, width1),
                shaped(1, width1),
                shaped(width2, 2 * width1),
                shaped(1, width2),
                shaped(1, width2),
            ],
            in_specs=[VMEM] * 6,
            out_specs=[VMEM] * 8,
            compiler_params=pltpu.CompilerParams(vmem_limit_bytes=MEMORY),
            name="finish",
        )(
            from_own,
            norm1,
            whole1,
            whole2,
            scales2,
            pooled,
        )
        return tuple(
            value.reshape(-1) if value.shape[0] == 1 else value for value in outs
        )

    return on_device


def solution(mesh):
    in_specs = (
        P(None, ("clouds", "points")),
        P("clouds"),
        P(("clouds", "points")),
        P(None, ("clouds", "points")),
        P(),
        P(),
        P(),
        P(),
        P(),
        P(),
        P("clouds", None),
    )
    out_specs = (P("clouds", None), P(None, ("clouds", "points")), P(), P(), P(), P(), P(), P())
    return jax.shard_map(
        program(mesh), mesh=mesh, in_specs=in_specs, out_specs=out_specs, check_vma=False
    )
```
